32 devices in a mesh: store: 16 (over z, y, x), rep: 2 (over core).
Axes of the slice: x: 2, y: 2, z: 4, core: 2. Of those that a mesh axis runs over, the one named last changes fastest.
Arguments:
- features: bfloat16 [32768, 768], P('store'), may hold values from -6 to 6
- owners_near: int32 [16384, 1], P(('store', 'rep')), may hold values from 0 to 15; in each aligned block of 512 rows (0 to 511, 512 to 1023, ...) at most 64 rows name the same one
- slots_near: int32 [16384, 1], P(('store', 'rep')), may hold values from 0 to 2047
- owners_far: int32 [98304, 1], P(('store', 'rep')), may hold values from 0 to 15; in each aligned block of 3072 rows (0 to 3071, 3072 to 6143, ...) at most 384 rows name the same one
- slots_far: int32 [98304, 1], P(('store', 'rep')), may hold values from 0 to 2047
- adjacency_low: int32 [16384, 15], P(('store', 'rep')), may hold values from 0 to 3583
- adjacency_top: int32 [4096, 10], P(('store', 'rep')), may hold values from 0 to 511
- labels: int32 [4096], P(('store', 'rep')), may hold values from 0 to 152
- weights_low: float32 [1536, 1024], replicated, may hold values from -0.15625 to 0.15625
- weights_top: float32 [2048, 153], replicated, may hold values from -0.25 to 0.25
- first_low: float32 [1536, 1024], P(('store', 'rep')), may hold values from -0.00390625 to 0.00390625
- second_low: float32 [1536, 1024], P(('store', 'rep')), may hold values from 1e-09 to 1e-07
- first_top: float32 [2048, 153], P(('store', 'rep')), may hold values from -0.03125 to 0.03125
- second_top: float32 [2048, 153], P(('store', 'rep')), may hold values from 1e-07 to 1e-05
Outputs:
- logits: float32 [4096, 153], P(('store', 'rep'))
- new_low: float32 [1536, 1024], replicated
- new_first_low: float32 [1536, 1024], P(('store', 'rep'))
- new_second_low: float32 [1536, 1024], P(('store', 'rep'))
- new_top: float32 [2048, 153], replicated
- new_first_top: float32 [2048, 153], P(('store', 'rep'))
- new_second_top: float32 [2048, 153], P(('store', 'rep'))
The draws below stay inside these ranges and needn't reach their ends.
Inputs may be any that keep to these rules, and one draw needn't show every extreme that they name: `owners_near`: within the rows of one trainer, no store index is named more than 64 times, and some index is named exactly that often. `owners_far`: within the rows of one trainer, no store index is named more than 384 times, and some index is named exactly that often.
All inputs are finite; a program needn't handle non-finite values.
Results may differ from the reference program's by a relative error of at most 0.005.
Values may be sent and summed in bfloat16 or wider, within the bound.
No kernel may reach another device: no remote copies, remote signals or barrier semaphores. Data moves between devices by JAX's collectives and lax.ppermute only.
A program may use at most 128 MiB of HBM per device.

```python
import math
import jax
import jax.numpy as jnp
import numpy as np
from jax import lax

FEAT = 768
HIDDEN_SIZE = 1024
CLASSES = 153
SEEDS = 128
NEAR = 512
FAR = 3072
NODES_DEV = 2048
FAN_TOP = 10
FAN_LOW = 15
TRAINERS = 32
NODES = 32768
CAP_NEAR = 64
CAP_FAR = 384
N_STORE = 16


def plant(array, stream_key, least, top_value):
    shape = array.shape
    index_at = [jax.random.randint(jax.random.fold_in(stream_key, axis), (), 0, shape[axis]) for axis in range(len(shape))]
    array = array.at[tuple(index_at)].set(least)
    longest = shape.index(max(shape))
    index_at[longest] = (index_at[longest] + 1) % shape[longest]
    return array.at[tuple(index_at)].set(top_value)


def levels(own_key, dims, shards, least, largest):
    level = 1.0
    for axis_at, blocks in shards:
        draws = jax.random.uniform(jax.random.fold_in(jax.random.fold_in(own_key, 6), axis_at), (blocks,), jnp.float32, least / len(shards), largest / len(shards))
        level = level * jnp.repeat(jnp.exp(draws), dims[axis_at] // blocks).reshape((-1,) + (1,) * (len(dims) - 1 - axis_at))
    return level


def assign_block(rng, own, number, rows, count, top, most, skew):
    ranking = jax.random.permutation(rng, count)
    packed, ordinary = shares(count, rows * top, most, skew, True), shares(count, rows * top, most, skew, False)
    places = jnp.arange(count)

    def named(tallies, turn):
        used = int((tallies > 0).sum())
        fixed = max(1, used // 4)
        passed = fixed + (places - fixed + turn * (used - fixed)) % max(1, count - fixed)
        return jnp.zeros((count,), jnp.int32).at[ranking[jnp.where(places < fixed, places, passed)]].set(jnp.asarray(tallies, jnp.int32))

    tallies = jnp.where(number % 4 == 0, named(packed, number // 4), named(ordinary, number - number // 4 - 1))
    mixed = jax.random.permutation(jax.random.fold_in(own, 3), count)
    donor, taker = mixed[0:count // 2 * 2:2], mixed[1:count // 2 * 2:2]
    room = jnp.minimum(tallies[donor] - 1, most - tallies[taker]) // 2
    room = jnp.where((donor == ranking[0]) | (taker == ranking[0]) | (tallies[taker] == 0), 0, jnp.maximum(room, 0))
    passed = jax.random.randint(jax.random.fold_in(own, 4), (count // 2,), 0, 1 << 20) % (room + 1)
    tallies = tallies.at[donor].add(-passed).at[taker].add(passed)
    members = jnp.searchsorted(jnp.cumsum(tallies), jnp.arange(rows * top), side="right").astype(jnp.int32)
    listing = members.reshape(top, rows).T
    listing = listing[jax.random.permutation(jax.random.fold_in(own, 1), rows)]
    turn = jax.random.randint(jax.random.fold_in(own, 2), (rows, 1), 0, top)
    return jnp.take_along_axis(listing, (jnp.arange(top)[None, :] + turn) % top, axis=1)


def shares(count, total, bound, slope, full):
    weights = [(1 << 20) // math.isqrt(rank ** slope) + 1 for rank in range(1, count + 1)]
    largest = bound if full else min(bound, max(-(-total // count), total * weights[0] // sum(weights)))
    least = 1 if total - largest >= count - 1 else 0
    given, rest = [largest] + [least] * (count - 1), total - largest - least * (count - 1)
    while rest > 0:
        movable = [i for i in range(1, count) if given[i] < largest] or [i for i in range(1, count) if given[i] < bound]
        mass, budget = sum([weights[i] for i in movable]), rest
        for i in movable:
            extra = min(bound - given[i], max(1, budget * weights[i] // mass), rest)
            given[i] = given[i] + extra
            rest = rest - extra
    return np.array(given)


def bell_draw(rng, shape, deviation, limit, split=(), held_as=jnp.bfloat16):
    result = deviation * jax.random.normal(rng, shape, jnp.float32)
    if split:
        result = result * levels(rng, shape, split, -0.22, 0.18)
    return jnp.clip(result, -limit, limit).astype(held_as)


def setup_inputs(seed: int = 0) -> dict:
    key_of = jax.random.split(jax.random.key(seed), 15)
    features = bell_draw(key_of[0], (NODES, FEAT), 1.0, 6.0, ((0, 16),))
    owners_near_keys = jax.random.split(jax.random.fold_in(key_of[1], 1), (TRAINERS * NEAR) // NEAR)
    owners_near_turns = jax.random.permutation(jax.random.fold_in(key_of[1], 3), (TRAINERS * NEAR) // NEAR)
    owners_near = jax.vmap(lambda own, number: assign_block(jax.random.fold_in(key_of[1], 2), own, number, NEAR, N_STORE, 1, CAP_NEAR, 2))(owners_near_keys, owners_near_turns).reshape((TRAINERS * NEAR, 1))
    slots_near = plant(jax.random.randint(key_of[2], (TRAINERS * NEAR, 1), 0, NODES_DEV), jax.random.fold_in(key_of[2], 1), 0, NODES_DEV - 1).astype(jnp.int32)
    owners_far_keys = jax.random.split(jax.random.fold_in(key_of[3], 1), (TRAINERS * FAR) // FAR)
    owners_far_turns = jax.random.permutation(jax.random.fold_in(key_of[3], 3), (TRAINERS * FAR) // FAR)
    owners_far = jax.vmap(lambda own, number: assign_block(jax.random.fold_in(key_of[3], 2), own, number, FAR, N_STORE, 1, CAP_FAR, 2))(owners_far_keys, owners_far_turns).reshape((TRAINERS * FAR, 1))
    slots_far = plant(jax.random.randint(key_of[4], (TRAINERS * FAR, 1), 0, NODES_DEV), jax.random.fold_in(key_of[4], 1), 0, NODES_DEV - 1).astype(jnp.int32)
    adjacency_low = plant(jax.random.randint(key_of[5], (TRAINERS * NEAR, FAN_LOW), 0, NEAR + FAR), jax.random.fold_in(key_of[5], 1), 0, (NEAR + FAR) - 1).astype(jnp.int32)
    adjacency_top = plant(jax.random.randint(key_of[6], (TRAINERS * SEEDS, FAN_TOP), 0, NEAR), jax.random.fold_in(key_of[6], 1), 0, NEAR - 1).astype(jnp.int32)
    labels = plant(jax.random.randint(key_of[7], (TRAINERS * SEEDS,), 0, CLASSES), jax.random.fold_in(key_of[7], 1), 0, CLASSES - 1).astype(jnp.int32)
    weights_low = bell_draw(key_of[8], (2 * FEAT, HIDDEN_SIZE), (2 * FEAT) ** -0.5, 0.15625, (), jnp.float32)
    weights_top = bell_draw(key_of[9], (2 * HIDDEN_SIZE, CLASSES), (HIDDEN_SIZE // 2) ** -0.5, 0.25, (), jnp.float32)
    first_low = bell_draw(key_of[10], (2 * FEAT, HIDDEN_SIZE), 0.0003, 0.00390625, ((0, 32),), jnp.float32)
    second_low = jnp.clip(jnp.exp(math.log(1.0000000116860974e-07) - 4.6051702 * jax.random.uniform(key_of[11], (2 * FEAT, HIDDEN_SIZE), jnp.float32) ** levels(key_of[11], (2 * FEAT, HIDDEN_SIZE), ((0, 32),), -0.2, 0.2)), 9.999999717180685e-10, 1.0000000116860974e-07)
    first_top = bell_draw(key_of[12], (2 * HIDDEN_SIZE, CLASSES), 0.002, 0.03125, ((0, 32),), jnp.float32)
    second_top = jnp.clip(jnp.exp(math.log(9.999999747378752e-06) - 4.6051701 * jax.random.uniform(key_of[13], (2 * HIDDEN_SIZE, CLASSES), jnp.float32) ** levels(key_of[13], (2 * HIDDEN_SIZE, CLASSES), ((0, 32),), -0.2, 0.2)), 1.0000000116860974e-07, 9.999999747378752e-06)
    return {"features": features, "owners_near": owners_near, "slots_near": slots_near, "owners_far": owners_far, "slots_far": slots_far, "adjacency_low": adjacency_low, "adjacency_top": adjacency_top, "labels": labels, "weights_low": weights_low, "weights_top": weights_top, "first_low": first_low, "second_low": second_low, "first_top": first_top, "second_top": second_top}


beta_one = 0.9
beta_two = 0.999
bias_one = 1.0 - 0.9 ** 10
bias_two = 1.0 - 0.999 ** 10
learn_rate = 0.01
adam_eps = 1e-08

def gelu_tanh(values):
    return jax.nn.gelu(values, approximate=True)

def local_step(fetched, adjacency_low, adjacency_top, labels, low_bf, top_bf, scale):
    near_rows = adjacency_low.shape[0]
    seed_rows = labels.shape[0]
    width = top_bf.shape[0] // 2
    classes_all = top_bf.shape[1]
    gathered = jnp.zeros((near_rows, fetched.shape[1]), jnp.float32)
    for column in range(adjacency_low.shape[1]):
        gathered = gathered + fetched[adjacency_low[:, column]].astype(jnp.float32)
    low_mean = (gathered / adjacency_low.shape[1]).astype(jnp.bfloat16)
    low_input = jnp.concatenate([fetched[:near_rows], low_mean], axis=1)
    pre_hidden = jnp.dot(low_input, low_bf, preferred_element_type=jnp.float32)
    hidden = gelu_tanh(pre_hidden).astype(jnp.bfloat16)
    top_sum = jnp.zeros((seed_rows, width), jnp.float32)
    for column in range(adjacency_top.shape[1]):
        top_sum = top_sum + hidden[adjacency_top[:, column]].astype(jnp.float32)
    top_mean = (top_sum / adjacency_top.shape[1]).astype(jnp.bfloat16)
    top_input = jnp.concatenate([hidden[:seed_rows], top_mean], axis=1)
    logits = jnp.dot(top_input, top_bf, preferred_element_type=jnp.float32)
    powers = jnp.exp(logits)
    chances = powers / lax.optimization_barrier(jnp.sum(powers, axis=1, keepdims=True))
    targets = (labels[:, None] == jnp.arange(classes_all, dtype=jnp.int32)[None, :]).astype(jnp.float32)
    dlogits = ((chances - targets) * scale).astype(jnp.bfloat16)
    grad_top = lax.dot_general(top_input, dlogits, (((0,), (0,)), ((), ())), preferred_element_type=jnp.float32)
    dinput = lax.dot_general(dlogits, top_bf, (((1,), (1,)), ((), ())), preferred_element_type=jnp.float32)
    dhidden = jnp.zeros((near_rows, width), jnp.float32).at[:seed_rows].add(dinput[:, :width])
    spread = dinput[:, width:] / adjacency_top.shape[1]
    for column in range(adjacency_top.shape[1]):
        dhidden = dhidden.at[adjacency_top[:, column]].add(spread)
    unused, pullback = jax.vjp(gelu_tanh, pre_hidden)
    dpre = pullback(dhidden)[0].astype(jnp.bfloat16)
    grad_low = lax.dot_general(low_input, dpre, (((0,), (0,)), ((), ())), preferred_element_type=jnp.float32)
    return (logits, grad_low, grad_top)

def adam_update(weight, moment, square, gradient):
    moment_new = beta_one * moment + (1.0 - beta_one) * gradient
    square_new = beta_two * square + (1.0 - beta_two) * gradient * gradient
    update = moment_new / bias_one / (jnp.sqrt(square_new / bias_two) + adam_eps)
    return (weight - learn_rate * update, moment_new, square_new)

def reference(features, owners_near, slots_near, owners_far, slots_far, adjacency_low, adjacency_top, labels, weights_low, weights_top, first_low, second_low, first_top, second_top):
    trainers = owners_near.shape[0] // NEAR
    near_ids = (owners_near[:, 0] * NODES_DEV + slots_near[:, 0]).reshape(trainers, NEAR)
    far_ids = (owners_far[:, 0] * NODES_DEV + slots_far[:, 0]).reshape(trainers, -1)
    low_lists = adjacency_low.reshape(trainers, NEAR, -1)
    top_lists = adjacency_top.reshape(trainers, SEEDS, -1)
    label_rows = labels.reshape(trainers, SEEDS)
    low_bf = weights_low.astype(jnp.bfloat16)
    top_bf = weights_top.astype(jnp.bfloat16)
    scale = 1.0 / (trainers * SEEDS)

    def one_trainer(totals, pieces):
        near_part, far_part, low_part, top_part, label_part = pieces
        fetched = features[jnp.concatenate([near_part, far_part])]
        logit_rows, grad_low, grad_top = local_step(fetched, low_part, top_part, label_part, low_bf, top_bf, scale)
        return ((totals[0] + grad_low, totals[1] + grad_top), logit_rows)
    start = (jnp.zeros(weights_low.shape, jnp.float32), jnp.zeros(weights_top.shape, jnp.float32))
    (grad_low, grad_top), logit_all = lax.scan(one_trainer, start, (near_ids, far_ids, low_lists, top_lists, label_rows))
    new_low, new_first_low, new_second_low = adam_update(weights_low, first_low, second_low, grad_low)
    new_top, new_first_top, new_second_top = adam_update(weights_top, first_top, second_top, grad_top)
    return (logit_all.reshape(trainers * SEEDS, CLASSES), new_low, new_first_low, new_second_low, new_top, new_first_top, new_second_top)
```

```python
import functools
import math

import jax
import jax.numpy as jnp
from jax import lax
from jax.experimental import pallas as pl
from jax.experimental.pallas import tpu as pltpu
from jax.sharding import PartitionSpec as P

beta_one = 0.9
beta_two = 0.999
bias_one = 1.0 - 0.9**10
bias_two = 1.0 - 0.999**10
learn_rate = 0.01
adam_eps = 1e-08

PLANE = 4
LANES = 128
MIB = 1024 * 1024

VMEM = pl.BlockSpec(memory_space=pltpu.VMEM)
SMEM = pl.BlockSpec(memory_space=pltpu.SMEM)


def dot(a, b, ca=1, cb=0):
    return lax.dot_general(a, b, (((ca,), (cb,)), ((), ())), preferred_element_type=jnp.float32)


def compose_kernel(nodes, per_plane, groups, adj_ref, table_ref, near_ref, ids_ref):
    fan, near_rows = adj_ref.shape
    his = table_ref.shape[1]
    table = table_ref[...]
    top_part = table // 65536
    mid_part = (table // 256) % 256
    low_part = table % 256
    parts = jnp.concatenate([top_part, mid_part, low_part], axis=0).astype(jnp.float32).astype(jnp.bfloat16)
    row_hi = lax.broadcasted_iota(jnp.int32, (his, near_rows), 0)
    row_lo = lax.broadcasted_iota(jnp.int32, (LANES, near_rows), 0)
    for column in range(fan):
        position = adj_ref[column : column + 1, :]
        marks = jnp.where(row_hi == position // LANES, 1.0, 0.0).astype(jnp.bfloat16)
        found = dot(parts, marks)
        value = found[:LANES] * 65536.0 + found[LANES : 2 * LANES] * 256.0 + found[2 * LANES :]
        value = jnp.where(row_lo == position % LANES, value, 0.0)
        ids_ref[column : column + 1, :] = jnp.sum(value, axis=0, keepdims=True).astype(jnp.int32)
    near = near_ref[...]
    plane = near // per_plane
    row_plane = lax.broadcasted_iota(jnp.int32, (groups, near_rows), 0)
    marks = jnp.where(row_plane == plane, 1.0, 0.0)
    earlier = lax.broadcasted_iota(jnp.int32, (near_rows, near_rows), 0) < lax.broadcasted_iota(
        jnp.int32, (near_rows, near_rows), 1
    )
    counts = dot(marks.astype(jnp.bfloat16), jnp.where(earlier, 1.0, 0.0).astype(jnp.bfloat16))
    rank = jnp.sum(counts * marks, axis=0, keepdims=True).astype(jnp.int32)
    ids_ref[fan : fan + 1, :] = near + rank * nodes


def compose(adjacency, table, near, nodes, per_plane, groups):
    near_rows, fan = adjacency.shape
    return pl.pallas_call(
        functools.partial(compose_kernel, nodes, per_plane, groups),
        out_shape=jax.ShapeDtypeStruct((fan + 1, near_rows), jnp.int32),
        in_specs=[VMEM, VMEM, VMEM],
        out_specs=VMEM,
        compiler_params=pltpu.CompilerParams(vmem_limit_bytes=32 * MIB),
        name="compose_ids",
    )(adjacency.T, table, near)


def partial_kernel(places, fan, near_rows, capacity, *refs):
    index_ref = refs[0]
    piece_refs = refs[1 : 1 + len(places)]
    out_ref, table, sums, kept = refs[1 + len(places) :]
    units = piece_refs[0].shape[1] // LANES
    total = table.shape[0] // 8 - 1
    chunk = 256

    def fill(piece, start):
        def step(i, carry):
            values = piece[pl.ds(pl.multiple_of(i * chunk, chunk), chunk), :].astype(jnp.float32)
            base = (start + i * chunk) * 8
            for unit in range(units):
                table[pl.ds(base + unit, chunk, stride=8), :] = values[
                    :, unit * LANES : (unit + 1) * LANES
                ]
            return carry

        lax.fori_loop(0, piece.shape[0] // chunk, step, 0)

    for piece, start in zip(piece_refs, places):
        fill(piece, start)
    table[total * 8 :, :] = jnp.zeros((8, LANES), jnp.float32)
    trainers = out_ref.shape[0]
    unroll = 8

    for trainer in range(trainers):
        kept[...] = jnp.zeros_like(kept)

        def step(i, carry):
            for u in range(unroll):
                n = i * unroll + u
                rows = [
                    table[pl.ds(pl.multiple_of(index_ref[trainer, j, n], 8), 8), :]
                    for j in range(fan)
                ]
                while len(rows) > 1:
                    rows = [a + b for a, b in zip(rows[0::2], rows[1::2])] + (
                        rows[-1:] if len(rows) % 2 else []
                    )
                sums[pl.ds(pl.multiple_of(n * 8, 8), 8), :] = rows[0]
                source = pl.multiple_of(index_ref[trainer, fan, n], 8)
                target = pl.multiple_of(index_ref[trainer, fan + 1, n], 8)
                kept[pl.ds(target, 8), :] = table[pl.ds(source, 8), :]
            return carry

        lax.fori_loop(0, near_rows // unroll, step, 0)
        for unit in range(units):
            lanes = slice(unit * LANES, (unit + 1) * LANES)
            out_ref[trainer, :near_rows, lanes] = sums[
                pl.ds(unit, near_rows, stride=8), :
            ].astype(jnp.bfloat16)
            out_ref[trainer, near_rows:, lanes] = kept[
                pl.ds(unit, capacity, stride=8), :
            ].astype(jnp.bfloat16)


def partial_sums(index, pieces, places, total, capacity):
    trainers, columns, near_rows = index.shape
    width = pieces[0].shape[1]
    return pl.pallas_call(
        functools.partial(partial_kernel, places, columns - 2, near_rows, capacity),
        out_shape=jax.ShapeDtypeStruct((trainers, near_rows + capacity, width), jnp.bfloat16),
        in_specs=[SMEM] + [VMEM] * len(pieces),
        out_specs=VMEM,
        scratch_shapes=[
            pltpu.VMEM(((total + 1) * 8, LANES), jnp.float32),
            pltpu.VMEM(((near_rows + 1) * 8, LANES), jnp.float32),
            pltpu.VMEM(((capacity + 1) * 8, LANES), jnp.float32),
        ],
        compiler_params=pltpu.CompilerParams(vmem_limit_bytes=60 * MIB),
        name="partial_sums",
    )(index, *pieces)


def trainer_kernel(sizes, scale, *refs):
    groups, rows_low, rows_top, classes, class_pad = sizes
    place_ref, labels_ref, adj_ref, column_ref, wl_ref, wt_ref = refs[:6]
    block_refs = refs[6 : 6 + groups]
    logits_ref, keep_ref, send_ref, li, hidden, slope, top_in, wt = refs[6 + groups :]
    seeds, fan_top = adj_ref.shape
    near_rows, low_width = li.shape
    feat = low_width // 2
    width = hidden.shape[1]
    capacity = block_refs[0].shape[0] - near_rows
    here, mine, rep = place_ref[0], place_ref[1], place_ref[2]
    fan_low = place_ref[3].astype(jnp.float32)

    column = column_ref[...]
    rows_cap = lax.broadcasted_iota(jnp.int32, (capacity, near_rows), 0)
    near = None
    total = None
    for k in range(groups):
        marks = jnp.where(rows_cap + k * capacity == column, 1.0, 0.0).astype(jnp.bfloat16)
        term = dot(marks, block_refs[k][near_rows:, :], 0, 0)
        near = term if near is None else near + term
        part = block_refs[k][:near_rows, :].astype(jnp.float32)
        total = part if total is None else total + part
    li[:, :feat] = near.astype(jnp.bfloat16)
    li[:, feat:] = (total / fan_low).astype(jnp.bfloat16)

    wt[...] = jnp.zeros_like(wt)
    wt[:, :classes] = wt_ref[...].astype(jnp.bfloat16)

    factor = math.sqrt(2.0 / math.pi)
    step = 256
    for c in range(width // step):
        cols = slice(c * step, (c + 1) * step)
        v = dot(li[...], wl_ref[:, cols].astype(jnp.bfloat16))
        square = v * v
        t = jnp.tanh(factor * (v + 0.044715 * v * square))
        half = 0.5 * (1.0 + t)
        hidden[:, cols] = (v * half).astype(jnp.bfloat16)
        slope[:, cols] = half + 0.5 * v * (1.0 - t * t) * factor * (1.0 + 3.0 * 0.044715 * square)

    lane_near = lax.broadcasted_iota(jnp.int32, (seeds, near_rows), 1)
    counts = jnp.zeros((seeds, near_rows), jnp.float32)
    for j in range(fan_top):
        counts = counts + jnp.where(adj_ref[:, j : j + 1] == lane_near, 1.0, 0.0)
    counts = counts.astype(jnp.bfloat16)
    top_in[:, :width] = hidden[:seeds, :]
    top_in[:, width:] = (dot(counts, hidden[...]) / fan_top).astype(jnp.bfloat16)
    logits = dot(top_in[...], wt[...])
    logits_ref[...] = logits[:, :classes]
    lane_class = lax.broadcasted_iota(jnp.int32, (seeds, class_pad), 1)
    powers = jnp.where(lane_class < classes, jnp.exp(logits), 0.0)
    chances = powers / jnp.sum(powers, axis=1, keepdims=True)
    targets = jnp.where(lane_class == labels_ref[...], 1.0, 0.0)
    dlogits = ((chances - targets) * scale).astype(jnp.bfloat16)
    dinput = dot(dlogits, wt[...], 1, 1)
    spread = dinput[:, width:] / fan_top
    high = spread.astype(jnp.bfloat16)
    low = (spread - high.astype(jnp.float32)).astype(jnp.bfloat16)
    dhidden = dot(counts, high, 0, 0) + dot(counts, low, 0, 0)
    hidden[:seeds, :] = ((dhidden[:seeds] + dinput[:, :width]) * slope[:seeds, :]).astype(jnp.bfloat16)
    hidden[seeds:, :] = (dhidden[seeds:] * slope[seeds:, :]).astype(jnp.bfloat16)

    first = rep == 0
    members = low_width // rows_low
    stores = members // 2
    lane_groups = width // class_pad
    sub = rows_top // lane_groups

    def slot(store):
        plane, inner = store // PLANE, store % PLANE
        relative = plane - here
        relative = jnp.where(relative < 0, relative + groups, relative)
        return lax.bitwise_xor(mine, jnp.int32(inner)), relative

    tile = 384
    pair = 2 * rows_low
    for m in range(low_width // tile):
        grad = dot(li[:, m * tile : (m + 1) * tile], hidden[...], 0, 0)
        for s in range(tile // pair):
            even = grad[s * pair : s * pair + rows_low]
            odd = grad[s * pair + rows_low : (s + 1) * pair]
            a, b = slot(m * (tile // pair) + s)
            keep_ref[a, b, :rows_low, :] = jnp.where(first, even, odd)
            send_ref[a, b, :rows_low, :] = jnp.where(first, odd, even).astype(jnp.bfloat16)
    grad = dot(top_in[...], dlogits, 0, 0)
    for s in range(stores):
        even = grad[2 * s * rows_top : (2 * s + 1) * rows_top]
        odd = grad[(2 * s + 1) * rows_top : (2 * s + 2) * rows_top]
        own = jnp.where(first, even, odd)
        other = jnp.where(first, odd, even)
        a, b = slot(s)
        own = jnp.concatenate([own[g * sub : (g + 1) * sub] for g in range(lane_groups)], axis=1)
        other = jnp.concatenate([other[g * sub : (g + 1) * sub] for g in range(lane_groups)], axis=1)
        keep_ref[a, b, rows_low:, :] = own
        send_ref[a, b, rows_low:, :] = other.astype(jnp.bfloat16)


def trainer_step(place, labels, adj_top, column, wl, wt, blocks, sizes, scale):
    groups, rows_low, rows_top, classes, class_pad = sizes
    seeds = adj_top.shape[0]
    low_width, width = wl.shape
    near_rows = column.shape[1]
    rows = rows_low + rows_top * class_pad // width
    return pl.pallas_call(
        functools.partial(trainer_kernel, sizes, scale),
        out_shape=(
            jax.ShapeDtypeStruct((seeds, classes), jnp.float32),
            jax.ShapeDtypeStruct((PLANE, groups, rows, width), jnp.float32),
            jax.ShapeDtypeStruct((PLANE, groups, rows, width), jnp.bfloat16),
        ),
        in_specs=[SMEM] + [VMEM] * (5 + groups),
        out_specs=(VMEM, VMEM, VMEM),
        scratch_shapes=[
            pltpu.VMEM((near_rows, low_width), jnp.bfloat16),
            pltpu.VMEM((near_rows, width), jnp.bfloat16),
            pltpu.VMEM((near_rows, width), jnp.float32),
            pltpu.VMEM((seeds, 2 * width), jnp.bfloat16),
            pltpu.VMEM((2 * width, class_pad), jnp.bfloat16),
        ],
        compiler_params=pltpu.CompilerParams(vmem_limit_bytes=60 * MIB),
        name="trainer_step",
    )(place, labels, adj_top, column, wl, wt, *blocks)


def adam_part(gradient, moment, square):
    moment_new = beta_one * moment + (1.0 - beta_one) * gradient
    square_new = beta_two * square + (1.0 - beta_two) * gradient * gradient
    update = moment_new / bias_one / (jnp.sqrt(square_new / bias_two) + adam_eps)
    return learn_rate * update, moment_new, square_new


def adam_kernel(class_pad, parts, *refs):
    part_refs = refs[:parts]
    ml, sl, mt, st, nml, nsl, nmt, nst, delta = refs[parts:]
    rows_low, width = ml.shape
    rows_top, classes = mt.shape
    lane_groups = width // class_pad
    sub = rows_top // lane_groups
    total = part_refs[0][...]
    for ref in part_refs[1:]:
        total = total + ref[...].astype(jnp.float32)
    step, nml[...], nsl[...] = adam_part(total[:rows_low], ml[...], sl[...])
    top = total[rows_low:]
    pieces = []
    for g in range(lane_groups):
        rows = slice(g * sub, (g + 1) * sub)
        gradient = top[:, g * class_pad : g * class_pad + classes]
        piece, nmt[rows, :], nst[rows, :] = adam_part(gradient, mt[rows, :], st[rows, :])
        pieces.append(
            jnp.concatenate([piece, jnp.zeros((sub, class_pad - classes), jnp.float32)], axis=1)
        )
    whole = jnp.concatenate([step, jnp.concatenate(pieces, axis=1)], axis=0)
    delta[...] = whole.astype(jnp.bfloat16)


def adam_share(parts, ml, sl, mt, st, class_pad):
    rows, width = parts[0].shape
    shape = lambda a: jax.ShapeDtypeStruct(a.shape, jnp.float32)
    return pl.pallas_call(
        functools.partial(adam_kernel, class_pad, len(parts)),
        out_shape=(shape(ml), shape(sl), shape(mt), shape(st), jax.ShapeDtypeStruct((rows, width), jnp.bfloat16)),
        in_specs=[VMEM] * (len(parts) + 4),
        out_specs=(VMEM,) * 5,
        compiler_params=pltpu.CompilerParams(vmem_limit_bytes=32 * MIB),
        name="adam_share",
    )(*parts, ml, sl, mt, st)


def apply_kernel(sizes, place_ref, wl, wt, *refs):
    groups, rows_low, rows_top, classes, class_pad = sizes
    delta_refs, (nl, nt) = refs[: 2 * PLANE], refs[2 * PLANE :]
    here, mine, rep = place_ref[0], place_ref[1], place_ref[2]
    width = wl.shape[2]
    lane_groups = width // class_pad
    sub = rows_top // lane_groups
    for d in range(PLANE):
        for half in range(2):
            for k in range(groups):
                plane = here + k
                plane = jnp.where(plane >= groups, plane - groups, plane)
                store = plane * PLANE + lax.bitwise_xor(mine, jnp.int32(d))
                core = rep if half == 0 else 1 - rep
                position = store * 2 + core
                delta = delta_refs[2 * d + half][k].astype(jnp.float32)
                nl[position] = wl[position] - delta[:rows_low]
                for g in range(lane_groups):
                    rows = slice(g * sub, (g + 1) * sub)
                    nt[position, rows, :] = (
                        wt[position, rows, :]
                        - delta[rows_low:, g * class_pad : g * class_pad + classes]
                    )


def apply_updates(place, wl, wt, deltas, sizes):
    groups, rows_low, rows_top, classes, class_pad = sizes
    low3 = wl.reshape(-1, rows_low, wl.shape[1])
    top3 = wt.reshape(-1, rows_top, wt.shape[1])
    nl, nt = pl.pallas_call(
        functools.partial(apply_kernel, sizes),
        out_shape=(
            jax.ShapeDtypeStruct(low3.shape, jnp.float32),
            jax.ShapeDtypeStruct(top3.shape, jnp.float32),
        ),
        in_specs=[SMEM] + [VMEM] * (2 + len(deltas)),
        out_specs=(VMEM, VMEM),
        compiler_params=pltpu.CompilerParams(vmem_limit_bytes=60 * MIB),
        name="apply_updates",
    )(place, low3, top3, *deltas)
    return nl.reshape(wl.shape), nt.reshape(wt.shape)


def per_device(
    features,
    owners_near,
    slots_near,
    owners_far,
    slots_far,
    adjacency_low,
    adjacency_top,
    labels,
    weights_low,
    weights_top,
    first_low,
    second_low,
    first_top,
    second_top,
):
    stores = lax.axis_size("store")
    groups = stores // PLANE
    members = stores * lax.axis_size("rep")
    index = lax.axis_index("store")
    here, mine, rep = index // PLANE, index % PLANE, lax.axis_index("rep")
    store_rows = features.shape[0]
    half = store_rows // 2
    near_rows, fan = adjacency_low.shape
    far_rows = owners_far.shape[0]
    nodes = stores * store_rows
    per_plane = PLANE * store_rows
    near_limit = 2 * near_rows // stores
    capacity = min(near_rows, PLANE * near_limit)
    classes = weights_top.shape[1]
    class_pad = -(-classes // LANES) * LANES
    rows_low, rows_top = first_low.shape[0], first_top.shape[0]
    sizes = (groups, rows_low, rows_top, classes, class_pad)
    bf16 = jnp.bfloat16

    def across(x, distance):
        return lax.ppermute(x, "store", [(i, i ^ distance) for i in range(stores)])

    def along(x, hops):
        return lax.ppermute(x, "store", [(i, (i + hops * PLANE) % stores) for i in range(stores)])

    def sibling(x):
        return lax.ppermute(x, "rep", [(0, 1), (1, 0)])

    own_half = lax.dynamic_slice_in_dim(features, rep * half, half, 0)
    from_x = across(own_half, 1)
    from_y = across(own_half, 2)
    gid_near = owners_near[:, 0] * store_rows + slots_near[:, 0]
    gid_far = owners_far[:, 0] * store_rows + slots_far[:, 0]
    table = jnp.concatenate([gid_near, gid_far]).reshape(-1, LANES)
    table = jnp.pad(table, ((0, -table.shape[0] % 16), (0, 0))).T
    near_line = gid_near.reshape(1, near_rows)
    ids = compose(adjacency_low, table, near_line, nodes, per_plane, groups)
    ids_all = [ids] + [along(ids, -k) for k in range(1, groups)]
    quarter = half // 2
    corner_a = across(from_x[:quarter], 2)
    corner_b = across(from_y[quarter:], 1)
    parts = [from_x, from_y, corner_a, corner_b]
    pieces = [features, from_x, sibling(from_x), from_y, sibling(from_y)]
    pieces += [corner_a, corner_b, sibling(corner_a), sibling(corner_b)]
    places = [0, store_rows, store_rows + half, 2 * store_rows, 2 * store_rows + half]
    places += [3 * store_rows + quarter * i for i in range(4)]

    def local_rows(ids_of):
        neighbours = ids_of[:fan]
        packed = ids_of[fan : fan + 1]
        rank, near_gid = packed // nodes, packed % nodes
        gid = jnp.concatenate([neighbours, near_gid], axis=0)
        held = gid // per_plane == here
        distance = lax.bitwise_xor((gid // store_rows) % PLANE, mine)
        row = gid % store_rows
        turned = jnp.where(distance == 0, row, (row + rep * half) % store_rows)
        row = jnp.where(held, distance * store_rows + turned, per_plane)
        target = jnp.where(held[fan:], rank, capacity)
        return jnp.concatenate([row, target], axis=0) * 8

    per_call = -(-groups // 4)
    order = list(range(1, groups)) + [0]
    blocks = {}
    for start in range(0, groups, per_call):
        turns = order[start : start + per_call]
        lists = jnp.stack([local_rows(ids_all[k]) for k in turns])
        made = partial_sums(lists, pieces, places, per_plane, capacity)
        for i, k in enumerate(turns):
            blocks[k] = along(made[i], k) if k else made[i]

    packed = ids[fan : fan + 1]
    source = (here - (packed % nodes) // per_plane) % groups
    column = source * capacity + packed // nodes
    place = jnp.stack([here, mine, rep, jnp.int32(fan)]).astype(jnp.int32)
    scale = 1.0 / (labels.shape[0] * members)
    logits, keep, send = trainer_step(
        place,
        labels[:, None],
        adjacency_top,
        column,
        weights_low,
        weights_top,
        [blocks[k] for k in range(groups)],
        sizes,
        scale,
    )
    total = keep + sibling(send).astype(jnp.float32)
    arrived = [across(total[d].astype(bf16), d) for d in range(1, PLANE)]
    total = total[0] + sum(a.astype(jnp.float32) for a in arrived)
    shares = [total[0]] + [along(total[k].astype(bf16), k) for k in range(1, groups)]
    new_first_low, new_second_low, new_first_top, new_second_top, delta = adam_share(
        shares, first_low, second_low, first_top, second_top, class_pad
    )
    lined = jnp.stack([delta] + [along(delta, -k) for k in range(1, groups)])
    sheets = [lined] + [across(lined, d) for d in range(1, PLANE)]
    deltas = []
    for sheet in sheets:
        deltas += [sheet, sibling(sheet)]
    new_low, new_top = apply_updates(place, weights_low, weights_top, deltas, sizes)
    return (logits, new_low, new_first_low, new_second_low, new_top, new_first_top, new_second_top)


def solution(mesh):
    both = P(("store", "rep"), None)
    return jax.shard_map(
        per_device,
        mesh=mesh,
        in_specs=(P("store", None),)
        + (both,) * 6
        + (P(("store", "rep")), P(), P(), both, both, both, both),
        out_specs=(both, P(), both, both, P(), both, both),
        check_vma=False,
    )
```

```python
import functools
import math

import jax
import jax.numpy as jnp
from jax import lax
from jax.experimental import pallas as pl
from jax.experimental.pallas import tpu as pltpu
from jax.sharding import PartitionSpec as P

beta_one = 0.9
beta_two = 0.999
bias_one = 1.0 - 0.9**10
bias_two = 1.0 - 0.999**10
learn_rate = 0.01
adam_eps = 1e-08

PLANE = 4
LANES = 128
MIB = 1024 * 1024

VMEM = pl.BlockSpec(memory_space=pltpu.VMEM)
SMEM = pl.BlockSpec(memory_space=pltpu.SMEM)


def dot(a, b, ca=1, cb=0):
    return lax.dot_general(a, b, (((ca,), (cb,)), ((), ())), preferred_element_type=jnp.float32)


def compose_kernel(store_rows, stores, capacity, place_ref, adj_ref, table_ref, near_ref, ids_ref, request_ref, column_ref):
    fan, near_rows = adj_ref.shape
    his = table_ref.shape[1]
    groups = stores // PLANE
    here, mine = place_ref[0], place_ref[1]
    table = table_ref[...]
    parts = jnp.concatenate([table // 65536, (table // 256) % 256, table % 256], axis=0)
    parts = parts.astype(jnp.float32).astype(jnp.bfloat16)
    row_hi = lax.broadcasted_iota(jnp.int32, (his, near_rows), 0)
    row_lo = lax.broadcasted_iota(jnp.int32, (LANES, near_rows), 0)
    for column in range(fan):
        position = adj_ref[column : column + 1, :]
        marks = jnp.where(row_hi == position // LANES, 1.0, 0.0).astype(jnp.bfloat16)
        found = dot(parts, marks)
        value = found[:LANES] * 65536.0 + found[LANES : 2 * LANES] * 256.0 + found[2 * LANES :]
        value = jnp.where(row_lo == position % LANES, value, 0.0)
        ids_ref[column : column + 1, :] = jnp.sum(value, axis=0, keepdims=True).astype(jnp.int32)
    near = near_ref[...]
    owner, slot = near // store_rows, near % store_rows
    row_owner = lax.broadcasted_iota(jnp.int32, (stores, near_rows), 0)
    marks = jnp.where(row_owner == owner, 1.0, 0.0)
    earlier = lax.broadcasted_iota(jnp.int32, (near_rows, near_rows), 0) < lax.broadcasted_iota(
        jnp.int32, (near_rows, near_rows), 1
    )
    counts = dot(marks.astype(jnp.bfloat16), jnp.where(earlier, 1.0, 0.0).astype(jnp.bfloat16))
    rank = jnp.sum(counts * marks, axis=0, keepdims=True).astype(jnp.int32)
    wanted = lax.broadcasted_iota(jnp.int32, (stores * capacity, near_rows), 0)
    marks = jnp.where(wanted == owner * capacity + rank, 1.0, 0.0).astype(jnp.bfloat16)
    line = lax.broadcasted_iota(jnp.int32, (8, near_rows), 0)
    halves = jnp.where(line == 0, slot // 256, jnp.where(line == 1, slot % 256, 0))
    found = dot(halves.astype(jnp.float32).astype(jnp.bfloat16), marks, 1, 1)
    request_ref[...] = (found[0:1] * 256.0 + found[1:2]).astype(jnp.int32)
    hops = here - owner // PLANE
    hops = jnp.where(hops < 0, hops + groups, hops)
    distance = lax.bitwise_xor(owner % PLANE, mine)
    column_ref[...] = (distance * groups + hops) * capacity + rank


def compose(place, adjacency, table, near, store_rows, stores, capacity):
    near_rows, fan = adjacency.shape
    return pl.pallas_call(
        functools.partial(compose_kernel, store_rows, stores, capacity),
        out_shape=(
            jax.ShapeDtypeStruct((fan, near_rows), jnp.int32),
            jax.ShapeDtypeStruct((1, stores * capacity), jnp.int32),
            jax.ShapeDtypeStruct((1, near_rows), jnp.int32),
        ),
        in_specs=[SMEM, VMEM, VMEM, VMEM],
        out_specs=(VMEM, VMEM, VMEM),
        compiler_params=pltpu.CompilerParams(vmem_limit_bytes=32 * MIB),
        name="compose_ids",
    )(place, adjacency.T, table, near)


def near_kernel(groups, place_ref, request_ref, features_ref, out_ref):
    here, mine = place_ref[0], place_ref[1]
    store_rows = features_ref.shape[0]
    capacity = request_ref.shape[1]
    slots = lax.broadcasted_iota(jnp.int32, (store_rows, PLANE * capacity), 0)
    for k in range(groups):
        plane = here + k
        plane = jnp.where(plane >= groups, plane - groups, plane)
        lines = []
        for d in range(PLANE):
            trainer = plane * PLANE + lax.bitwise_xor(mine, jnp.int32(d))
            lines.append(request_ref[pl.ds(trainer, 1), :])
        marks = jnp.where(slots == jnp.concatenate(lines, axis=1), 1.0, 0.0).astype(jnp.bfloat16)
        out_ref[k] = dot(marks, features_ref[...], 0, 0).astype(jnp.bfloat16)


def near_rows_held(place, requests, features, groups):
    capacity = requests.shape[1]
    return pl.pallas_call(
        functools.partial(near_kernel, groups),
        out_shape=jax.ShapeDtypeStruct((groups, PLANE * capacity, features.shape[1]), jnp.bfloat16),
        in_specs=[SMEM, VMEM, VMEM],
        out_specs=VMEM,
        compiler_params=pltpu.CompilerParams(vmem_limit_bytes=32 * MIB),
        name="near_rows",
    )(place, requests, features)


def sort_pairs(count):
    pairs = []
    size = 1
    while size < count:
        step = size
        while step >= 1:
            for start in range(step % size, count - step, 2 * step):
                for i in range(min(step, count - start - step)):
                    a, b = start + i, start + i + step
                    if a // (2 * size) == b // (2 * size):
                        pairs.append((a, b))
            step //= 2
        size *= 2
    return pairs


def list_kernel(store_rows, groups, first, block, place_ref, *refs):
    ids_refs, out_ref = refs[:-1], refs[-1]
    here, mine, rep = place_ref[0], place_ref[1], place_ref[2]
    fan, near_rows = ids_refs[0].shape
    per_plane = PLANE * store_rows
    lanes = lax.broadcasted_iota(jnp.int32, (near_rows, near_rows), 0) // block
    spots = lax.broadcasted_iota(jnp.int32, (near_rows, near_rows), 1)
    blocks = jnp.where(lanes == spots, 1.0, 0.0).astype(jnp.bfloat16)
    for k, ids_ref in enumerate(ids_refs):
        gid = ids_ref[...]
        owner, row = gid // store_rows, gid % store_rows
        distance = lax.bitwise_xor(owner % PLANE, mine)
        turned = row + rep * (store_rows // 2)
        turned = jnp.where(turned >= store_rows, turned - store_rows, turned)
        row = distance * store_rows + jnp.where(distance == 0, row, turned)
        row = jnp.where(owner // PLANE == here, row, per_plane)
        rows = [row[j : j + 1] for j in range(fan)]
        for a, b in sort_pairs(fan):
            rows[a], rows[b] = jnp.minimum(rows[a], rows[b]), jnp.maximum(rows[a], rows[b])
        for j in range(fan):
            out_ref[k, j : j + 1, :] = rows[j] * 8
        if first < fan:
            more = jnp.where(rows[first] < per_plane, 1.0, 0.0).astype(jnp.bfloat16)
            more = dot(jnp.broadcast_to(more, (8, near_rows)), blocks)
            out_ref[k, fan : fan + 1, :] = more[0:1].astype(jnp.int32)
        else:
            out_ref[k, fan : fan + 1, :] = jnp.zeros((1, near_rows), jnp.int32)


def row_lists(place, ids_all, store_rows, first, block):
    fan, near_rows = ids_all[0].shape
    groups = len(ids_all)
    return pl.pallas_call(
        functools.partial(list_kernel, store_rows, groups, first, block),
        out_shape=jax.ShapeDtypeStruct((groups, fan + 1, near_rows), jnp.int32),
        in_specs=[SMEM] + [VMEM] * groups,
        out_specs=VMEM,
        compiler_params=pltpu.CompilerParams(vmem_limit_bytes=32 * MIB),
        name="row_lists",
    )(place, *ids_all)


def partial_kernel(places, turns, first, block, *refs):
    index_ref = refs[0]
    piece_refs = refs[1 : 1 + len(places)]
    out_ref, table, sums = refs[1 + len(places) : 4 + len(places)]
    buffers = refs[4 + len(places) : -1]
    arrived = refs[-1]
    fan, near_rows = index_ref.shape[1] - 1, index_ref.shape[2]
    units = piece_refs[0].shape[1] // LANES
    total = table.shape[0] // 8 - 1
    chunk = 256

    def row(at):
        return table[pl.ds(pl.multiple_of(at, 8), 8), :]

    def tree(rows):
        while len(rows) > 1:
            odd = rows[-1:] if len(rows) % 2 else []
            rows = [a + b for a, b in zip(rows[0::2], rows[1::2])] + odd
        return rows[0]

    copies = [
        pltpu.make_async_copy(piece, buffer, arrived.at[i])
        for i, (piece, buffer) in enumerate(zip(piece_refs, buffers))
    ]
    for copy in copies:
        copy.start()
    table[total * 8 :, :] = jnp.zeros((8, LANES), jnp.float32)
    for copy, buffer, start in zip(copies, buffers, places):
        copy.wait()

        def fill(i, carry):
            values = buffer[pl.ds(pl.multiple_of(i * chunk, chunk), chunk), :].astype(jnp.float32)
            base = (start + i * chunk) * 8
            for unit in range(units):
                table[pl.ds(base + unit, chunk, stride=8), :] = values[
                    :, unit * LANES : (unit + 1) * LANES
                ]
            return carry

        lax.fori_loop(0, buffer.shape[0] // chunk, fill, 0)

    unroll = 16
    for at, turn in enumerate(turns):

        def step(i, carry):
            for u in range(unroll):
                n = i * unroll + u
                sums[pl.ds(pl.multiple_of(n * 8, 8), 8), :] = tree(
                    [row(index_ref[turn, j, n]) for j in range(first)]
                )
            return carry

        lax.fori_loop(0, near_rows // unroll, step, 0)

        def rest(i, carry):
            @pl.when(index_ref[turn, fan, i] > 0)
            def _():
                for u in range(block):
                    n = i * block + u
                    spot = pl.ds(pl.multiple_of(n * 8, 8), 8)
                    sums[spot, :] = sums[spot, :] + tree(
                        [row(index_ref[turn, j, n]) for j in range(first, fan)]
                    )

            return carry

        if first < fan:
            lax.fori_loop(0, near_rows // block, rest, 0)
        for unit in range(units):
            lanes = slice(unit * LANES, (unit + 1) * LANES)
            out_ref[at, :, lanes] = sums[pl.ds(unit, near_rows, stride=8), :].astype(jnp.bfloat16)


def partial_sums(index, pieces, places, turns, total, first, block):
    near_rows = index.shape[2]
    width = pieces[0].shape[1]
    return pl.pallas_call(
        functools.partial(partial_kernel, places, turns, first, block),
        out_shape=jax.ShapeDtypeStruct((len(turns), near_rows, width), jnp.bfloat16),
        in_specs=[SMEM] + [pl.BlockSpec(memory_space=pl.ANY)] * len(pieces),
        out_specs=VMEM,
        scratch_shapes=[
            pltpu.VMEM(((total + 1) * 8, LANES), jnp.float32),
            pltpu.VMEM(((near_rows + 1) * 8, LANES), jnp.float32),
        ]
        + [pltpu.VMEM(piece.shape, piece.dtype) for piece in pieces]
        + [pltpu.SemaphoreType.DMA((len(pieces),))],
        compiler_params=pltpu.CompilerParams(vmem_limit_bytes=60 * MIB),
        name="partial_sums",
    )(index, *pieces)


def trainer_kernel(sizes, scale, *refs):
    groups, rows_low, rows_top, classes, class_pad = sizes
    place_ref, labels_ref, adj_ref, column_ref, wl_ref, wt_ref = refs[:6]
    block_refs = refs[6 : 6 + groups]
    near_refs = refs[6 + groups : 6 + groups + PLANE]
    logits_ref, keep_ref, send_ref, li, hidden, slope, top_in, wt = refs[6 + groups + PLANE :]
    seeds, fan_top = adj_ref.shape
    near_rows, low_width = li.shape
    feat = low_width // 2
    width = hidden.shape[1]
    capacity = near_refs[0].shape[0]
    here, mine, rep = place_ref[0], place_ref[1], place_ref[2]
    fan_low = place_ref[3].astype(jnp.float32)

    column = column_ref[...]
    rows_cap = lax.broadcasted_iota(jnp.int32, (capacity, near_rows), 0)
    near = None
    for d in range(PLANE):
        marks = jnp.where(rows_cap + d * capacity == column, 1.0, 0.0).astype(jnp.bfloat16)
        term = dot(marks, near_refs[d][...], 0, 0)
        near = term if near is None else near + term
    total = block_refs[0][...].astype(jnp.float32)
    for k in range(1, groups):
        total = total + block_refs[k][...].astype(jnp.float32)
    li[:, :feat] = near.astype(jnp.bfloat16)
    li[:, feat:] = (total / fan_low).astype(jnp.bfloat16)

    wt[...] = jnp.zeros_like(wt)
    wt[:, :classes] = wt_ref[...].astype(jnp.bfloat16)

    factor = math.sqrt(2.0 / math.pi)
    step = 256
    for c in range(width // step):
        cols = slice(c * step, (c + 1) * step)
        v = dot(li[...], wl_ref[:, cols].astype(jnp.bfloat16))
        square = v * v
        t = jnp.tanh(factor * (v + 0.044715 * v * square))
        half = 0.5 * (1.0 + t)
        hidden[:, cols] = (v * half).astype(jnp.bfloat16)
        slope[:, cols] = half + 0.5 * v * (1.0 - t * t) * factor * (1.0 + 3.0 * 0.044715 * square)

    lane_near = lax.broadcasted_iota(jnp.int32, (seeds, near_rows), 1)
    counts = jnp.zeros((seeds, near_rows), jnp.float32)
    for j in range(fan_top):
        counts = counts + jnp.where(adj_ref[:, j : j + 1] == lane_near, 1.0, 0.0)
    counts = counts.astype(jnp.bfloat16)
    top_in[:, :width] = hidden[:seeds, :]
    top_in[:, width:] = (dot(counts, hidden[...]) / fan_top).astype(jnp.bfloat16)
    logits = dot(top_in[...], wt[...])
    logits_ref[...] = logits[:, :classes]
    lane_class = lax.broadcasted_iota(jnp.int32, (seeds, class_pad), 1)
    powers = jnp.where(lane_class < classes, jnp.exp(logits), 0.0)
    chances = powers / jnp.sum(powers, axis=1, keepdims=True)
    targets = jnp.where(lane_class == labels_ref[...], 1.0, 0.0)
    dlogits = ((chances - targets) * scale).astype(jnp.bfloat16)
    dinput = dot(dlogits, wt[...], 1, 1)
    spread = dinput[:, width:] / fan_top
    high = spread.astype(jnp.bfloat16)
    low = (spread - high.astype(jnp.float32)).astype(jnp.bfloat16)
    dhidden = dot(counts, high, 0, 0) + dot(counts, low, 0, 0)
    hidden[:seeds, :] = ((dhidden[:seeds] + dinput[:, :width]) * slope[:seeds, :]).astype(jnp.bfloat16)
    hidden[seeds:, :] = (dhidden[seeds:] * slope[seeds:, :]).astype(jnp.bfloat16)

    first = rep == 0
    members = low_width // rows_low
    stores = members // 2
    lane_groups = width // class_pad
    sub = rows_top // lane_groups

    def slot(store):
        plane, inner = store // PLANE, store % PLANE
        relative = plane - here
        relative = jnp.where(relative < 0, relative + groups, relative)
        return lax.bitwise_xor(mine, jnp.int32(inner)), relative

    tile = 384
    pair = 2 * rows_low
    for m in range(low_width // tile):
        grad = dot(li[:, m * tile : (m + 1) * tile], hidden[...], 0, 0)
        for s in range(tile // pair):
            even = grad[s * pair : s * pair + rows_low]
            odd = grad[s * pair + rows_low : (s + 1) * pair]
            a, b = slot(m * (tile // pair) + s)
            keep_ref[a, b, :rows_low, :] = jnp.where(first, even, odd)
            send_ref[a, b, :rows_low, :] = jnp.where(first, odd, even).astype(jnp.bfloat16)
    grad = dot(top_in[...], dlogits, 0, 0)
    for s in range(stores):
        even = grad[2 * s * rows_top : (2 * s + 1) * rows_top]
        odd = grad[(2 * s + 1) * rows_top : (2 * s + 2) * rows_top]
        own = jnp.where(first, even, odd)
        other = jnp.where(first, odd, even)
        a, b = slot(s)
        own = jnp.concatenate([own[g * sub : (g + 1) * sub] for g in range(lane_groups)], axis=1)
        other = jnp.concatenate([other[g * sub : (g + 1) * sub] for g in range(lane_groups)], axis=1)
        keep_ref[a, b, rows_low:, :] = own
        send_ref[a, b, rows_low:, :] = other.astype(jnp.bfloat16)


def trainer_step(place, labels, adj_top, column, wl, wt, blocks, nears, sizes, scale):
    groups, rows_low, rows_top, classes, class_pad = sizes
    seeds = adj_top.shape[0]
    low_width, width = wl.shape
    near_rows = column.shape[1]
    rows = rows_low + rows_top * class_pad // width
    return pl.pallas_call(
        functools.partial(trainer_kernel, sizes, scale),
        out_shape=(
            jax.ShapeDtypeStruct((seeds, classes), jnp.float32),
            jax.ShapeDtypeStruct((PLANE, groups, rows, width), jnp.float32),
            jax.ShapeDtypeStruct((PLANE, groups, rows, width), jnp.bfloat16),
        ),
        in_specs=[SMEM] + [VMEM] * (5 + groups + PLANE),
        out_specs=(VMEM, VMEM, VMEM),
        scratch_shapes=[
            pltpu.VMEM((near_rows, low_width), jnp.bfloat16),
            pltpu.VMEM((near_rows, width), jnp.bfloat16),
            pltpu.VMEM((near_rows, width), jnp.float32),
            pltpu.VMEM((seeds, 2 * width), jnp.bfloat16),
            pltpu.VMEM((2 * width, class_pad), jnp.bfloat16),
        ],
        compiler_params=pltpu.CompilerParams(vmem_limit_bytes=60 * MIB),
        name="trainer_step",
    )(place, labels, adj_top, column, wl, wt, *blocks, *nears)


def adam_part(gradient, moment, square):
    moment_new = beta_one * moment + (1.0 - beta_one) * gradient
    square_new = beta_two * square + (1.0 - beta_two) * gradient * gradient
    update = moment_new / bias_one / (jnp.sqrt(square_new / bias_two) + adam_eps)
    return learn_rate * update, moment_new, square_new


def adam_kernel(class_pad, parts, *refs):
    part_refs = refs[:parts]
    ml, sl, mt, st, nml, nsl, nmt, nst, delta = refs[parts:]
    rows_low, width = ml.shape
    rows_top, classes = mt.shape
    lane_groups = width // class_pad
    sub = rows_top // lane_groups
    total = part_refs[0][...]
    for ref in part_refs[1:]:
        total = total + ref[...].astype(jnp.float32)
    step, nml[...], nsl[...] = adam_part(total[:rows_low], ml[...], sl[...])
    top = total[rows_low:]
    pieces = []
    for g in range(lane_groups):
        rows = slice(g * sub, (g + 1) * sub)
        gradient = top[:, g * class_pad : g * class_pad + classes]
        piece, nmt[rows, :], nst[rows, :] = adam_part(gradient, mt[rows, :], st[rows, :])
        pieces.append(
            jnp.concatenate([piece, jnp.zeros((sub, class_pad - classes), jnp.float32)], axis=1)
        )
    whole = jnp.concatenate([step, jnp.concatenate(pieces, axis=1)], axis=0)
    delta[...] = whole.astype(jnp.bfloat16)


def adam_share(parts, ml, sl, mt, st, class_pad):
    rows, width = parts[0].shape
    shape = lambda a: jax.ShapeDtypeStruct(a.shape, jnp.float32)
    return pl.pallas_call(
        functools.partial(adam_kernel, class_pad, len(parts)),
        out_shape=(shape(ml), shape(sl), shape(mt), shape(st), jax.ShapeDtypeStruct((rows, width), jnp.bfloat16)),
        in_specs=[VMEM] * (len(parts) + 4),
        out_specs=(VMEM,) * 5,
        compiler_params=pltpu.CompilerParams(vmem_limit_bytes=32 * MIB),
        name="adam_share",
    )(*parts, ml, sl, mt, st)


def apply_kernel(sizes, place_ref, wl, wt, *refs):
    groups, rows_low, rows_top, classes, class_pad = sizes
    delta_refs, (nl, nt) = refs[: 2 * PLANE], refs[2 * PLANE :]
    here, mine, rep = place_ref[0], place_ref[1], place_ref[2]
    width = wl.shape[-1]
    lane_groups = width // class_pad
    sub = rows_top // lane_groups
    for d in range(PLANE):
        for half in range(2):
            for k in range(groups):
                plane = here + k
                plane = jnp.where(plane >= groups, plane - groups, plane)
                store = plane * PLANE + lax.bitwise_xor(mine, jnp.int32(d))
                core = rep if half == 0 else 1 - rep
                position = store * 2 + core
                delta = delta_refs[2 * d + half][k].astype(jnp.float32)
                if len(wl.shape) == 2:
                    rows = pl.ds(pl.multiple_of(position * rows_low, 8), rows_low)
                    nl[rows, :] = wl[rows, :] - delta[:rows_low]
                else:
                    nl[position] = wl[position] - delta[:rows_low]
                for g in range(lane_groups):
                    step = delta[rows_low:, g * class_pad : g * class_pad + classes]
                    if len(wt.shape) == 2:
                        rows = pl.ds(pl.multiple_of(position * rows_top + g * sub, 8), sub)
                        nt[rows, :] = wt[rows, :] - step
                    else:
                        rows = slice(g * sub, (g + 1) * sub)
                        nt[position, rows, :] = wt[position, rows, :] - step


def apply_updates(place, wl, wt, deltas, sizes):
    groups, rows_low, rows_top, classes, class_pad = sizes
    sub = rows_top * class_pad // wl.shape[1]
    low3 = wl if rows_low % 8 == 0 else wl.reshape(-1, rows_low, wl.shape[1])
    top3 = wt if sub % 8 == 0 else wt.reshape(-1, rows_top, wt.shape[1])
    nl, nt = pl.pallas_call(
        functools.partial(apply_kernel, sizes),
        out_shape=(
            jax.ShapeDtypeStruct(low3.shape, jnp.float32),
            jax.ShapeDtypeStruct(top3.shape, jnp.float32),
        ),
        in_specs=[SMEM] + [VMEM] * (2 + len(deltas)),
        out_specs=(VMEM, VMEM),
        compiler_params=pltpu.CompilerParams(vmem_limit_bytes=60 * MIB),
        name="apply_updates",
    )(place, low3, top3, *deltas)
    return nl.reshape(wl.shape), nt.reshape(wt.shape)


def per_device(
    features,
    owners_near,
    slots_near,
    owners_far,
    slots_far,
    adjacency_low,
    adjacency_top,
    labels,
    weights_low,
    weights_top,
    first_low,
    second_low,
    first_top,
    second_top,
):
    stores = lax.axis_size("store")
    groups = stores // PLANE
    members = stores * lax.axis_size("rep")
    index = lax.axis_index("store")
    here, mine, rep = index // PLANE, index % PLANE, lax.axis_index("rep")
    store_rows = features.shape[0]
    half = store_rows // 2
    near_rows, fan = adjacency_low.shape
    capacity = 2 * near_rows // stores
    classes = weights_top.shape[1]
    class_pad = -(-classes // LANES) * LANES
    rows_low, rows_top = first_low.shape[0], first_top.shape[0]
    sizes = (groups, rows_low, rows_top, classes, class_pad)
    bf16 = jnp.bfloat16
    place = jnp.stack([here, mine, rep, jnp.int32(fan)]).astype(jnp.int32)

    def across(x, distance):
        return lax.ppermute(x, "store", [(i, i ^ distance) for i in range(stores)])

    def along(x, hops):
        return lax.ppermute(x, "store", [(i, (i + hops * PLANE) % stores) for i in range(stores)])

    def sibling(x):
        return lax.ppermute(x, "rep", [(0, 1), (1, 0)])

    quarter = half // 2
    own_a = lax.dynamic_slice_in_dim(features, rep * half, quarter, 0)
    own_b = lax.dynamic_slice_in_dim(features, rep * half + quarter, quarter, 0)
    x_a, y_b = across(own_a, 1), across(own_b, 2)
    x_b, y_a = across(own_b, 1), across(own_a, 2)
    gid_near = owners_near[:, 0] * store_rows + slots_near[:, 0]
    gid_far = owners_far[:, 0] * store_rows + slots_far[:, 0]
    table = jnp.concatenate([gid_near, gid_far]).reshape(-1, LANES)
    table = jnp.pad(table, ((0, -table.shape[0] % 16), (0, 0))).T
    ids, requests, column = compose(
        place, adjacency_low, table, gid_near.reshape(1, near_rows), store_rows, stores, capacity
    )
    ids_all = [ids] + [along(ids, -k) for k in range(1, groups)]
    requests = lax.all_to_all(requests.reshape(stores, capacity), "store", 0, 0, tiled=True)
    held = near_rows_held(place, requests, features, groups)
    first, block = min(8, fan), 8
    lists = row_lists(place, ids_all, store_rows, first, block)
    lined = [held[0]] + [along(held[k], k) for k in range(1, groups)]
    corner_a, corner_b = across(x_a, 2), across(y_b, 1)
    pieces, places = [features], [0]
    for turn, (one, two) in enumerate([(x_a, x_b), (y_a, y_b), (corner_a, corner_b)]):
        pieces += [one, two, sibling(one), sibling(two)]
        places += [(turn + 1) * store_rows + quarter * i for i in range(4)]

    per_call = -(-groups // 4)
    order = [groups // 2] + [k for k in range(1, groups) if k != groups // 2] + [0]
    blocks = {}
    for start in range(0, groups, per_call):
        turns = order[start : start + per_call]
        made = partial_sums(lists, pieces, places, turns, PLANE * store_rows, first, block)
        for i, k in enumerate(turns):
            blocks[k] = along(made[i], k) if k else made[i]

    nears = []
    for d in range(PLANE):
        sheet = jnp.concatenate([part[d * capacity : (d + 1) * capacity] for part in lined])
        nears.append(across(sheet, d) if d else sheet)

    scale = 1.0 / (labels.shape[0] * members)
    logits, keep, send = trainer_step(
        place,
        labels[:, None],
        adjacency_top,
        column,
        weights_low,
        weights_top,
        [blocks[k] for k in range(groups)],
        nears,
        sizes,
        scale,
    )
    total = keep + sibling(send).astype(jnp.float32)
    arrived = [across(total[d].astype(bf16), d) for d in range(1, PLANE)]
    total = total[0] + sum(a.astype(jnp.float32) for a in arrived)
    shares = [total[0]] + [along(total[k].astype(bf16), k) for k in range(1, groups)]
    new_first_low, new_second_low, new_first_top, new_second_top, delta = adam_share(
        shares, first_low, second_low, first_top, second_top, class_pad
    )
    lined = jnp.stack([delta] + [along(delta, -k) for k in range(1, groups)])
    sheets = [lined] + [across(lined, d) for d in range(1, PLANE)]
    deltas = []
    for sheet in sheets:
        deltas += [sheet, sibling(sheet)]
    new_low, new_top = apply_updates(place, weights_low, weights_top, deltas, sizes)
    return (logits, new_low, new_first_low, new_second_low, new_top, new_first_top, new_second_top)


def solution(mesh):
    both = P(("store", "rep"), None)
    return jax.shard_map(
        per_device,
        mesh=mesh,
        in_specs=(P("store", None),)
        + (both,) * 6
        + (P(("store", "rep")), P(), P(), both, both, both, both),
        out_specs=(both, P(), both, both, P(), both, both),
        check_vma=False,
    )
```

```python
import functools
import math

import jax
import jax.numpy as jnp
from jax import lax
from jax.experimental import pallas as pl
from jax.experimental.pallas import tpu as pltpu
from jax.sharding import PartitionSpec as P

beta_one = 0.9
beta_two = 0.999
bias_one = 1.0 - 0.9**10
bias_two = 1.0 - 0.999**10
learn_rate = 0.01
adam_eps = 1e-08

PLANE = 4
LANES = 128
MIB = 1024 * 1024

VMEM = pl.BlockSpec(memory_space=pltpu.VMEM)
SMEM = pl.BlockSpec(memory_space=pltpu.SMEM)


def dot(a, b, ca=1, cb=0):
    return lax.dot_general(a, b, (((ca,), (cb,)), ((), ())), preferred_element_type=jnp.float32)


def compose_kernel(store_rows, stores, capacity, place_ref, adj_ref, table_ref, near_ref, ids_ref, request_ref, column_ref):
    fan, near_rows = adj_ref.shape
    his = table_ref.shape[1]
    groups = stores // PLANE
    here, mine = place_ref[0], place_ref[1]
    table = table_ref[...]
    parts = jnp.concatenate([table // 65536, (table // 256) % 256, table % 256], axis=0)
    parts = parts.astype(jnp.float32).astype(jnp.bfloat16)
    row_hi = lax.broadcasted_iota(jnp.int32, (his, near_rows), 0)
    row_lo = lax.broadcasted_iota(jnp.int32, (LANES, near_rows), 0)
    for column in range(fan):
        position = adj_ref[column : column + 1, :]
        marks = jnp.where(row_hi == position // LANES, 1.0, 0.0).astype(jnp.bfloat16)
        found = dot(parts, marks)
        value = found[:LANES] * 65536.0 + found[LANES : 2 * LANES] * 256.0 + found[2 * LANES :]
        value = jnp.where(row_lo == position % LANES, value, 0.0)
        ids_ref[column : column + 1, :] = jnp.sum(value, axis=0, keepdims=True).astype(jnp.int32)
    near = near_ref[...]
    owner, slot = near // store_rows, near % store_rows
    row_owner = lax.broadcasted_iota(jnp.int32, (stores, near_rows), 0)
    marks = jnp.where(row_owner == owner, 1.0, 0.0)
    earlier = lax.broadcasted_iota(jnp.int32, (near_rows, near_rows), 0) < lax.broadcasted_iota(
        jnp.int32, (near_rows, near_rows), 1
    )
    counts = dot(marks.astype(jnp.bfloat16), jnp.where(earlier, 1.0, 0.0).astype(jnp.bfloat16))
    rank = jnp.sum(counts * marks, axis=0, keepdims=True).astype(jnp.int32)
    wanted = lax.broadcasted_iota(jnp.int32, (stores * capacity, near_rows), 0)
    marks = jnp.where(wanted == owner * capacity + rank, 1.0, 0.0).astype(jnp.bfloat16)
    line = lax.broadcasted_iota(jnp.int32, (8, near_rows), 0)
    halves = jnp.where(line == 0, slot // 256, jnp.where(line == 1, slot % 256, 0))
    found = dot(halves.astype(jnp.float32).astype(jnp.bfloat16), marks, 1, 1)
    request_ref[...] = (found[0:1] * 256.0 + found[1:2]).astype(jnp.int32)
    hops = here - owner // PLANE
    hops = jnp.where(hops < 0, hops + groups, hops)
    distance = lax.bitwise_xor(owner % PLANE, mine)
    column_ref[...] = (distance * groups + hops) * capacity + rank


def compose(place, adjacency, table, near, store_rows, stores, capacity):
    near_rows, fan = adjacency.shape
    return pl.pallas_call(
        functools.partial(compose_kernel, store_rows, stores, capacity),
        out_shape=(
            jax.ShapeDtypeStruct((fan, near_rows), jnp.int32),
            jax.ShapeDtypeStruct((1, stores * capacity), jnp.int32),
            jax.ShapeDtypeStruct((1, near_rows), jnp.int32),
        ),
        in_specs=[SMEM, VMEM, VMEM, VMEM],
        out_specs=(VMEM, VMEM, VMEM),
        compiler_params=pltpu.CompilerParams(vmem_limit_bytes=32 * MIB),
        name="compose_ids",
    )(place, adjacency.T, table, near)


def near_kernel(groups, place_ref, request_ref, features_ref, out_ref):
    here, mine = place_ref[0], place_ref[1]
    store_rows = features_ref.shape[0]
    capacity = request_ref.shape[1]
    slots = lax.broadcasted_iota(jnp.int32, (store_rows, PLANE * capacity), 0)
    for k in range(groups):
        plane = here + k
        plane = jnp.where(plane >= groups, plane - groups, plane)
        lines = []
        for d in range(PLANE):
            trainer = plane * PLANE + lax.bitwise_xor(mine, jnp.int32(d))
            lines.append(request_ref[pl.ds(trainer, 1), :])
        marks = jnp.where(slots == jnp.concatenate(lines, axis=1), 1.0, 0.0).astype(jnp.bfloat16)
        out_ref[k] = dot(marks, features_ref[...], 0, 0).astype(jnp.bfloat16)


def near_rows_held(place, requests, features, groups):
    capacity = requests.shape[1]
    return pl.pallas_call(
        functools.partial(near_kernel, groups),
        out_shape=jax.ShapeDtypeStruct((groups, PLANE * capacity, features.shape[1]), jnp.bfloat16),
        in_specs=[SMEM, VMEM, VMEM],
        out_specs=VMEM,
        compiler_params=pltpu.CompilerParams(vmem_limit_bytes=32 * MIB),
        name="near_rows",
    )(place, requests, features)


def sort_pairs(count):
    pairs = []
    size = 1
    while size < count:
        step = size
        while step >= 1:
            for start in range(step % size, count - step, 2 * step):
                for i in range(min(step, count - start - step)):
                    a, b = start + i, start + i + step
                    if a // (2 * size) == b // (2 * size):
                        pairs.append((a, b))
            step //= 2
        size *= 2
    return pairs


def list_kernel(store_rows, groups, first, block, place_ref, *refs):
    ids_refs, out_refs = refs[:groups], refs[groups:]
    here, mine = place_ref[0], place_ref[1]
    cores, fan, near_rows = ids_refs[0].shape
    per_plane = PLANE * store_rows
    lanes = lax.broadcasted_iota(jnp.int32, (near_rows, near_rows), 0) // block
    spots = lax.broadcasted_iota(jnp.int32, (near_rows, near_rows), 1)
    blocks = jnp.where(lanes == spots, 1.0, 0.0).astype(jnp.bfloat16)
    for ids_ref, out_ref in zip(ids_refs, out_refs):
        for core in range(cores):
            gid = ids_ref[core]
            owner, row = gid // store_rows, gid % store_rows
            row = lax.bitwise_xor(owner % PLANE, mine) * store_rows + row
            row = jnp.where(owner // PLANE == here, row, per_plane)
            rows = [row[j : j + 1] for j in range(fan)]
            for a, b in sort_pairs(fan):
                rows[a], rows[b] = jnp.minimum(rows[a], rows[b]), jnp.maximum(rows[a], rows[b])
            for j in range(fan):
                out_ref[core, j : j + 1, :] = rows[j] * 8
            if first < fan:
                more = jnp.where(rows[first] < per_plane, 1.0, 0.0).astype(jnp.bfloat16)
                more = dot(jnp.broadcast_to(more, (8, near_rows)), blocks)
                out_ref[core, fan : fan + 1, :] = more[0:1].astype(jnp.int32)
            else:
                out_ref[core, fan : fan + 1, :] = jnp.zeros((1, near_rows), jnp.int32)


def row_lists(place, ids_all, store_rows, first, block):
    cores, fan, near_rows = ids_all[0].shape
    groups = len(ids_all)
    return pl.pallas_call(
        functools.partial(list_kernel, store_rows, groups, first, block),
        out_shape=(jax.ShapeDtypeStruct((cores, fan + 1, near_rows), jnp.int32),) * groups,
        in_specs=[SMEM] + [VMEM] * groups,
        out_specs=(VMEM,) * groups,
        compiler_params=pltpu.CompilerParams(vmem_limit_bytes=32 * MIB),
        name="row_lists",
    )(place, *ids_all)


def partial_kernel(places, first, block, *refs):
    index_ref = refs[0]
    piece_refs = refs[1 : 1 + len(places)]
    out_ref, table, sums = refs[1 + len(places) : 4 + len(places)]
    buffers = refs[4 + len(places) : -1]
    arrived = refs[-1]
    fan, near_rows = index_ref.shape[1] - 1, index_ref.shape[2]
    units = piece_refs[0].shape[1] // LANES
    total = table.shape[0] // 8 - 1
    chunk = 256

    def row(at):
        return table[pl.ds(pl.multiple_of(at, 8), 8), :]

    def tree(rows):
        while len(rows) > 1:
            odd = rows[-1:] if len(rows) % 2 else []
            rows = [a + b for a, b in zip(rows[0::2], rows[1::2])] + odd
        return rows[0]

    copies = [
        pltpu.make_async_copy(piece, buffer, arrived.at[i])
        for i, (piece, buffer) in enumerate(zip(piece_refs, buffers))
    ]
    for copy in copies:
        copy.start()
    table[total * 8 :, :] = jnp.zeros((8, LANES), jnp.float32)
    for copy, buffer, start in zip(copies, buffers, places):
        copy.wait()

        def fill(i, carry):
            values = buffer[pl.ds(pl.multiple_of(i * chunk, chunk), chunk), :].astype(jnp.float32)
            base = (start + i * chunk) * 8
            for unit in range(units):
                table[pl.ds(base + unit, chunk, stride=8), :] = values[
                    :, unit * LANES : (unit + 1) * LANES
                ]
            return carry

        lax.fori_loop(0, buffer.shape[0] // chunk, fill, 0)

    unroll = 16
    for turn in range(index_ref.shape[0]):

        def step(i, carry):
            for u in range(unroll):
                n = i * unroll + u
                sums[pl.ds(pl.multiple_of(n * 8, 8), 8), :] = tree(
                    [row(index_ref[turn, j, n]) for j in range(first)]
                )
            return carry

        lax.fori_loop(0, near_rows // unroll, step, 0)

        def rest(i, carry):
            @pl.when(index_ref[turn, fan, i] > 0)
            def _():
                for u in range(block):
                    n = i * block + u
                    spot = pl.ds(pl.multiple_of(n * 8, 8), 8)
                    sums[spot, :] = sums[spot, :] + tree(
                        [row(index_ref[turn, j, n]) for j in range(first, fan)]
                    )

            return carry

        if first < fan:
            lax.fori_loop(0, near_rows // block, rest, 0)
        for unit in range(units):
            lanes = slice(unit * LANES, (unit + 1) * LANES)
            out_ref[turn, :, lanes] = sums[pl.ds(unit, near_rows, stride=8), :].astype(jnp.bfloat16)


def partial_sums(index, pieces, places, total, first, block):
    trainers, unused, near_rows = index.shape
    width = pieces[0].shape[1]
    return pl.pallas_call(
        functools.partial(partial_kernel, places, first, block),
        out_shape=jax.ShapeDtypeStruct((trainers, near_rows, width), jnp.bfloat16),
        in_specs=[SMEM] + [pl.BlockSpec(memory_space=pl.ANY)] * len(pieces),
        out_specs=VMEM,
        scratch_shapes=[
            pltpu.VMEM(((total + 1) * 8, LANES), jnp.float32),
            pltpu.VMEM(((near_rows + 1) * 8, LANES), jnp.float32),
        ]
        + [pltpu.VMEM(piece.shape, piece.dtype) for piece in pieces]
        + [pltpu.SemaphoreType.DMA((len(pieces),))],
        compiler_params=pltpu.CompilerParams(vmem_limit_bytes=60 * MIB),
        name="partial_sums",
    )(index, *pieces)


def trainer_kernel(sizes, scale, *refs):
    groups, rows_low, rows_top, classes, class_pad = sizes
    place_ref, labels_ref, adj_ref, column_ref, wl_ref, wt_ref = refs[:6]
    mean_refs, near_refs = refs[6:8], refs[8 : 8 + PLANE]
    logits_ref, keep_ref, send_ref, li, hidden, slope, top_in, wt = refs[8 + PLANE :]
    seeds, fan_top = adj_ref.shape
    near_rows, low_width = li.shape
    feat = low_width // 2
    width = hidden.shape[1]
    capacity = near_refs[0].shape[0]
    here, mine, rep = place_ref[0], place_ref[1], place_ref[2]

    column = column_ref[...]
    rows_cap = lax.broadcasted_iota(jnp.int32, (capacity, near_rows), 0)
    near = None
    for d in range(PLANE):
        marks = jnp.where(rows_cap + d * capacity == column, 1.0, 0.0).astype(jnp.bfloat16)
        term = dot(marks, near_refs[d][...], 0, 0)
        near = term if near is None else near + term
    li[:, :feat] = near.astype(jnp.bfloat16)
    share = feat // 2
    for turn, mean_ref in enumerate(mean_refs):
        core = rep if turn == 0 else 1 - rep
        li[:, pl.ds(pl.multiple_of(feat + core * share, LANES), share)] = mean_ref[...]

    wt[...] = jnp.zeros_like(wt)
    wt[:, :classes] = wt_ref[...].astype(jnp.bfloat16)

    factor = math.sqrt(2.0 / math.pi)
    step = 256
    for c in range(width // step):
        cols = slice(c * step, (c + 1) * step)
        v = dot(li[...], wl_ref[:, cols].astype(jnp.bfloat16))
        square = v * v
        t = jnp.tanh(factor * (v + 0.044715 * v * square))
        half = 0.5 * (1.0 + t)
        hidden[:, cols] = (v * half).astype(jnp.bfloat16)
        slope[:, cols] = half + 0.5 * v * (1.0 - t * t) * factor * (1.0 + 3.0 * 0.044715 * square)

    lane_near = lax.broadcasted_iota(jnp.int32, (seeds, near_rows), 1)
    counts = jnp.zeros((seeds, near_rows), jnp.float32)
    for j in range(fan_top):
        counts = counts + jnp.where(adj_ref[:, j : j + 1] == lane_near, 1.0, 0.0)
    counts = counts.astype(jnp.bfloat16)
    top_in[:, :width] = hidden[:seeds, :]
    top_in[:, width:] = (dot(counts, hidden[...]) / fan_top).astype(jnp.bfloat16)
    logits = dot(top_in[...], wt[...])
    logits_ref[...] = logits[:, :classes]
    lane_class = lax.broadcasted_iota(jnp.int32, (seeds, class_pad), 1)
    powers = jnp.where(lane_class < classes, jnp.exp(logits), 0.0)
    chances = powers / jnp.sum(powers, axis=1, keepdims=True)
    targets = jnp.where(lane_class == labels_ref[...], 1.0, 0.0)
    dlogits = ((chances - targets) * scale).astype(jnp.bfloat16)
    dinput = dot(dlogits, wt[...], 1, 1)
    spread = dinput[:, width:] / fan_top
    high = spread.astype(jnp.bfloat16)
    low = (spread - high.astype(jnp.float32)).astype(jnp.bfloat16)
    dhidden = dot(counts, high, 0, 0) + dot(counts, low, 0, 0)
    hidden[:seeds, :] = ((dhidden[:seeds] + dinput[:, :width]) * slope[:seeds, :]).astype(jnp.bfloat16)
    hidden[seeds:, :] = (dhidden[seeds:] * slope[seeds:, :]).astype(jnp.bfloat16)

    first = rep == 0
    members = low_width // rows_low
    stores = members // 2
    lane_groups = width // class_pad
    sub = rows_top // lane_groups

    def slot(store):
        plane, inner = store // PLANE, store % PLANE
        relative = plane - here
        relative = jnp.where(relative < 0, relative + groups, relative)
        return lax.bitwise_xor(mine, jnp.int32(inner)), relative

    tile = 384
    pair = 2 * rows_low
    for m in range(low_width // tile):
        grad = dot(li[:, m * tile : (m + 1) * tile], hidden[...], 0, 0)
        for s in range(tile // pair):
            even = grad[s * pair : s * pair + rows_low]
            odd = grad[s * pair + rows_low : (s + 1) * pair]
            a, b = slot(m * (tile // pair) + s)
            keep_ref[a, b, :rows_low, :] = jnp.where(first, even, odd)
            send_ref[a, b, :rows_low, :] = jnp.where(first, odd, even).astype(jnp.bfloat16)
    grad = dot(top_in[...], dlogits, 0, 0)
    for s in range(stores):
        even = grad[2 * s * rows_top : (2 * s + 1) * rows_top]
        odd = grad[(2 * s + 1) * rows_top : (2 * s + 2) * rows_top]
        own = jnp.where(first, even, odd)
        other = jnp.where(first, odd, even)
        a, b = slot(s)
        own = jnp.concatenate([own[g * sub : (g + 1) * sub] for g in range(lane_groups)], axis=1)
        other = jnp.concatenate([other[g * sub : (g + 1) * sub] for g in range(lane_groups)], axis=1)
        keep_ref[a, b, rows_low:, :] = own
        send_ref[a, b, rows_low:, :] = other.astype(jnp.bfloat16)


def trainer_step(place, labels, adj_top, column, wl, wt, means, nears, sizes, scale):
    groups, rows_low, rows_top, classes, class_pad = sizes
    seeds = adj_top.shape[0]
    low_width, width = wl.shape
    near_rows = column.shape[1]
    rows = rows_low + rows_top * class_pad // width
    return pl.pallas_call(
        functools.partial(trainer_kernel, sizes, scale),
        out_shape=(
            jax.ShapeDtypeStruct((seeds, classes), jnp.float32),
            jax.ShapeDtypeStruct((PLANE, groups, rows, width), jnp.float32),
            jax.ShapeDtypeStruct((PLANE, groups, rows, width), jnp.bfloat16),
        ),
        in_specs=[SMEM] + [VMEM] * (7 + PLANE),
        out_specs=(VMEM, VMEM, VMEM),
        scratch_shapes=[
            pltpu.VMEM((near_rows, low_width), jnp.bfloat16),
            pltpu.VMEM((near_rows, width), jnp.bfloat16),
            pltpu.VMEM((near_rows, width), jnp.float32),
            pltpu.VMEM((seeds, 2 * width), jnp.bfloat16),
            pltpu.VMEM((2 * width, class_pad), jnp.bfloat16),
        ],
        compiler_params=pltpu.CompilerParams(vmem_limit_bytes=60 * MIB),
        name="trainer_step",
    )(place, labels, adj_top, column, wl, wt, *means, *nears)


def adam_part(gradient, moment, square):
    moment_new = beta_one * moment + (1.0 - beta_one) * gradient
    square_new = beta_two * square + (1.0 - beta_two) * gradient * gradient
    update = moment_new / bias_one / (jnp.sqrt(square_new / bias_two) + adam_eps)
    return learn_rate * update, moment_new, square_new


def adam_kernel(class_pad, parts, *refs):
    part_refs = refs[:parts]
    ml, sl, mt, st, nml, nsl, nmt, nst, delta = refs[parts:]
    rows_low, width = ml.shape
    rows_top, classes = mt.shape
    lane_groups = width // class_pad
    sub = rows_top // lane_groups
    total = part_refs[0][...]
    for ref in part_refs[1:]:
        total = total + ref[...].astype(jnp.float32)
    step, nml[...], nsl[...] = adam_part(total[:rows_low], ml[...], sl[...])
    top = total[rows_low:]
    pieces = []
    for g in range(lane_groups):
        rows = slice(g * sub, (g + 1) * sub)
        gradient = top[:, g * class_pad : g * class_pad + classes]
        piece, nmt[rows, :], nst[rows, :] = adam_part(gradient, mt[rows, :], st[rows, :])
        pieces.append(
            jnp.concatenate([piece, jnp.zeros((sub, class_pad - classes), jnp.float32)], axis=1)
        )
    whole = jnp.concatenate([step, jnp.concatenate(pieces, axis=1)], axis=0)
    delta[...] = whole.astype(jnp.bfloat16)


def adam_share(parts, ml, sl, mt, st, class_pad):
    rows, width = parts[0].shape
    shape = lambda a: jax.ShapeDtypeStruct(a.shape, jnp.float32)
    return pl.pallas_call(
        functools.partial(adam_kernel, class_pad, len(parts)),
        out_shape=(shape(ml), shape(sl), shape(mt), shape(st), jax.ShapeDtypeStruct((rows, width), jnp.bfloat16)),
        in_specs=[VMEM] * (len(parts) + 4),
        out_specs=(VMEM,) * 5,
        compiler_params=pltpu.CompilerParams(vmem_limit_bytes=32 * MIB),
        name="adam_share",
    )(*parts, ml, sl, mt, st)


def apply_kernel(sizes, place_ref, wl, wt, *refs):
    groups, rows_low, rows_top, classes, class_pad = sizes
    delta_refs, (nl, nt) = refs[: 2 * PLANE], refs[2 * PLANE :]
    here, mine, rep = place_ref[0], place_ref[1], place_ref[2]
    width = wl.shape[-1]
    lane_groups = width // class_pad
    sub = rows_top // lane_groups
    for d in range(PLANE):
        for half in range(2):
            for k in range(groups):
                plane = here + k
                plane = jnp.where(plane >= groups, plane - groups, plane)
                store = plane * PLANE + lax.bitwise_xor(mine, jnp.int32(d))
                core = rep if half == 0 else 1 - rep
                position = store * 2 + core
                delta = delta_refs[2 * d + half][k].astype(jnp.float32)
                if len(wl.shape) == 2:
                    rows = pl.ds(pl.multiple_of(position * rows_low, 8), rows_low)
                    nl[rows, :] = wl[rows, :] - delta[:rows_low]
                else:
                    nl[position] = wl[position] - delta[:rows_low]
                for g in range(lane_groups):
                    step = delta[rows_low:, g * class_pad : g * class_pad + classes]
                    if len(wt.shape) == 2:
                        rows = pl.ds(pl.multiple_of(position * rows_top + g * sub, 8), sub)
                        nt[rows, :] = wt[rows, :] - step
                    else:
                        rows = slice(g * sub, (g + 1) * sub)
                        nt[position, rows, :] = wt[position, rows, :] - step


def apply_updates(place, wl, wt, deltas, sizes):
    groups, rows_low, rows_top, classes, class_pad = sizes
    sub = rows_top * class_pad // wl.shape[1]
    low3 = wl if rows_low % 8 == 0 else wl.reshape(-1, rows_low, wl.shape[1])
    top3 = wt if sub % 8 == 0 else wt.reshape(-1, rows_top, wt.shape[1])
    nl, nt = pl.pallas_call(
        functools.partial(apply_kernel, sizes),
        out_shape=(
            jax.ShapeDtypeStruct(low3.shape, jnp.float32),
            jax.ShapeDtypeStruct(top3.shape, jnp.float32),
        ),
        in_specs=[SMEM] + [VMEM] * (2 + len(deltas)),
        out_specs=(VMEM, VMEM),
        compiler_params=pltpu.CompilerParams(vmem_limit_bytes=60 * MIB),
        name="apply_updates",
    )(place, low3, top3, *deltas)
    return nl.reshape(wl.shape), nt.reshape(wt.shape)


def per_device(
    features,
    owners_near,
    slots_near,
    owners_far,
    slots_far,
    adjacency_low,
    adjacency_top,
    labels,
    weights_low,
    weights_top,
    first_low,
    second_low,
    first_top,
    second_top,
):
    stores = lax.axis_size("store")
    groups = stores // PLANE
    members = stores * lax.axis_size("rep")
    index = lax.axis_index("store")
    here, mine, rep = index // PLANE, index % PLANE, lax.axis_index("rep")
    store_rows = features.shape[0]
    half = store_rows // 2
    near_rows, fan = adjacency_low.shape
    capacity = 2 * near_rows // stores
    classes = weights_top.shape[1]
    class_pad = -(-classes // LANES) * LANES
    rows_low, rows_top = first_low.shape[0], first_top.shape[0]
    sizes = (groups, rows_low, rows_top, classes, class_pad)
    bf16 = jnp.bfloat16
    place = jnp.stack([here, mine, rep]).astype(jnp.int32)

    def across(x, distance):
        return lax.ppermute(x, "store", [(i, i ^ distance) for i in range(stores)])

    def along(x, hops):
        return lax.ppermute(x, "store", [(i, (i + hops * PLANE) % stores) for i in range(stores)])

    def sibling(x):
        return lax.ppermute(x, "rep", [(0, 1), (1, 0)])

    share = features.shape[1] // 2
    own = lax.dynamic_slice_in_dim(features, rep * share, share, 1)
    from_x, from_y = across(own, 1), across(own, 2)
    gid_near = owners_near[:, 0] * store_rows + slots_near[:, 0]
    gid_far = owners_far[:, 0] * store_rows + slots_far[:, 0]
    table = jnp.concatenate([gid_near, gid_far]).reshape(-1, LANES)
    table = jnp.pad(table, ((0, -table.shape[0] % 16), (0, 0))).T
    ids, requests, column = compose(
        place, adjacency_low, table, gid_near.reshape(1, near_rows), store_rows, stores, capacity
    )
    pair = jnp.stack([ids, sibling(ids)])
    ids_all = [pair] + [along(pair, -k) for k in range(1, groups)]
    requests = lax.all_to_all(requests.reshape(stores, capacity), "store", 0, 0, tiled=True)
    held = near_rows_held(place, requests, features, groups)
    first, block = min(8, fan), 8
    lists = row_lists(place, ids_all, store_rows, first, block)
    lined = [held[0]] + [along(held[k], k) for k in range(1, groups)]
    corner_a, corner_b = across(from_x[:half], 2), across(from_y[half:], 1)
    pieces = [own, from_x, from_y, corner_a, corner_b]
    places = [0, store_rows, 2 * store_rows, 3 * store_rows, 3 * store_rows + half]

    total = 0.0
    for k in [groups // 2] + [k for k in range(1, groups) if k != groups // 2] + [0]:
        made = partial_sums(lists[k], pieces, places, PLANE * store_rows, first, block)
        total = total + (along(made, k) if k else made).astype(jnp.float32)
    means = (total / fan).astype(bf16)
    means = [means[0], sibling(means[1])]

    nears = []
    for d in range(PLANE):
        sheet = jnp.concatenate([part[d * capacity : (d + 1) * capacity] for part in lined])
        nears.append(across(sheet, d) if d else sheet)

    scale = 1.0 / (labels.shape[0] * members)
    logits, keep, send = trainer_step(
        place,
        labels[:, None],
        adjacency_top,
        column,
        weights_low,
        weights_top,
        means,
        nears,
        sizes,
        scale,
    )
    total = keep + sibling(send).astype(jnp.float32)
    arrived = [across(total[d].astype(bf16), d) for d in range(1, PLANE)]
    total = total[0] + sum(a.astype(jnp.float32) for a in arrived)
    shares = [total[0]] + [along(total[k].astype(bf16), k) for k in range(1, groups)]
    new_first_low, new_second_low, new_first_top, new_second_top, delta = adam_share(
        shares, first_low, second_low, first_top, second_top, class_pad
    )
    lined = jnp.stack([delta] + [along(delta, -k) for k in range(1, groups)])
    sheets = [lined] + [across(lined, d) for d in range(1, PLANE)]
    deltas = []
    for sheet in sheets:
        deltas += [sheet, sibling(sheet)]
    new_low, new_top = apply_updates(place, weights_low, weights_top, deltas, sizes)
    return (logits, new_low, new_first_low, new_second_low, new_top, new_first_top, new_second_top)


def solution(mesh):
    both = P(("store", "rep"), None)
    return jax.shard_map(
        per_device,
        mesh=mesh,
        in_specs=(P("store", None),)
        + (both,) * 6
        + (P(("store", "rep")), P(), P(), both, both, both, both),
        out_specs=(both, P(), both, both, P(), both, both),
        check_vma=False,
    )
```

```python
import functools
import math

import jax
import jax.numpy as jnp
from jax import lax
from jax.experimental import pallas as pl
from jax.experimental.pallas import tpu as pltpu
from jax.sharding import PartitionSpec as P

beta_one = 0.9
beta_two = 0.999
bias_one = 1.0 - 0.9**10
bias_two = 1.0 - 0.999**10
learn_rate = 0.01
adam_eps = 1e-08

PLANE = 4
LANES = 128
MIB = 1024 * 1024

VMEM = pl.BlockSpec(memory_space=pltpu.VMEM)
SMEM = pl.BlockSpec(memory_space=pltpu.SMEM)


def dot(a, b, ca=1, cb=0):
    return lax.dot_general(a, b, (((ca,), (cb,)), ((), ())), preferred_element_type=jnp.float32)


def cut_kernel(first, rows, columns, by_core, place_ref, source_ref, *refs):
    out_ref, done = refs[-2:]
    start = pl.multiple_of(place_ref[2] * rows, 16) if by_core else first
    copy = pltpu.make_async_copy(
        source_ref.at[pl.ds(start, rows), columns[0] : columns[1]], out_ref, done
    )
    copy.start()
    copy.wait()


def cut(place, source, first, rows, columns, after, by_core=False):
    anywhere = pl.BlockSpec(memory_space=pl.ANY)
    return pl.pallas_call(
        functools.partial(cut_kernel, first, rows, columns, by_core),
        out_shape=jax.ShapeDtypeStruct((rows, columns[1] - columns[0]), source.dtype),
        in_specs=[SMEM] + [anywhere] * (1 + len(after)),
        out_specs=anywhere,
        scratch_shapes=[pltpu.SemaphoreType.DMA],
        name="cut_block",
    )(place, source, *after)


def pack_kernel(count, *refs):
    out_ref, done = refs[-2:]
    copies, start = [], 0
    for i, ref in enumerate(refs[:count]):
        rows = ref.shape[0]
        copies.append(
            pltpu.make_async_copy(ref, out_ref.at[start : start + rows, :], done.at[i])
        )
        start += rows
    for copy in copies:
        copy.start()
    for copy in copies:
        copy.wait()


def pack(arrays, after):
    anywhere = pl.BlockSpec(memory_space=pl.ANY)
    rows = sum(array.shape[0] for array in arrays)
    return pl.pallas_call(
        functools.partial(pack_kernel, len(arrays)),
        out_shape=jax.ShapeDtypeStruct((rows, arrays[0].shape[1]), arrays[0].dtype),
        in_specs=[anywhere] * (len(arrays) + len(after)),
        out_specs=anywhere,
        scratch_shapes=[pltpu.SemaphoreType.DMA((len(arrays),))],
        name="pack_blocks",
    )(*arrays, *after)


def compose_kernel(store_rows, groups, capacity, place_ref, adj_ref, table_ref, near_ref, ids_ref, column_ref):
    fan, near_rows = adj_ref.shape
    his = table_ref.shape[1]
    here = place_ref[0]
    table = table_ref[...]
    parts = jnp.concatenate([table // 65536, (table // 256) % 256, table % 256], axis=0)
    parts = parts.astype(jnp.float32).astype(jnp.bfloat16)
    row_hi = lax.broadcasted_iota(jnp.int32, (his, near_rows), 0)
    row_lo = lax.broadcasted_iota(jnp.int32, (LANES, near_rows), 0)
    for column in range(fan):
        position = adj_ref[column : column + 1, :]
        marks = jnp.where(row_hi == position // LANES, 1.0, 0.0).astype(jnp.bfloat16)
        found = dot(parts, marks)
        value = found[:LANES] * 65536.0 + found[LANES : 2 * LANES] * 256.0 + found[2 * LANES :]
        value = jnp.where(row_lo == position % LANES, value, 0.0)
        ids_ref[column : column + 1, :] = jnp.sum(value, axis=0, keepdims=True).astype(jnp.int32)
    near = near_ref[...]
    per_plane = PLANE * store_rows
    plane, row = near // per_plane, near % per_plane + 1
    row_plane = lax.broadcasted_iota(jnp.int32, (groups, near_rows), 0)
    marks = jnp.where(row_plane == plane, 1.0, 0.0)
    earlier = lax.broadcasted_iota(jnp.int32, (near_rows, near_rows), 0) < lax.broadcasted_iota(
        jnp.int32, (near_rows, near_rows), 1
    )
    counts = dot(marks.astype(jnp.bfloat16), jnp.where(earlier, 1.0, 0.0).astype(jnp.bfloat16))
    rank = jnp.sum(counts * marks, axis=0, keepdims=True).astype(jnp.int32)
    wanted = lax.broadcasted_iota(jnp.int32, (groups * capacity, near_rows), 0)
    marks = jnp.where(wanted == plane * capacity + rank, 1.0, 0.0).astype(jnp.bfloat16)
    line = lax.broadcasted_iota(jnp.int32, (8, near_rows), 0)
    halves = jnp.where(line == 0, row // 256, jnp.where(line == 1, row % 256, 0))
    found = dot(halves.astype(jnp.float32).astype(jnp.bfloat16), marks, 1, 1)
    found = (found[0:1] * 256.0 + found[1:2]).astype(jnp.int32)
    for line in range(groups * capacity // near_rows):
        ids_ref[fan + line : fan + line + 1, :] = found[:, line * near_rows : (line + 1) * near_rows]
    hops = here - plane
    hops = jnp.where(hops < 0, hops + groups, hops)
    column_ref[...] = hops * capacity + rank


def compose(place, adjacency, table, near, store_rows, groups, capacity):
    near_rows, fan = adjacency.shape
    rows = fan + groups * capacity // near_rows
    return pl.pallas_call(
        functools.partial(compose_kernel, store_rows, groups, capacity),
        out_shape=(
            jax.ShapeDtypeStruct((rows, near_rows), jnp.int32),
            jax.ShapeDtypeStruct((1, near_rows), jnp.int32),
        ),
        in_specs=[SMEM, VMEM, VMEM, VMEM],
        out_specs=(VMEM, VMEM),
        compiler_params=pltpu.CompilerParams(vmem_limit_bytes=32 * MIB),
        name="compose_ids",
    )(place, adjacency.T, table, near)


def sort_pairs(count):
    pairs = []
    size = 1
    while size < count:
        step = size
        while step >= 1:
            for start in range(step % size, count - step, 2 * step):
                for i in range(min(step, count - start - step)):
                    a, b = start + i, start + i + step
                    if a // (2 * size) == b // (2 * size):
                        pairs.append((a, b))
            step //= 2
        size *= 2
    return pairs


def depths_of(fan):
    return [d for d in (2, 3, 4, 5, 6, 8) if d < fan] + [fan]


def list_kernel(store_rows, fan, capacity, block, place_ref, *refs):
    groups = len(refs) // 2
    ids_refs, out_refs = refs[:groups], refs[groups:]
    here, mine, rep = place_ref[0], place_ref[1], place_ref[2]
    near_rows = ids_refs[0].shape[1]
    per_plane = PLANE * store_rows
    sub = lax.broadcasted_iota(jnp.int32, (near_rows, near_rows), 0)
    lane = lax.broadcasted_iota(jnp.int32, (near_rows, near_rows), 1)
    before = jnp.where(sub < lane, 1.0, 0.0).astype(jnp.bfloat16)
    nodes = lax.broadcasted_iota(jnp.int32, (1, near_rows), 1)
    classes = lax.broadcasted_iota(jnp.int32, (fan + 1, near_rows), 0)

    def turn(row):
        half = store_rows // 2
        distance, slot = lax.bitwise_xor(row // store_rows, mine), row % store_rows
        core, inner = slot // half, slot % half
        other = jnp.where(core == rep, 0, (PLANE - 1) * half)
        return jnp.where(distance == 0, slot, (distance + 1) * half + other + inner)

    for ids_ref, out_ref in zip(ids_refs, out_refs):
        gid = ids_ref[:fan, :]
        held = gid // per_plane == here
        row = jnp.where(held, turn(gid % per_plane), per_plane)
        count = jnp.sum(jnp.where(held, 1, 0), axis=0, keepdims=True)
        rows = [row[j : j + 1] for j in range(fan)]
        for a, b in sort_pairs(fan):
            rows[a], rows[b] = jnp.minimum(rows[a], rows[b]), jnp.maximum(rows[a], rows[b])
        marks = jnp.where(classes == count, 1.0, 0.0)
        rank = dot(marks.astype(jnp.bfloat16), before)
        sizes = jnp.sum(marks, axis=1, keepdims=True)
        larger = jnp.zeros((1, 1), jnp.float32)
        place = jnp.zeros((1, near_rows), jnp.float32)
        ends = {}
        for c in range(fan, -1, -1):
            ends[c] = larger
            place = place + marks[c : c + 1] * (rank[c : c + 1] + larger)
            larger = larger + sizes[c : c + 1]
        order = jnp.where(sub == place.astype(jnp.int32), 1.0, 0.0).astype(jnp.bfloat16)
        lines = jnp.concatenate(rows + [nodes], axis=0)
        parts = jnp.concatenate([lines // 256, lines % 256], axis=0)
        found = dot(parts.astype(jnp.float32).astype(jnp.bfloat16), order, 1, 1)
        found = (found[: fan + 1] * 256.0 + found[fan + 1 :]).astype(jnp.int32)
        out_ref[: fan + 1, :] = found * 8
        ahead = jnp.zeros((1, near_rows), jnp.int32)
        for i, d in enumerate(depths_of(fan)[:-1]):
            blocks = (ends[d].astype(jnp.int32) + (block - 1)) // block
            ahead = ahead + jnp.where(nodes == i, blocks, 0)
        out_ref[fan + 1 : fan + 2, :] = ahead
        lists = jnp.concatenate(
            [ids_ref[i : i + 1, :] for i in range(fan, ids_ref.shape[0])], axis=1
        )
        own = jnp.zeros((1, capacity), jnp.int32)
        for g in range(groups):
            own = own + jnp.where(here == g, lists[:, g * capacity : (g + 1) * capacity], 0)
        own = jnp.where(own == 0, per_plane, turn(own - 1))
        out_ref[fan + 2 : fan + 3, :capacity] = own * 8


def row_lists(place, ids_all, store_rows, fan, capacity, block):
    near_rows = ids_all[0].shape[1]
    groups = len(ids_all)
    return pl.pallas_call(
        functools.partial(list_kernel, store_rows, fan, capacity, block),
        out_shape=(jax.ShapeDtypeStruct((fan + 3, near_rows), jnp.int32),) * groups,
        in_specs=[SMEM] + [VMEM] * groups,
        out_specs=(VMEM,) * groups,
        compiler_params=pltpu.CompilerParams(vmem_limit_bytes=32 * MIB),
        name="row_lists",
    )(place, *ids_all)


def partial_kernel(count, columns, places, capacity, block, *refs):
    index_refs, piece_refs = refs[:count], refs[count : count + len(places)]
    out_ref, table, sums, kept = refs[-5 - len(places) : -1 - len(places)]
    buffers = refs[-1 - len(places) : -1]
    arrived = refs[-1]
    fan, near_rows = index_refs[0].shape[0] - 3, index_refs[0].shape[1]
    units = buffers[0].shape[1] // LANES
    total = table.shape[0] // 8 - 1
    chunk = 256

    def row(at):
        return table[pl.ds(pl.multiple_of(at, 8), 8), :]

    def tree(rows):
        while len(rows) > 1:
            odd = rows[-1:] if len(rows) % 2 else []
            rows = [a + b for a, b in zip(rows[0::2], rows[1::2])] + odd
        return rows[0]

    sources = [piece_refs[0].at[:, columns[0] : columns[1]]] + list(piece_refs[1:])
    copies = [
        pltpu.make_async_copy(source, buffer, arrived.at[i])
        for i, (source, buffer) in enumerate(zip(sources, buffers))
    ]
    for copy in copies:
        copy.start()
    table[total * 8 :, :] = jnp.zeros((8, LANES), jnp.float32)
    for copy, buffer, start in zip(copies, buffers, places):
        copy.wait()

        def fill(i, carry):
            values = buffer[pl.ds(pl.multiple_of(i * chunk, chunk), chunk), :].astype(jnp.float32)
            base = (start + i * chunk) * 8
            for unit in range(units):
                table[pl.ds(base + unit, chunk, stride=8), :] = values[
                    :, unit * LANES : (unit + 1) * LANES
                ]
            return carry

        lax.fori_loop(0, buffer.shape[0] // chunk, fill, 0)

    near_unroll = 16
    for turn, index_ref in enumerate(index_refs):
        begin = 0
        depths = depths_of(fan)
        for at in range(len(depths) - 1, -1, -1):
            depth = depths[at]

            def step(i, carry):
                for u in range(block):
                    n = i * block + u
                    spot = pl.multiple_of(index_ref[fan, n], 8)
                    sums[pl.ds(spot, 8), :] = tree([row(index_ref[j, n]) for j in range(depth)])
                return carry

            end = index_ref[fan + 1, at - 1] if at else near_rows // block
            lax.fori_loop(begin, end, step, 0)
            begin = end

        def near(i, carry):
            for u in range(near_unroll):
                n = i * near_unroll + u
                kept[pl.ds(pl.multiple_of(n * 8, 8), 8), :] = row(index_ref[fan + 2, n])
            return carry

        lax.fori_loop(0, capacity // near_unroll, near, 0)
        for unit in range(units):
            lanes = slice(unit * LANES, (unit + 1) * LANES)
            out_ref[turn, :near_rows, lanes] = sums[
                pl.ds(unit, near_rows, stride=8), :
            ].astype(jnp.bfloat16)
            out_ref[turn, near_rows:, lanes] = kept[
                pl.ds(unit, capacity, stride=8), :
            ].astype(jnp.bfloat16)


def partial_sums(lists, pieces, places, columns, total, capacity, block, after):
    near_rows = lists[0].shape[1]
    width = columns[1] - columns[0]
    rows = [piece.shape[0] for piece in pieces]
    return pl.pallas_call(
        functools.partial(partial_kernel, len(lists), columns, places, capacity, block),
        out_shape=jax.ShapeDtypeStruct((len(lists), near_rows + capacity, width), jnp.bfloat16),
        in_specs=[SMEM] * len(lists) + [pl.BlockSpec(memory_space=pl.ANY)] * (len(pieces) + len(after)),
        out_specs=VMEM,
        scratch_shapes=[
            pltpu.VMEM(((total + 1) * 8, LANES), jnp.float32),
            pltpu.VMEM(((near_rows + 1) * 8, LANES), jnp.float32),
            pltpu.VMEM(((capacity + 1) * 8, LANES), jnp.float32),
        ]
        + [pltpu.VMEM((count, width), jnp.bfloat16) for count in rows]
        + [pltpu.SemaphoreType.DMA((len(pieces),))],
        compiler_params=pltpu.CompilerParams(vmem_limit_bytes=52 * MIB),
        name="partial_sums",
    )(*lists, *pieces, *after)


def trainer_kernel(sizes, scale, *refs):
    groups, rows_low, rows_top, classes, class_pad = sizes
    place_ref, labels_ref, adj_ref, column_ref, wl_ref, wt_ref = refs[:6]
    block_refs = refs[6:-8]
    logits_ref, keep_ref, send_ref, li, hidden, slope, top_in, wt = refs[-8:]
    seeds, fan_top = adj_ref.shape
    near_rows, low_width = li.shape
    feat = low_width // 2
    width = hidden.shape[1]
    capacity = block_refs[0].shape[0] - near_rows
    here, mine, rep = place_ref[0], place_ref[1], place_ref[2]
    fan_low = place_ref[3].astype(jnp.float32)

    column = column_ref[...]
    rows_cap = lax.broadcasted_iota(jnp.int32, (capacity, near_rows), 0)
    marks = [
        jnp.where(rows_cap + k * capacity == column, 1.0, 0.0).astype(jnp.bfloat16)
        for k in range(groups)
    ]
    for part in range(len(block_refs) // groups):
        blocks = block_refs[part * groups : (part + 1) * groups]
        share = blocks[0].shape[1]
        near = total = None
        for k in range(groups):
            term = dot(marks[k], blocks[k][near_rows:, :], 0, 0)
            near = term if near is None else near + term
            term = blocks[k][:near_rows, :].astype(jnp.float32)
            total = term if total is None else total + term
        li[:, part * share : (part + 1) * share] = near.astype(jnp.bfloat16)
        li[:, feat + part * share : feat + (part + 1) * share] = (total / fan_low).astype(jnp.bfloat16)

    wt[...] = jnp.zeros_like(wt)
    wt[:, :classes] = wt_ref[...].astype(jnp.bfloat16)

    factor = math.sqrt(2.0 / math.pi)
    step = 256
    for c in range(width // step):
        cols = slice(c * step, (c + 1) * step)
        v = dot(li[...], wl_ref[:, cols].astype(jnp.bfloat16))
        square = v * v
        t = jnp.tanh(factor * (v + 0.044715 * v * square))
        half = 0.5 * (1.0 + t)
        hidden[:, cols] = (v * half).astype(jnp.bfloat16)
        slope[:, cols] = half + 0.5 * v * (1.0 - t * t) * factor * (1.0 + 3.0 * 0.044715 * square)

    lane_near = lax.broadcasted_iota(jnp.int32, (seeds, near_rows), 1)
    counts = jnp.zeros((seeds, near_rows), jnp.float32)
    for j in range(fan_top):
        counts = counts + jnp.where(adj_ref[:, j : j + 1] == lane_near, 1.0, 0.0)
    counts = counts.astype(jnp.bfloat16)
    top_in[:, :width] = hidden[:seeds, :]
    top_in[:, width:] = (dot(counts, hidden[...]) / fan_top).astype(jnp.bfloat16)
    logits = dot(top_in[...], wt[...])
    logits_ref[...] = logits[:, :classes]
    lane_class = lax.broadcasted_iota(jnp.int32, (seeds, class_pad), 1)
    powers = jnp.where(lane_class < classes, jnp.exp(logits), 0.0)
    chances = powers / jnp.sum(powers, axis=1, keepdims=True)
    targets = jnp.where(lane_class == labels_ref[...], 1.0, 0.0)
    dlogits = ((chances - targets) * scale).astype(jnp.bfloat16)
    dinput = dot(dlogits, wt[...], 1, 1)
    spread = dinput[:, width:] / fan_top
    high = spread.astype(jnp.bfloat16)
    low = (spread - high.astype(jnp.float32)).astype(jnp.bfloat16)
    dhidden = dot(counts, high, 0, 0) + dot(counts, low, 0, 0)
    hidden[:seeds, :] = ((dhidden[:seeds] + dinput[:, :width]) * slope[:seeds, :]).astype(jnp.bfloat16)
    hidden[seeds:, :] = (dhidden[seeds:] * slope[seeds:, :]).astype(jnp.bfloat16)

    first = rep == 0
    members = low_width // rows_low
    stores = members // 2
    lane_groups = width // class_pad
    sub = rows_top // lane_groups

    def slot(store):
        plane, inner = store // PLANE, store % PLANE
        relative = plane - here
        relative = jnp.where(relative < 0, relative + groups, relative)
        return lax.bitwise_xor(mine, jnp.int32(inner)), relative

    tile = 384
    pair = 2 * rows_low
    for m in range(low_width // tile):
        grad = dot(li[:, m * tile : (m + 1) * tile], hidden[...], 0, 0)
        for s in range(tile // pair):
            even = grad[s * pair : s * pair + rows_low]
            odd = grad[s * pair + rows_low : (s + 1) * pair]
            a, b = slot(m * (tile // pair) + s)
            keep_ref[a, b, :rows_low, :] = jnp.where(first, even, odd)
            send_ref[a, b, :rows_low, :] = jnp.where(first, odd, even).astype(jnp.bfloat16)
    grad = dot(top_in[...], dlogits, 0, 0)
    for s in range(stores):
        even = grad[2 * s * rows_top : (2 * s + 1) * rows_top]
        odd = grad[(2 * s + 1) * rows_top : (2 * s + 2) * rows_top]
        own = jnp.where(first, even, odd)
        other = jnp.where(first, odd, even)
        a, b = slot(s)
        own = jnp.concatenate([own[g * sub : (g + 1) * sub] for g in range(lane_groups)], axis=1)
        other = jnp.concatenate([other[g * sub : (g + 1) * sub] for g in range(lane_groups)], axis=1)
        keep_ref[a, b, rows_low:, :] = own
        send_ref[a, b, rows_low:, :] = other.astype(jnp.bfloat16)


def trainer_step(place, labels, adj_top, column, wl, wt, blocks, sizes, scale):
    groups, rows_low, rows_top, classes, class_pad = sizes
    seeds = adj_top.shape[0]
    low_width, width = wl.shape
    near_rows = column.shape[1]
    rows = rows_low + rows_top * class_pad // width
    return pl.pallas_call(
        functools.partial(trainer_kernel, sizes, scale),
        out_shape=(
            jax.ShapeDtypeStruct((seeds, classes), jnp.float32),
            jax.ShapeDtypeStruct((PLANE, groups, rows, width), jnp.float32),
            jax.ShapeDtypeStruct((PLANE, groups, rows, width), jnp.bfloat16),
        ),
        in_specs=[SMEM] + [VMEM] * (5 + len(blocks)),
        out_specs=(VMEM, VMEM, VMEM),
        scratch_shapes=[
            pltpu.VMEM((near_rows, low_width), jnp.bfloat16),
            pltpu.VMEM((near_rows, width), jnp.bfloat16),
            pltpu.VMEM((near_rows, width), jnp.float32),
            pltpu.VMEM((seeds, 2 * width), jnp.bfloat16),
            pltpu.VMEM((2 * width, class_pad), jnp.bfloat16),
        ],
        compiler_params=pltpu.CompilerParams(vmem_limit_bytes=60 * MIB),
        name="trainer_step",
    )(place, labels, adj_top, column, wl, wt, *blocks)


def adam_part(gradient, moment, square):
    moment_new = beta_one * moment + (1.0 - beta_one) * gradient
    square_new = beta_two * square + (1.0 - beta_two) * gradient * gradient
    update = moment_new / bias_one / (jnp.sqrt(square_new / bias_two) + adam_eps)
    return learn_rate * update, moment_new, square_new


def adam_kernel(class_pad, parts, *refs):
    part_refs = refs[:parts]
    ml, sl, mt, st, nml, nsl, nmt, nst, delta = refs[parts:]
    rows_low, width = ml.shape
    rows_top, classes = mt.shape
    lane_groups = width // class_pad
    sub = rows_top // lane_groups
    total = part_refs[0][...]
    for ref in part_refs[1:]:
        total = total + ref[...].astype(jnp.float32)
    step, nml[...], nsl[...] = adam_part(total[:rows_low], ml[...], sl[...])
    top = total[rows_low:]
    pieces = []
    for g in range(lane_groups):
        rows = slice(g * sub, (g + 1) * sub)
        gradient = top[:, g * class_pad : g * class_pad + classes]
        piece, nmt[rows, :], nst[rows, :] = adam_part(gradient, mt[rows, :], st[rows, :])
        pieces.append(
            jnp.concatenate([piece, jnp.zeros((sub, class_pad - classes), jnp.float32)], axis=1)
        )
    whole = jnp.concatenate([step, jnp.concatenate(pieces, axis=1)], axis=0)
    delta[...] = whole.astype(jnp.bfloat16)


def adam_share(parts, ml, sl, mt, st, class_pad):
    rows, width = parts[0].shape
    shape = lambda a: jax.ShapeDtypeStruct(a.shape, jnp.float32)
    return pl.pallas_call(
        functools.partial(adam_kernel, class_pad, len(parts)),
        out_shape=(shape(ml), shape(sl), shape(mt), shape(st), jax.ShapeDtypeStruct((rows, width), jnp.bfloat16)),
        in_specs=[VMEM] * (len(parts) + 4),
        out_specs=(VMEM,) * 5,
        compiler_params=pltpu.CompilerParams(vmem_limit_bytes=32 * MIB),
        name="adam_share",
    )(*parts, ml, sl, mt, st)


def apply_kernel(sizes, place_ref, wl, wt, *refs):
    groups, rows_low, rows_top, classes, class_pad = sizes
    delta_refs, (nl, nt) = refs[: 2 * PLANE], refs[2 * PLANE :]
    here, mine, rep = place_ref[0], place_ref[1], place_ref[2]
    width = wl.shape[-1]
    lane_groups = width // class_pad
    sub = rows_top // lane_groups
    for d in range(PLANE):
        for half in range(2):
            for k in range(groups):
                plane = here + k
                plane = jnp.where(plane >= groups, plane - groups, plane)
                store = plane * PLANE + lax.bitwise_xor(mine, jnp.int32(d))
                core = rep if half == 0 else 1 - rep
                position = store * 2 + core
                delta = delta_refs[2 * d + half][k].astype(jnp.float32)
                if len(wl.shape) == 2:
                    rows = pl.ds(pl.multiple_of(position * rows_low, 8), rows_low)
                    nl[rows, :] = wl[rows, :] - delta[:rows_low]
                else:
                    nl[position] = wl[position] - delta[:rows_low]
                for g in range(lane_groups):
                    step = delta[rows_low:, g * class_pad : g * class_pad + classes]
                    if len(wt.shape) == 2:
                        rows = pl.ds(pl.multiple_of(position * rows_top + g * sub, 8), sub)
                        nt[rows, :] = wt[rows, :] - step
                    else:
                        rows = slice(g * sub, (g + 1) * sub)
                        nt[position, rows, :] = wt[position, rows, :] - step


def apply_updates(place, wl, wt, deltas, sizes):
    groups, rows_low, rows_top, classes, class_pad = sizes
    sub = rows_top * class_pad // wl.shape[1]
    low3 = wl if rows_low % 8 == 0 else wl.reshape(-1, rows_low, wl.shape[1])
    top3 = wt if sub % 8 == 0 else wt.reshape(-1, rows_top, wt.shape[1])
    nl, nt = pl.pallas_call(
        functools.partial(apply_kernel, sizes),
        out_shape=(
            jax.ShapeDtypeStruct(low3.shape, jnp.float32),
            jax.ShapeDtypeStruct(top3.shape, jnp.float32),
        ),
        in_specs=[SMEM] + [VMEM] * (2 + len(deltas)),
        out_specs=(VMEM, VMEM),
        compiler_params=pltpu.CompilerParams(vmem_limit_bytes=60 * MIB),
        name="apply_updates",
    )(place, low3, top3, *deltas)
    return nl.reshape(wl.shape), nt.reshape(wt.shape)


def per_device(
    features,
    owners_near,
    slots_near,
    owners_far,
    slots_far,
    adjacency_low,
    adjacency_top,
    labels,
    weights_low,
    weights_top,
    first_low,
    second_low,
    first_top,
    second_top,
):
    stores = lax.axis_size("store")
    groups = stores // PLANE
    members = stores * lax.axis_size("rep")
    index = lax.axis_index("store")
    here, mine, rep = index // PLANE, index % PLANE, lax.axis_index("rep")
    store_rows = features.shape[0]
    half = store_rows // 2
    near_rows, fan = adjacency_low.shape
    capacity = min(near_rows, PLANE * (2 * near_rows // stores))
    classes = weights_top.shape[1]
    class_pad = -(-classes // LANES) * LANES
    rows_low, rows_top = first_low.shape[0], first_top.shape[0]
    sizes = (groups, rows_low, rows_top, classes, class_pad)
    bf16 = jnp.bfloat16
    place = jnp.stack([here, mine, rep, jnp.int32(fan)]).astype(jnp.int32)

    def across(x, distance):
        return lax.ppermute(x, "store", [(i, i ^ distance) for i in range(stores)])

    def along(x, hops):
        return lax.ppermute(x, "store", [(i, (i + hops * PLANE) % stores) for i in range(stores)])

    def sibling(x):
        return lax.ppermute(x, "rep", [(0, 1), (1, 0)])

    gid_near = owners_near[:, 0] * store_rows + slots_near[:, 0]
    gid_far = owners_far[:, 0] * store_rows + slots_far[:, 0]
    table = jnp.concatenate([gid_near, gid_far]).reshape(-1, LANES)
    table = jnp.pad(table, ((0, -table.shape[0] % 16), (0, 0))).T
    ids, column = compose(
        place, adjacency_low, table, gid_near.reshape(1, near_rows), store_rows, groups, capacity
    )
    ids_all = [ids] + [along(ids, -k) for k in range(1, groups)]
    block = 16
    lists = row_lists(place, ids_all, store_rows, fan, capacity, block)

    share = features.shape[1] // 2
    quarter = half // 2
    places = [0, store_rows, store_rows + 3 * half]
    far = groups // 2
    calls = [[far], [k for k in range(1, groups) if k != far], [0]]
    blocks, pieces, waits = {}, (), ()
    first, second = (lists[0],), ()
    for part in range(2):
        columns, whole = (part * share, (part + 1) * share), (0, share)
        own = cut(place, features, 0, half, columns, pieces[1:], True)
        from_x, from_y = across(own, 1), across(own, 2)
        corner_a = across(cut(place, from_x, 0, quarter, whole, first), 2)
        corner_b = across(cut(place, from_y, quarter, quarter, whole, first), 1)
        brought = pack([from_x, from_y, corner_a, corner_b], second)
        pieces = (features, brought, sibling(brought))
        for turns in calls:
            made = partial_sums(
                [lists[k] for k in turns],
                pieces,
                places,
                columns,
                PLANE * store_rows,
                capacity,
                block,
                waits,
            )
            waits = (made,)
            for i, k in enumerate(turns):
                blocks[part, k] = along(made[i], k) if k else made[i]
            if turns == calls[0]:
                first, second = (made,), (blocks[part, far],)
            if turns == calls[1]:
                second += (made,)

    scale = 1.0 / (labels.shape[0] * members)
    logits, keep, send = trainer_step(
        place,
        labels[:, None],
        adjacency_top,
        column,
        weights_low,
        weights_top,
        [blocks[part, k] for part in range(2) for k in range(groups)],
        sizes,
        scale,
    )
    total = keep + sibling(send).astype(jnp.float32)
    arrived = [across(total[d].astype(bf16), d) for d in range(1, PLANE)]
    total = total[0] + sum(a.astype(jnp.float32) for a in arrived)
    shares = [total[0]] + [along(total[k].astype(bf16), k) for k in range(1, groups)]
    new_first_low, new_second_low, new_first_top, new_second_top, delta = adam_share(
        shares, first_low, second_low, first_top, second_top, class_pad
    )
    lined = jnp.stack([delta] + [along(delta, -k) for k in range(1, groups)])
    sheets = [lined] + [across(lined, d) for d in range(1, PLANE)]
    deltas = []
    for sheet in sheets:
        deltas += [sheet, sibling(sheet)]
    new_low, new_top = apply_updates(place, weights_low, weights_top, deltas, sizes)
    return (logits, new_low, new_first_low, new_second_low, new_top, new_first_top, new_second_top)


def solution(mesh):
    both = P(("store", "rep"), None)
    return jax.shard_map(
        per_device,
        mesh=mesh,
        in_specs=(P("store", None),)
        + (both,) * 6
        + (P(("store", "rep")), P(), P(), both, both, both, both),
        out_specs=(both, P(), both, both, P(), both, both),
        check_vma=False,
    )
```

```python
import functools
import math

import jax
import jax.numpy as jnp
from jax import lax
from jax.experimental import pallas as pl
from jax.experimental.pallas import tpu as pltpu
from jax.sharding import PartitionSpec as P

beta_one = 0.9
beta_two = 0.999
bias_one = 1.0 - 0.9**10
bias_two = 1.0 - 0.999**10
learn_rate = 0.01
adam_eps = 1e-08

PLANE = 4
LANES = 128
MIB = 1024 * 1024

VMEM = pl.BlockSpec(memory_space=pltpu.VMEM)
SMEM = pl.BlockSpec(memory_space=pltpu.SMEM)


def dot(a, b, ca=1, cb=0):
    return lax.dot_general(a, b, (((ca,), (cb,)), ((), ())), preferred_element_type=jnp.float32)


def cut_kernel(first, rows, columns, by_core, place_ref, source_ref, *refs):
    out_ref, done = refs[-2:]
    start = pl.multiple_of(place_ref[2] * rows, 16) if by_core else first
    copy = pltpu.make_async_copy(
        source_ref.at[pl.ds(start, rows), columns[0] : columns[1]], out_ref, done
    )
    copy.start()
    copy.wait()


def cut(place, source, first, rows, columns, after, by_core=False):
    anywhere = pl.BlockSpec(memory_space=pl.ANY)
    return pl.pallas_call(
        functools.partial(cut_kernel, first, rows, columns, by_core),
        out_shape=jax.ShapeDtypeStruct((rows, columns[1] - columns[0]), source.dtype),
        in_specs=[SMEM] + [anywhere] * (1 + len(after)),
        out_specs=VMEM,
        scratch_shapes=[pltpu.SemaphoreType.DMA],
        name="cut_block",
    )(place, source, *after)


def pack_kernel(count, *refs):
    out_ref, done = refs[-2:]
    copies, start = [], 0
    for i, ref in enumerate(refs[:count]):
        rows = ref.shape[0]
        copies.append(
            pltpu.make_async_copy(ref, out_ref.at[start : start + rows, :], done.at[i])
        )
        start += rows
    for copy in copies:
        copy.start()
    for copy in copies:
        copy.wait()


def pack(arrays, after):
    anywhere = pl.BlockSpec(memory_space=pl.ANY)
    rows = sum(array.shape[0] for array in arrays)
    return pl.pallas_call(
        functools.partial(pack_kernel, len(arrays)),
        out_shape=jax.ShapeDtypeStruct((rows, arrays[0].shape[1]), arrays[0].dtype),
        in_specs=[anywhere] * (len(arrays) + len(after)),
        out_specs=VMEM,
        scratch_shapes=[pltpu.SemaphoreType.DMA((len(arrays),))],
        name="pack_blocks",
    )(*arrays, *after)


def compose_kernel(store_rows, groups, capacity, place_ref, adj_ref, table_ref, near_ref, ids_ref, column_ref):
    fan, near_rows = adj_ref.shape
    his = table_ref.shape[1]
    here = place_ref[0]
    table = table_ref[...]
    parts = jnp.concatenate([table // 65536, (table // 256) % 256, table % 256], axis=0)
    parts = parts.astype(jnp.float32).astype(jnp.bfloat16)
    row_hi = lax.broadcasted_iota(jnp.int32, (his, near_rows), 0)
    row_lo = lax.broadcasted_iota(jnp.int32, (LANES, near_rows), 0)
    for column in range(fan):
        position = adj_ref[column : column + 1, :]
        marks = jnp.where(row_hi == position // LANES, 1.0, 0.0).astype(jnp.bfloat16)
        found = dot(parts, marks)
        value = found[:LANES] * 65536.0 + found[LANES : 2 * LANES] * 256.0 + found[2 * LANES :]
        value = jnp.where(row_lo == position % LANES, value, 0.0)
        ids_ref[column : column + 1, :] = jnp.sum(value, axis=0, keepdims=True).astype(jnp.int32)
    near = near_ref[...]
    per_plane = PLANE * store_rows
    plane, row = near // per_plane, near % per_plane + 1
    row_plane = lax.broadcasted_iota(jnp.int32, (groups, near_rows), 0)
    marks = jnp.where(row_plane == plane, 1.0, 0.0)
    earlier = lax.broadcasted_iota(jnp.int32, (near_rows, near_rows), 0) < lax.broadcasted_iota(
        jnp.int32, (near_rows, near_rows), 1
    )
    counts = dot(marks.astype(jnp.bfloat16), jnp.where(earlier, 1.0, 0.0).astype(jnp.bfloat16))
    rank = jnp.sum(counts * marks, axis=0, keepdims=True).astype(jnp.int32)
    wanted = lax.broadcasted_iota(jnp.int32, (groups * capacity, near_rows), 0)
    marks = jnp.where(wanted == plane * capacity + rank, 1.0, 0.0).astype(jnp.bfloat16)
    line = lax.broadcasted_iota(jnp.int32, (8, near_rows), 0)
    halves = jnp.where(line == 0, row // 256, jnp.where(line == 1, row % 256, 0))
    found = dot(halves.astype(jnp.float32).astype(jnp.bfloat16), marks, 1, 1)
    found = (found[0:1] * 256.0 + found[1:2]).astype(jnp.int32)
    for line in range(groups * capacity // near_rows):
        ids_ref[fan + line : fan + line + 1, :] = found[:, line * near_rows : (line + 1) * near_rows]
    hops = here - plane
    hops = jnp.where(hops < 0, hops + groups, hops)
    column_ref[...] = hops * capacity + rank


def compose(place, adjacency, table, near, store_rows, groups, capacity):
    near_rows, fan = adjacency.shape
    rows = fan + groups * capacity // near_rows
    return pl.pallas_call(
        functools.partial(compose_kernel, store_rows, groups, capacity),
        out_shape=(
            jax.ShapeDtypeStruct((rows, near_rows), jnp.int32),
            jax.ShapeDtypeStruct((1, near_rows), jnp.int32),
        ),
        in_specs=[SMEM, VMEM, VMEM, VMEM],
        out_specs=(VMEM, VMEM),
        compiler_params=pltpu.CompilerParams(vmem_limit_bytes=32 * MIB),
        name="compose_ids",
    )(place, adjacency.T, table, near)


def sort_pairs(count):
    pairs = []
    size = 1
    while size < count:
        step = size
        while step >= 1:
            for start in range(step % size, count - step, 2 * step):
                for i in range(min(step, count - start - step)):
                    a, b = start + i, start + i + step
                    if a // (2 * size) == b // (2 * size):
                        pairs.append((a, b))
            step //= 2
        size *= 2
    return pairs


def depths_of(fan):
    return [d for d in (2, 3, 4, 5, 6, 8) if d < fan] + [fan]


def list_kernel(store_rows, fan, capacity, block, place_ref, *refs):
    groups = len(refs) // 2
    ids_refs, out_refs = refs[:groups], refs[groups:]
    here, mine, rep = place_ref[0], place_ref[1], place_ref[2]
    near_rows = ids_refs[0].shape[1]
    per_plane = PLANE * store_rows
    sub = lax.broadcasted_iota(jnp.int32, (near_rows, near_rows), 0)
    lane = lax.broadcasted_iota(jnp.int32, (near_rows, near_rows), 1)
    before = jnp.where(sub < lane, 1.0, 0.0).astype(jnp.bfloat16)
    nodes = lax.broadcasted_iota(jnp.int32, (1, near_rows), 1)
    classes = lax.broadcasted_iota(jnp.int32, (fan + 1, near_rows), 0)

    def turn(row):
        half = store_rows // 2
        distance, slot = lax.bitwise_xor(row // store_rows, mine), row % store_rows
        core, inner = slot // half, slot % half
        other = jnp.where(core == rep, 0, (PLANE - 1) * half)
        return jnp.where(distance == 0, slot, (distance + 1) * half + other + inner)

    for ids_ref, out_ref in zip(ids_refs, out_refs):
        gid = ids_ref[:fan, :]
        held = gid // per_plane == here
        row = jnp.where(held, turn(gid % per_plane), per_plane)
        count = jnp.sum(jnp.where(held, 1, 0), axis=0, keepdims=True)
        rows = [row[j : j + 1] for j in range(fan)]
        for a, b in sort_pairs(fan):
            rows[a], rows[b] = jnp.minimum(rows[a], rows[b]), jnp.maximum(rows[a], rows[b])
        marks = jnp.where(classes == count, 1.0, 0.0)
        rank = dot(marks.astype(jnp.bfloat16), before)
        sizes = jnp.sum(marks, axis=1, keepdims=True)
        larger = jnp.zeros((1, 1), jnp.float32)
        place = jnp.zeros((1, near_rows), jnp.float32)
        ends = {}
        for c in range(fan, -1, -1):
            ends[c] = larger
            place = place + marks[c : c + 1] * (rank[c : c + 1] + larger)
            larger = larger + sizes[c : c + 1]
        order = jnp.where(sub == place.astype(jnp.int32), 1.0, 0.0).astype(jnp.bfloat16)
        lines = jnp.concatenate(rows + [nodes], axis=0)
        parts = jnp.concatenate([lines // 256, lines % 256], axis=0)
        found = dot(parts.astype(jnp.float32).astype(jnp.bfloat16), order, 1, 1)
        found = (found[: fan + 1] * 256.0 + found[fan + 1 :]).astype(jnp.int32)
        out_ref[: fan + 1, :] = found * 8
        ahead = jnp.zeros((1, near_rows), jnp.int32)
        for i, d in enumerate(depths_of(fan)[:-1]):
            blocks = (ends[d].astype(jnp.int32) + (block - 1)) // block
            ahead = ahead + jnp.where(nodes == i, blocks, 0)
        out_ref[fan + 1 : fan + 2, :] = ahead
        lists = jnp.concatenate(
            [ids_ref[i : i + 1, :] for i in range(fan, ids_ref.shape[0])], axis=1
        )
        own = jnp.zeros((1, capacity), jnp.int32)
        for g in range(groups):
            own = own + jnp.where(here == g, lists[:, g * capacity : (g + 1) * capacity], 0)
        own = jnp.where(own == 0, per_plane, turn(own - 1))
        out_ref[fan + 2 : fan + 3, :capacity] = own * 8


def row_lists(place, ids_all, store_rows, fan, capacity, block):
    near_rows = ids_all[0].shape[1]
    groups = len(ids_all)
    return pl.pallas_call(
        functools.partial(list_kernel, store_rows, fan, capacity, block),
        out_shape=(jax.ShapeDtypeStruct((fan + 3, near_rows), jnp.int32),) * groups,
        in_specs=[SMEM] + [VMEM] * groups,
        out_specs=(VMEM,) * groups,
        compiler_params=pltpu.CompilerParams(vmem_limit_bytes=32 * MIB),
        name="row_lists",
    )(place, *ids_all)


def partial_kernel(count, columns, places, capacity, block, *refs):
    index_refs, piece_refs = refs[:count], refs[count : count + len(places)]
    out_ref, table, sums, kept = refs[-5 - len(places) : -1 - len(places)]
    buffers = refs[-1 - len(places) : -1]
    arrived = refs[-1]
    fan, near_rows = index_refs[0].shape[0] - 3, index_refs[0].shape[1]
    units = buffers[0].shape[1] // LANES
    total = table.shape[0] // 8 - 1
    chunk = 256

    def row(at):
        return table[pl.ds(pl.multiple_of(at, 8), 8), :]

    def tree(rows):
        while len(rows) > 1:
            odd = rows[-1:] if len(rows) % 2 else []
            rows = [a + b for a, b in zip(rows[0::2], rows[1::2])] + odd
        return rows[0]

    sources = [piece_refs[0].at[:, columns[0] : columns[1]]] + list(piece_refs[1:])
    copies = [
        pltpu.make_async_copy(source, buffer, arrived.at[i])
        for i, (source, buffer) in enumerate(zip(sources, buffers))
    ]
    for copy in copies:
        copy.start()
    table[total * 8 :, :] = jnp.zeros((8, LANES), jnp.float32)
    for copy, buffer, start in zip(copies, buffers, places):
        copy.wait()

        def fill(i, carry):
            values = buffer[pl.ds(pl.multiple_of(i * chunk, chunk), chunk), :].astype(jnp.float32)
            base = (start + i * chunk) * 8
            for unit in range(units):
                table[pl.ds(base + unit, chunk, stride=8), :] = values[
                    :, unit * LANES : (unit + 1) * LANES
                ]
            return carry

        lax.fori_loop(0, buffer.shape[0] // chunk, fill, 0)

    near_unroll = 16
    for turn, index_ref in enumerate(index_refs):
        begin = 0
        depths = depths_of(fan)
        for at in range(len(depths) - 1, -1, -1):
            depth = depths[at]

            def step(i, carry):
                for u in range(block):
                    n = i * block + u
                    spot = pl.multiple_of(index_ref[fan, n], 8)
                    sums[pl.ds(spot, 8), :] = tree([row(index_ref[j, n]) for j in range(depth)])
                return carry

            end = index_ref[fan + 1, at - 1] if at else near_rows // block
            lax.fori_loop(begin, end, step, 0)
            begin = end

        def near(i, carry):
            for u in range(near_unroll):
                n = i * near_unroll + u
                kept[pl.ds(pl.multiple_of(n * 8, 8), 8), :] = row(index_ref[fan + 2, n])
            return carry

        lax.fori_loop(0, capacity // near_unroll, near, 0)
        for unit in range(units):
            lanes = slice(unit * LANES, (unit + 1) * LANES)
            out_ref[turn, :near_rows, lanes] = sums[
                pl.ds(unit, near_rows, stride=8), :
            ].astype(jnp.bfloat16)
            out_ref[turn, near_rows:, lanes] = kept[
                pl.ds(unit, capacity, stride=8), :
            ].astype(jnp.bfloat16)


def partial_sums(lists, pieces, places, columns, total, capacity, block, after):
    near_rows = lists[0].shape[1]
    width = columns[1] - columns[0]
    rows = [piece.shape[0] for piece in pieces]
    return pl.pallas_call(
        functools.partial(partial_kernel, len(lists), columns, places, capacity, block),
        out_shape=jax.ShapeDtypeStruct((len(lists), near_rows + capacity, width), jnp.bfloat16),
        in_specs=[SMEM] * len(lists) + [pl.BlockSpec(memory_space=pl.ANY)] * (len(pieces) + len(after)),
        out_specs=VMEM,
        scratch_shapes=[
            pltpu.VMEM(((total + 1) * 8, LANES), jnp.float32),
            pltpu.VMEM(((near_rows + 1) * 8, LANES), jnp.float32),
            pltpu.VMEM(((capacity + 1) * 8, LANES), jnp.float32),
        ]
        + [pltpu.VMEM((count, width), jnp.bfloat16) for count in rows]
        + [pltpu.SemaphoreType.DMA((len(pieces),))],
        compiler_params=pltpu.CompilerParams(vmem_limit_bytes=52 * MIB),
        name="partial_sums",
    )(*lists, *pieces, *after)


def trainer_kernel(sizes, scale, *refs):
    groups, rows_low, rows_top, classes, class_pad = sizes
    place_ref, labels_ref, adj_ref, column_ref, wl_ref, wt_ref = refs[:6]
    block_refs = refs[6:-8]
    logits_ref, keep_ref, send_ref, li, hidden, slope, top_in, wt = refs[-8:]
    seeds, fan_top = adj_ref.shape
    near_rows, low_width = li.shape
    feat = low_width // 2
    width = hidden.shape[1]
    capacity = block_refs[0].shape[0] - near_rows
    here, mine, rep = place_ref[0], place_ref[1], place_ref[2]
    fan_low = place_ref[3].astype(jnp.float32)

    column = column_ref[...]
    rows_cap = lax.broadcasted_iota(jnp.int32, (capacity, near_rows), 0)
    marks = [
        jnp.where(rows_cap + k * capacity == column, 1.0, 0.0).astype(jnp.bfloat16)
        for k in range(groups)
    ]
    for part in range(len(block_refs) // groups):
        blocks = block_refs[part * groups : (part + 1) * groups]
        share = blocks[0].shape[1]
        near = total = None
        for k in range(groups):
            term = dot(marks[k], blocks[k][near_rows:, :], 0, 0)
            near = term if near is None else near + term
            term = blocks[k][:near_rows, :].astype(jnp.float32)
            total = term if total is None else total + term
        li[:, part * share : (part + 1) * share] = near.astype(jnp.bfloat16)
        li[:, feat + part * share : feat + (part + 1) * share] = (total / fan_low).astype(jnp.bfloat16)

    wt[...] = jnp.zeros_like(wt)
    wt[:, :classes] = wt_ref[...].astype(jnp.bfloat16)

    factor = math.sqrt(2.0 / math.pi)
    step = 256
    for c in range(width // step):
        cols = slice(c * step, (c + 1) * step)
        v = dot(li[...], wl_ref[:, cols].astype(jnp.bfloat16))
        square = v * v
        t = jnp.tanh(factor * (v + 0.044715 * v * square))
        half = 0.5 * (1.0 + t)
        hidden[:, cols] = (v * half).astype(jnp.bfloat16)
        slope[:, cols] = half + 0.5 * v * (1.0 - t * t) * factor * (1.0 + 3.0 * 0.044715 * square)

    lane_near = lax.broadcasted_iota(jnp.int32, (seeds, near_rows), 1)
    counts = jnp.zeros((seeds, near_rows), jnp.float32)
    for j in range(fan_top):
        counts = counts + jnp.where(adj_ref[:, j : j + 1] == lane_near, 1.0, 0.0)
    counts = counts.astype(jnp.bfloat16)
    top_in[:, :width] = hidden[:seeds, :]
    top_in[:, width:] = (dot(counts, hidden[...]) / fan_top).astype(jnp.bfloat16)
    logits = dot(top_in[...], wt[...])
    logits_ref[...] = logits[:, :classes]
    lane_class = lax.broadcasted_iota(jnp.int32, (seeds, class_pad), 1)
    powers = jnp.where(lane_class < classes, jnp.exp(logits), 0.0)
    chances = powers / jnp.sum(powers, axis=1, keepdims=True)
    targets = jnp.where(lane_class == labels_ref[...], 1.0, 0.0)
    dlogits = ((chances - targets) * scale).astype(jnp.bfloat16)
    dinput = dot(dlogits, wt[...], 1, 1)
    spread = dinput[:, width:] / fan_top
    high = spread.astype(jnp.bfloat16)
    low = (spread - high.astype(jnp.float32)).astype(jnp.bfloat16)
    dhidden = dot(counts, high, 0, 0) + dot(counts, low, 0, 0)
    hidden[:seeds, :] = ((dhidden[:seeds] + dinput[:, :width]) * slope[:seeds, :]).astype(jnp.bfloat16)
    hidden[seeds:, :] = (dhidden[seeds:] * slope[seeds:, :]).astype(jnp.bfloat16)

    first = rep == 0
    members = low_width // rows_low
    stores = members // 2
    lane_groups = width // class_pad
    sub = rows_top // lane_groups

    def slot(store):
        plane, inner = store // PLANE, store % PLANE
        relative = plane - here
        relative = jnp.where(relative < 0, relative + groups, relative)
        return lax.bitwise_xor(mine, jnp.int32(inner)), relative

    tile = 384
    pair = 2 * rows_low
    for m in range(low_width // tile):
        grad = dot(li[:, m * tile : (m + 1) * tile], hidden[...], 0, 0)
        for s in range(tile // pair):
            even = grad[s * pair : s * pair + rows_low]
            odd = grad[s * pair + rows_low : (s + 1) * pair]
            a, b = slot(m * (tile // pair) + s)
            keep_ref[a, b, :rows_low, :] = jnp.where(first, even, odd)
            send_ref[a, b, :rows_low, :] = jnp.where(first, odd, even).astype(jnp.bfloat16)
    grad = dot(top_in[...], dlogits, 0, 0)
    for s in range(stores):
        even = grad[2 * s * rows_top : (2 * s + 1) * rows_top]
        odd = grad[(2 * s + 1) * rows_top : (2 * s + 2) * rows_top]
        own = jnp.where(first, even, odd)
        other = jnp.where(first, odd, even)
        a, b = slot(s)
        own = jnp.concatenate([own[g * sub : (g + 1) * sub] for g in range(lane_groups)], axis=1)
        other = jnp.concatenate([other[g * sub : (g + 1) * sub] for g in range(lane_groups)], axis=1)
        keep_ref[a, b, rows_low:, :] = own
        send_ref[a, b, rows_low:, :] = other.astype(jnp.bfloat16)


def trainer_step(place, labels, adj_top, column, wl, wt, blocks, sizes, scale):
    groups, rows_low, rows_top, classes, class_pad = sizes
    seeds = adj_top.shape[0]
    low_width, width = wl.shape
    near_rows = column.shape[1]
    rows = rows_low + rows_top * class_pad // width
    return pl.pallas_call(
        functools.partial(trainer_kernel, sizes, scale),
        out_shape=(
            jax.ShapeDtypeStruct((seeds, classes), jnp.float32),
            jax.ShapeDtypeStruct((PLANE, groups, rows, width), jnp.float32),
            jax.ShapeDtypeStruct((PLANE, groups, rows, width), jnp.bfloat16),
        ),
        in_specs=[SMEM] + [VMEM] * (5 + len(blocks)),
        out_specs=(VMEM, VMEM, VMEM),
        scratch_shapes=[
            pltpu.VMEM((near_rows, low_width), jnp.bfloat16),
            pltpu.VMEM((near_rows, width), jnp.bfloat16),
            pltpu.VMEM((near_rows, width), jnp.float32),
            pltpu.VMEM((seeds, 2 * width), jnp.bfloat16),
            pltpu.VMEM((2 * width, class_pad), jnp.bfloat16),
        ],
        compiler_params=pltpu.CompilerParams(vmem_limit_bytes=60 * MIB),
        name="trainer_step",
    )(place, labels, adj_top, column, wl, wt, *blocks)


def adam_part(gradient, moment, square):
    moment_new = beta_one * moment + (1.0 - beta_one) * gradient
    square_new = beta_two * square + (1.0 - beta_two) * gradient * gradient
    update = moment_new / bias_one / (jnp.sqrt(square_new / bias_two) + adam_eps)
    return learn_rate * update, moment_new, square_new


def adam_kernel(class_pad, parts, *refs):
    part_refs = refs[:parts]
    ml, sl, mt, st, nml, nsl, nmt, nst, delta = refs[parts:]
    rows_low, width = ml.shape
    rows_top, classes = mt.shape
    lane_groups = width // class_pad
    sub = rows_top // lane_groups
    total = part_refs[0][...]
    for ref in part_refs[1:]:
        total = total + ref[...].astype(jnp.float32)
    step, nml[...], nsl[...] = adam_part(total[:rows_low], ml[...], sl[...])
    top = total[rows_low:]
    pieces = []
    for g in range(lane_groups):
        rows = slice(g * sub, (g + 1) * sub)
        gradient = top[:, g * class_pad : g * class_pad + classes]
        piece, nmt[rows, :], nst[rows, :] = adam_part(gradient, mt[rows, :], st[rows, :])
        pieces.append(
            jnp.concatenate([piece, jnp.zeros((sub, class_pad - classes), jnp.float32)], axis=1)
        )
    whole = jnp.concatenate([step, jnp.concatenate(pieces, axis=1)], axis=0)
    delta[...] = whole.astype(jnp.bfloat16)


def adam_share(parts, ml, sl, mt, st, class_pad):
    rows, width = parts[0].shape
    shape = lambda a: jax.ShapeDtypeStruct(a.shape, jnp.float32)
    return pl.pallas_call(
        functools.partial(adam_kernel, class_pad, len(parts)),
        out_shape=(shape(ml), shape(sl), shape(mt), shape(st), jax.ShapeDtypeStruct((rows, width), jnp.bfloat16)),
        in_specs=[VMEM] * (len(parts) + 4),
        out_specs=(VMEM,) * 5,
        compiler_params=pltpu.CompilerParams(vmem_limit_bytes=32 * MIB),
        name="adam_share",
    )(*parts, ml, sl, mt, st)


def apply_kernel(sizes, place_ref, wl, wt, *refs):
    groups, rows_low, rows_top, classes, class_pad = sizes
    delta_refs, (nl, nt) = refs[: 2 * PLANE], refs[2 * PLANE :]
    here, mine, rep = place_ref[0], place_ref[1], place_ref[2]
    width = wl.shape[-1]
    lane_groups = width // class_pad
    sub = rows_top // lane_groups
    for d in range(PLANE):
        for half in range(2):
            for k in range(groups):
                plane = here + k
                plane = jnp.where(plane >= groups, plane - groups, plane)
                store = plane * PLANE + lax.bitwise_xor(mine, jnp.int32(d))
                core = rep if half == 0 else 1 - rep
                position = store * 2 + core
                delta = delta_refs[2 * d + half][k].astype(jnp.float32)
                if len(wl.shape) == 2:
                    rows = pl.ds(pl.multiple_of(position * rows_low, 8), rows_low)
                    nl[rows, :] = wl[rows, :] - delta[:rows_low]
                else:
                    nl[position] = wl[position] - delta[:rows_low]
                for g in range(lane_groups):
                    step = delta[rows_low:, g * class_pad : g * class_pad + classes]
                    if len(wt.shape) == 2:
                        rows = pl.ds(pl.multiple_of(position * rows_top + g * sub, 8), sub)
                        nt[rows, :] = wt[rows, :] - step
                    else:
                        rows = slice(g * sub, (g + 1) * sub)
                        nt[position, rows, :] = wt[position, rows, :] - step


def apply_updates(place, wl, wt, deltas, sizes):
    groups, rows_low, rows_top, classes, class_pad = sizes
    sub = rows_top * class_pad // wl.shape[1]
    low3 = wl if rows_low % 8 == 0 else wl.reshape(-1, rows_low, wl.shape[1])
    top3 = wt if sub % 8 == 0 else wt.reshape(-1, rows_top, wt.shape[1])
    nl, nt = pl.pallas_call(
        functools.partial(apply_kernel, sizes),
        out_shape=(
            jax.ShapeDtypeStruct(low3.shape, jnp.float32),
            jax.ShapeDtypeStruct(top3.shape, jnp.float32),
        ),
        in_specs=[SMEM] + [VMEM] * (2 + len(deltas)),
        out_specs=(VMEM, VMEM),
        compiler_params=pltpu.CompilerParams(vmem_limit_bytes=60 * MIB),
        name="apply_updates",
    )(place, low3, top3, *deltas)
    return nl.reshape(wl.shape), nt.reshape(wt.shape)


def per_device(
    features,
    owners_near,
    slots_near,
    owners_far,
    slots_far,
    adjacency_low,
    adjacency_top,
    labels,
    weights_low,
    weights_top,
    first_low,
    second_low,
    first_top,
    second_top,
):
    stores = lax.axis_size("store")
    groups = stores // PLANE
    members = stores * lax.axis_size("rep")
    index = lax.axis_index("store")
    here, mine, rep = index // PLANE, index % PLANE, lax.axis_index("rep")
    store_rows = features.shape[0]
    half = store_rows // 2
    near_rows, fan = adjacency_low.shape
    capacity = min(near_rows, PLANE * (2 * near_rows // stores))
    classes = weights_top.shape[1]
    class_pad = -(-classes // LANES) * LANES
    rows_low, rows_top = first_low.shape[0], first_top.shape[0]
    sizes = (groups, rows_low, rows_top, classes, class_pad)
    bf16 = jnp.bfloat16
    place = jnp.stack([here, mine, rep, jnp.int32(fan)]).astype(jnp.int32)

    def across(x, distance):
        return lax.ppermute(x, "store", [(i, i ^ distance) for i in range(stores)])

    def along(x, hops):
        return lax.ppermute(x, "store", [(i, (i + hops * PLANE) % stores) for i in range(stores)])

    def sibling(x):
        return lax.ppermute(x, "rep", [(0, 1), (1, 0)])

    gid_near = owners_near[:, 0] * store_rows + slots_near[:, 0]
    gid_far = owners_far[:, 0] * store_rows + slots_far[:, 0]
    table = jnp.concatenate([gid_near, gid_far]).reshape(-1, LANES)
    table = jnp.pad(table, ((0, -table.shape[0] % 16), (0, 0))).T
    ids, column = compose(
        place, adjacency_low, table, gid_near.reshape(1, near_rows), store_rows, groups, capacity
    )
    ids_all = [ids] + [along(ids, -k) for k in range(1, groups)]
    block = 16
    lists = row_lists(place, ids_all, store_rows, fan, capacity, block)

    share = features.shape[1] // 2
    quarter = half // 2
    places = [0, store_rows, store_rows + 3 * half]
    far = groups // 2
    calls = [[far], [k for k in range(1, groups) if k != far], [0]]
    blocks, pieces, waits = {}, (), ()
    first, second = (lists[0],), ()
    for part in range(2):
        columns, whole = (part * share, (part + 1) * share), (0, share)
        own = cut(place, features, 0, half, columns, pieces[1:], True)
        from_x, from_y = across(own, 1), across(own, 2)
        corner_a = across(cut(place, from_x, 0, quarter, whole, first), 2)
        corner_b = across(cut(place, from_y, quarter, quarter, whole, first), 1)
        brought = pack([from_x, from_y, corner_a, corner_b], second)
        pieces = (features, brought, sibling(brought))
        for turns in calls:
            made = partial_sums(
                [lists[k] for k in turns],
                pieces,
                places,
                columns,
                PLANE * store_rows,
                capacity,
                block,
                waits,
            )
            waits = (made,)
            for i, k in enumerate(turns):
                blocks[part, k] = along(made[i], k) if k else made[i]
            if turns == calls[0]:
                first, second = (made,), (blocks[part, far],)
            if turns == calls[1]:
                second += (made,)

    scale = 1.0 / (labels.shape[0] * members)
    logits, keep, send = trainer_step(
        place,
        labels[:, None],
        adjacency_top,
        column,
        weights_low,
        weights_top,
        [blocks[part, k] for part in range(2) for k in range(groups)],
        sizes,
        scale,
    )
    total = keep + sibling(send).astype(jnp.float32)
    arrived = [across(total[d].astype(bf16), d) for d in range(1, PLANE)]
    total = total[0] + sum(a.astype(jnp.float32) for a in arrived)
    shares = [total[0]] + [along(total[k].astype(bf16), k) for k in range(1, groups)]
    new_first_low, new_second_low, new_first_top, new_second_top, delta = adam_share(
        shares, first_low, second_low, first_top, second_top, class_pad
    )
    lined = jnp.stack([delta] + [along(delta, -k) for k in range(1, groups)])
    sheets = [lined] + [across(lined, d) for d in range(1, PLANE)]
    deltas = []
    for sheet in sheets:
        deltas += [sheet, sibling(sheet)]
    new_low, new_top = apply_updates(place, weights_low, weights_top, deltas, sizes)
    return (logits, new_low, new_first_low, new_second_low, new_top, new_first_top, new_second_top)


def solution(mesh):
    both = P(("store", "rep"), None)
    return jax.shard_map(
        per_device,
        mesh=mesh,
        in_specs=(P("store", None),)
        + (both,) * 6
        + (P(("store", "rep")), P(), P(), both, both, both, both),
        out_specs=(both, P(), both, both, P(), both, both),
        check_vma=False,
    )
```

```python
import functools
import math

import jax
import jax.numpy as jnp
from jax import lax
from jax.experimental import pallas as pl
from jax.experimental.pallas import tpu as pltpu
from jax.sharding import PartitionSpec as P

beta_one = 0.9
beta_two = 0.999
bias_one = 1.0 - 0.9**10
bias_two = 1.0 - 0.999**10
learn_rate = 0.01
adam_eps = 1e-08

PLANE = 4
LANES = 128
MIB = 1024 * 1024

VMEM = pl.BlockSpec(memory_space=pltpu.VMEM)
SMEM = pl.BlockSpec(memory_space=pltpu.SMEM)


def dot(a, b, ca=1, cb=0):
    return lax.dot_general(a, b, (((ca,), (cb,)), ((), ())), preferred_element_type=jnp.float32)


def compose_kernel(store_rows, groups, capacity, place_ref, adj_ref, table_ref, near_ref, ids_ref, column_ref):
    fan, near_rows = adj_ref.shape
    his = table_ref.shape[1]
    here = place_ref[0]
    table = table_ref[...]
    parts = jnp.concatenate([table // 65536, (table // 256) % 256, table % 256], axis=0)
    parts = parts.astype(jnp.float32).astype(jnp.bfloat16)
    row_hi = lax.broadcasted_iota(jnp.int32, (his, near_rows), 0)
    row_lo = lax.broadcasted_iota(jnp.int32, (LANES, near_rows), 0)
    for column in range(fan):
        position = adj_ref[column : column + 1, :]
        marks = jnp.where(row_hi == position // LANES, 1.0, 0.0).astype(jnp.bfloat16)
        found = dot(parts, marks)
        value = found[:LANES] * 65536.0 + found[LANES : 2 * LANES] * 256.0 + found[2 * LANES :]
        value = jnp.where(row_lo == position % LANES, value, 0.0)
        ids_ref[column : column + 1, :] = jnp.sum(value, axis=0, keepdims=True).astype(jnp.int32)
    near = near_ref[...]
    per_plane = PLANE * store_rows
    plane, row = near // per_plane, near % per_plane + 1
    row_plane = lax.broadcasted_iota(jnp.int32, (groups, near_rows), 0)
    marks = jnp.where(row_plane == plane, 1.0, 0.0)
    earlier = lax.broadcasted_iota(jnp.int32, (near_rows, near_rows), 0) < lax.broadcasted_iota(
        jnp.int32, (near_rows, near_rows), 1
    )
    counts = dot(marks.astype(jnp.bfloat16), jnp.where(earlier, 1.0, 0.0).astype(jnp.bfloat16))
    rank = jnp.sum(counts * marks, axis=0, keepdims=True).astype(jnp.int32)
    wanted = lax.broadcasted_iota(jnp.int32, (groups * capacity, near_rows), 0)
    marks = jnp.where(wanted == plane * capacity + rank, 1.0, 0.0).astype(jnp.bfloat16)
    line = lax.broadcasted_iota(jnp.int32, (8, near_rows), 0)
    halves = jnp.where(line == 0, row // 256, jnp.where(line == 1, row % 256, 0))
    found = dot(halves.astype(jnp.float32).astype(jnp.bfloat16), marks, 1, 1)
    found = (found[0:1] * 256.0 + found[1:2]).astype(jnp.int32)
    for line in range(groups * capacity // near_rows):
        ids_ref[fan + line : fan + line + 1, :] = found[:, line * near_rows : (line + 1) * near_rows]
    hops = here - plane
    hops = jnp.where(hops < 0, hops + groups, hops)
    column_ref[...] = hops * capacity + rank


def compose(place, adjacency, table, near, store_rows, groups, capacity):
    near_rows, fan = adjacency.shape
    rows = fan + groups * capacity // near_rows
    return pl.pallas_call(
        functools.partial(compose_kernel, store_rows, groups, capacity),
        out_shape=(
            jax.ShapeDtypeStruct((rows, near_rows), jnp.int32),
            jax.ShapeDtypeStruct((1, near_rows), jnp.int32),
        ),
        in_specs=[SMEM, VMEM, VMEM, VMEM],
        out_specs=(VMEM, VMEM),
        compiler_params=pltpu.CompilerParams(vmem_limit_bytes=32 * MIB),
        name="compose_ids",
    )(place, adjacency.T, table, near)


def sort_pairs(count):
    pairs = []
    size = 1
    while size < count:
        step = size
        while step >= 1:
            for start in range(step % size, count - step, 2 * step):
                for i in range(min(step, count - start - step)):
                    a, b = start + i, start + i + step
                    if a // (2 * size) == b // (2 * size):
                        pairs.append((a, b))
            step //= 2
        size *= 2
    return pairs


def depths_of(fan):
    return [d for d in (2, 3, 4, 5, 6, 8) if d < fan] + [fan]


def list_kernel(store_rows, fan, capacity, block, place_ref, *refs):
    groups = len(refs) // 2
    ids_refs, out_refs = refs[:groups], refs[groups:]
    here, mine, rep = place_ref[0], place_ref[1], place_ref[2]
    near_rows = ids_refs[0].shape[1]
    per_plane = PLANE * store_rows
    sub = lax.broadcasted_iota(jnp.int32, (near_rows, near_rows), 0)
    lane = lax.broadcasted_iota(jnp.int32, (near_rows, near_rows), 1)
    before = jnp.where(sub < lane, 1.0, 0.0).astype(jnp.bfloat16)
    nodes = lax.broadcasted_iota(jnp.int32, (1, near_rows), 1)
    classes = lax.broadcasted_iota(jnp.int32, (fan + 1, near_rows), 0)

    def turn(row):
        distance, slot = lax.bitwise_xor(row // store_rows, mine), row % store_rows
        turned = slot + rep * (store_rows // 2)
        turned = jnp.where(turned >= store_rows, turned - store_rows, turned)
        return distance * store_rows + jnp.where(distance == 0, slot, turned)

    for ids_ref, out_ref in zip(ids_refs, out_refs):
        gid = ids_ref[:fan, :]
        held = gid // per_plane == here
        row = jnp.where(held, turn(gid % per_plane), per_plane)
        count = jnp.sum(jnp.where(held, 1, 0), axis=0, keepdims=True)
        rows = [row[j : j + 1] for j in range(fan)]
        for a, b in sort_pairs(fan):
            rows[a], rows[b] = jnp.minimum(rows[a], rows[b]), jnp.maximum(rows[a], rows[b])
        marks = jnp.where(classes == count, 1.0, 0.0)
        rank = dot(marks.astype(jnp.bfloat16), before)
        sizes = jnp.sum(marks, axis=1, keepdims=True)
        larger = jnp.zeros((1, 1), jnp.float32)
        place = jnp.zeros((1, near_rows), jnp.float32)
        ends = {}
        for c in range(fan, -1, -1):
            ends[c] = larger
            place = place + marks[c : c + 1] * (rank[c : c + 1] + larger)
            larger = larger + sizes[c : c + 1]
        order = jnp.where(sub == place.astype(jnp.int32), 1.0, 0.0).astype(jnp.bfloat16)
        lines = jnp.concatenate(rows + [nodes], axis=0)
        parts = jnp.concatenate([lines // 256, lines % 256], axis=0)
        found = dot(parts.astype(jnp.float32).astype(jnp.bfloat16), order, 1, 1)
        found = (found[: fan + 1] * 256.0 + found[fan + 1 :]).astype(jnp.int32)
        out_ref[: fan + 1, :] = found * 8
        ahead = jnp.zeros((1, near_rows), jnp.int32)
        for i, d in enumerate(depths_of(fan)[:-1]):
            blocks = (ends[d].astype(jnp.int32) + (block - 1)) // block
            ahead = ahead + jnp.where(nodes == i, blocks, 0)
        out_ref[fan + 1 : fan + 2, :] = ahead
        lists = jnp.concatenate(
            [ids_ref[i : i + 1, :] for i in range(fan, ids_ref.shape[0])], axis=1
        )
        own = jnp.zeros((1, capacity), jnp.int32)
        for g in range(groups):
            own = own + jnp.where(here == g, lists[:, g * capacity : (g + 1) * capacity], 0)
        own = jnp.where(own == 0, per_plane, turn(own - 1))
        out_ref[fan + 2 : fan + 3, :capacity] = own * 8


def row_lists(place, ids_all, store_rows, fan, capacity, block):
    near_rows = ids_all[0].shape[1]
    groups = len(ids_all)
    return pl.pallas_call(
        functools.partial(list_kernel, store_rows, fan, capacity, block),
        out_shape=(jax.ShapeDtypeStruct((fan + 3, near_rows), jnp.int32),) * groups,
        in_specs=[SMEM] + [VMEM] * groups,
        out_specs=(VMEM,) * groups,
        compiler_params=pltpu.CompilerParams(vmem_limit_bytes=32 * MIB),
        name="row_lists",
    )(place, *ids_all)


def partial_kernel(count, places, capacity, block, *refs):
    index_refs, piece_refs = refs[:count], refs[count : count + len(places)]
    out_ref, table, sums, kept = refs[-5 - len(places) : -1 - len(places)]
    buffers = refs[-1 - len(places) : -1]
    arrived = refs[-1]
    fan, near_rows = index_refs[0].shape[0] - 3, index_refs[0].shape[1]
    units = buffers[0].shape[1] // LANES
    total = table.shape[0] // 8 - 1
    chunk = 256

    def row(at):
        return table[pl.ds(pl.multiple_of(at, 8), 8), :]

    def tree(rows):
        while len(rows) > 1:
            odd = rows[-1:] if len(rows) % 2 else []
            rows = [a + b for a, b in zip(rows[0::2], rows[1::2])] + odd
        return rows[0]

    copies = [
        pltpu.make_async_copy(source, buffer, arrived.at[i])
        for i, (source, buffer) in enumerate(zip(piece_refs, buffers))
    ]
    for copy in copies:
        copy.start()
    table[total * 8 :, :] = jnp.zeros((8, LANES), jnp.float32)
    for copy, buffer, start in zip(copies, buffers, places):
        copy.wait()

        def fill(i, carry):
            values = buffer[pl.ds(pl.multiple_of(i * chunk, chunk), chunk), :].astype(jnp.float32)
            base = (start + i * chunk) * 8
            for unit in range(units):
                table[pl.ds(base + unit, chunk, stride=8), :] = values[
                    :, unit * LANES : (unit + 1) * LANES
                ]
            return carry

        lax.fori_loop(0, buffer.shape[0] // chunk, fill, 0)

    near_unroll = 16
    for turn, index_ref in enumerate(index_refs):
        begin = 0
        depths = depths_of(fan)
        for at in range(len(depths) - 1, -1, -1):
            depth = depths[at]

            def step(i, carry):
                for u in range(block):
                    n = i * block + u
                    spot = pl.multiple_of(index_ref[fan, n], 8)
                    sums[pl.ds(spot, 8), :] = tree([row(index_ref[j, n]) for j in range(depth)])
                return carry

            end = index_ref[fan + 1, at - 1] if at else near_rows // block
            lax.fori_loop(begin, end, step, 0)
            begin = end

        def near(i, carry):
            for u in range(near_unroll):
                n = i * near_unroll + u
                kept[pl.ds(pl.multiple_of(n * 8, 8), 8), :] = row(index_ref[fan + 2, n])
            return carry

        lax.fori_loop(0, capacity // near_unroll, near, 0)
        for unit in range(units):
            lanes = slice(unit * LANES, (unit + 1) * LANES)
            out_ref[turn, :near_rows, lanes] = sums[
                pl.ds(unit, near_rows, stride=8), :
            ].astype(jnp.bfloat16)
            out_ref[turn, near_rows:, lanes] = kept[
                pl.ds(unit, capacity, stride=8), :
            ].astype(jnp.bfloat16)


def partial_sums(lists, pieces, places, total, capacity, block):
    near_rows = lists[0].shape[1]
    width = pieces[0].shape[1]
    return pl.pallas_call(
        functools.partial(partial_kernel, len(lists), places, capacity, block),
        out_shape=jax.ShapeDtypeStruct((len(lists), near_rows + capacity, width), jnp.bfloat16),
        in_specs=[SMEM] * len(lists) + [pl.BlockSpec(memory_space=pl.ANY)] * len(pieces),
        out_specs=VMEM,
        scratch_shapes=[
            pltpu.VMEM(((total + 1) * 8, LANES), jnp.float32),
            pltpu.VMEM(((near_rows + 1) * 8, LANES), jnp.float32),
            pltpu.VMEM(((capacity + 1) * 8, LANES), jnp.float32),
        ]
        + [pltpu.VMEM(piece.shape, piece.dtype) for piece in pieces]
        + [pltpu.SemaphoreType.DMA((len(pieces),))],
        compiler_params=pltpu.CompilerParams(vmem_limit_bytes=60 * MIB),
        name="partial_sums",
    )(*lists, *pieces)


def trainer_kernel(sizes, scale, *refs):
    groups, rows_low, rows_top, classes, class_pad = sizes
    place_ref, labels_ref, adj_ref, column_ref, wl_ref, wt_ref = refs[:6]
    block_refs = refs[6:-10]
    logits_ref, keep_ref, send_ref, li, hidden, slope, top_in, wt, weights, arrived = refs[-10:]
    seeds, fan_top = adj_ref.shape
    near_rows, low_width = li.shape
    feat = low_width // 2
    width = hidden.shape[1]
    capacity = block_refs[0].shape[0] - near_rows
    here, mine, rep = place_ref[0], place_ref[1], place_ref[2]
    fan_low = place_ref[3].astype(jnp.float32)

    bring = pltpu.make_async_copy(wl_ref, weights, arrived)
    bring.start()
    column = column_ref[...]
    rows_cap = lax.broadcasted_iota(jnp.int32, (capacity, near_rows), 0)
    marks = [
        jnp.where(rows_cap + k * capacity == column, 1.0, 0.0).astype(jnp.bfloat16)
        for k in range(groups)
    ]
    for part in range(len(block_refs) // groups):
        blocks = block_refs[part * groups : (part + 1) * groups]
        share = blocks[0].shape[1]
        near = total = None
        for k in range(groups):
            term = dot(marks[k], blocks[k][near_rows:, :], 0, 0)
            near = term if near is None else near + term
            term = blocks[k][:near_rows, :].astype(jnp.float32)
            total = term if total is None else total + term
        li[:, part * share : (part + 1) * share] = near.astype(jnp.bfloat16)
        li[:, feat + part * share : feat + (part + 1) * share] = (total / fan_low).astype(jnp.bfloat16)

    wt[...] = jnp.zeros_like(wt)
    wt[:, :classes] = wt_ref[...].astype(jnp.bfloat16)

    bring.wait()
    factor = math.sqrt(2.0 / math.pi)
    step = 256
    for c in range(width // step):
        cols = slice(c * step, (c + 1) * step)
        v = dot(li[...], weights[:, cols].astype(jnp.bfloat16))
        square = v * v
        t = jnp.tanh(factor * (v + 0.044715 * v * square))
        half = 0.5 * (1.0 + t)
        hidden[:, cols] = (v * half).astype(jnp.bfloat16)
        slope[:, cols] = half + 0.5 * v * (1.0 - t * t) * factor * (1.0 + 3.0 * 0.044715 * square)

    lane_near = lax.broadcasted_iota(jnp.int32, (seeds, near_rows), 1)
    counts = jnp.zeros((seeds, near_rows), jnp.float32)
    for j in range(fan_top):
        counts = counts + jnp.where(adj_ref[:, j : j + 1] == lane_near, 1.0, 0.0)
    counts = counts.astype(jnp.bfloat16)
    top_in[:, :width] = hidden[:seeds, :]
    top_in[:, width:] = (dot(counts, hidden[...]) / fan_top).astype(jnp.bfloat16)
    logits = dot(top_in[...], wt[...])
    logits_ref[...] = logits[:, :classes]
    lane_class = lax.broadcasted_iota(jnp.int32, (seeds, class_pad), 1)
    powers = jnp.where(lane_class < classes, jnp.exp(logits), 0.0)
    chances = powers / jnp.sum(powers, axis=1, keepdims=True)
    targets = jnp.where(lane_class == labels_ref[...], 1.0, 0.0)
    dlogits = ((chances - targets) * scale).astype(jnp.bfloat16)
    dinput = dot(dlogits, wt[...], 1, 1)
    spread = dinput[:, width:] / fan_top
    high = spread.astype(jnp.bfloat16)
    low = (spread - high.astype(jnp.float32)).astype(jnp.bfloat16)
    dhidden = dot(counts, high, 0, 0) + dot(counts, low, 0, 0)
    hidden[:seeds, :] = ((dhidden[:seeds] + dinput[:, :width]) * slope[:seeds, :]).astype(jnp.bfloat16)
    hidden[seeds:, :] = (dhidden[seeds:] * slope[seeds:, :]).astype(jnp.bfloat16)

    first = rep == 0
    members = low_width // rows_low
    stores = members // 2
    lane_groups = width // class_pad
    sub = rows_top // lane_groups

    def slot(store):
        plane, inner = store // PLANE, store % PLANE
        relative = plane - here
        relative = jnp.where(relative < 0, relative + groups, relative)
        return lax.bitwise_xor(mine, jnp.int32(inner)), relative

    tile = 384
    pair = 2 * rows_low
    for m in range(low_width // tile):
        grad = dot(li[:, m * tile : (m + 1) * tile], hidden[...], 0, 0)
        for s in range(tile // pair):
            even = grad[s * pair : s * pair + rows_low]
            odd = grad[s * pair + rows_low : (s + 1) * pair]
            a, b = slot(m * (tile // pair) + s)
            keep_ref[a, b, :rows_low, :] = jnp.where(first, even, odd)
            send_ref[a, b, :rows_low, :] = jnp.where(first, odd, even).astype(jnp.bfloat16)
    grad = dot(top_in[...], dlogits, 0, 0)
    for s in range(stores):
        even = grad[2 * s * rows_top : (2 * s + 1) * rows_top]
        odd = grad[(2 * s + 1) * rows_top : (2 * s + 2) * rows_top]
        own = jnp.where(first, even, odd)
        other = jnp.where(first, odd, even)
        a, b = slot(s)
        own = jnp.concatenate([own[g * sub : (g + 1) * sub] for g in range(lane_groups)], axis=1)
        other = jnp.concatenate([other[g * sub : (g + 1) * sub] for g in range(lane_groups)], axis=1)
        keep_ref[a, b, rows_low:, :] = own
        send_ref[a, b, rows_low:, :] = other.astype(jnp.bfloat16)


def trainer_step(place, labels, adj_top, column, wl, wt, blocks, sizes, scale):
    groups, rows_low, rows_top, classes, class_pad = sizes
    seeds = adj_top.shape[0]
    low_width, width = wl.shape
    near_rows = column.shape[1]
    rows = rows_low + rows_top * class_pad // width
    return pl.pallas_call(
        functools.partial(trainer_kernel, sizes, scale),
        out_shape=(
            jax.ShapeDtypeStruct((seeds, classes), jnp.float32),
            jax.ShapeDtypeStruct((PLANE, groups, rows, width), jnp.float32),
            jax.ShapeDtypeStruct((PLANE, groups, rows, width), jnp.bfloat16),
        ),
        in_specs=[SMEM] + [VMEM] * 3 + [pl.BlockSpec(memory_space=pl.ANY)] + [VMEM] * (1 + len(blocks)),
        out_specs=(VMEM, VMEM, VMEM),
        scratch_shapes=[
            pltpu.VMEM((near_rows, low_width), jnp.bfloat16),
            pltpu.VMEM((near_rows, width), jnp.bfloat16),
            pltpu.VMEM((near_rows, width), jnp.float32),
            pltpu.VMEM((seeds, 2 * width), jnp.bfloat16),
            pltpu.VMEM((2 * width, class_pad), jnp.bfloat16),
            pltpu.VMEM((low_width, width), jnp.float32),
            pltpu.SemaphoreType.DMA,
        ],
        compiler_params=pltpu.CompilerParams(vmem_limit_bytes=60 * MIB),
        name="trainer_step",
    )(place, labels, adj_top, column, wl, wt, *blocks)


def adam_part(gradient, moment, square):
    moment_new = beta_one * moment + (1.0 - beta_one) * gradient
    square_new = beta_two * square + (1.0 - beta_two) * gradient * gradient
    update = moment_new / bias_one / (jnp.sqrt(square_new / bias_two) + adam_eps)
    return learn_rate * update, moment_new, square_new


def adam_kernel(class_pad, parts, *refs):
    part_refs = refs[:parts]
    ml, sl, mt, st, nml, nsl, nmt, nst, delta = refs[parts:]
    rows_low, width = ml.shape
    rows_top, classes = mt.shape
    lane_groups = width // class_pad
    sub = rows_top // lane_groups
    total = part_refs[0][...]
    for ref in part_refs[1:]:
        total = total + ref[...].astype(jnp.float32)
    step, nml[...], nsl[...] = adam_part(total[:rows_low], ml[...], sl[...])
    top = total[rows_low:]
    pieces = []
    for g in range(lane_groups):
        rows = slice(g * sub, (g + 1) * sub)
        gradient = top[:, g * class_pad : g * class_pad + classes]
        piece, nmt[rows, :], nst[rows, :] = adam_part(gradient, mt[rows, :], st[rows, :])
        pieces.append(
            jnp.concatenate([piece, jnp.zeros((sub, class_pad - classes), jnp.float32)], axis=1)
        )
    whole = jnp.concatenate([step, jnp.concatenate(pieces, axis=1)], axis=0)
    delta[...] = whole.astype(jnp.bfloat16)


def adam_share(parts, ml, sl, mt, st, class_pad):
    rows, width = parts[0].shape
    shape = lambda a: jax.ShapeDtypeStruct(a.shape, jnp.float32)
    return pl.pallas_call(
        functools.partial(adam_kernel, class_pad, len(parts)),
        out_shape=(shape(ml), shape(sl), shape(mt), shape(st), jax.ShapeDtypeStruct((rows, width), jnp.bfloat16)),
        in_specs=[VMEM] * (len(parts) + 4),
        out_specs=(VMEM,) * 5,
        compiler_params=pltpu.CompilerParams(vmem_limit_bytes=32 * MIB),
        name="adam_share",
    )(*parts, ml, sl, mt, st)


def apply_kernel(sizes, place_ref, wl, wt, *refs):
    groups, rows_low, rows_top, classes, class_pad = sizes
    delta_refs, (nl, nt) = refs[: 2 * PLANE], refs[2 * PLANE :]
    here = place_ref[0]
    lane_groups = wl.shape[-1] // class_pad
    sub = rows_top // lane_groups
    for turn, delta_ref in enumerate(delta_refs):

        @pl.when(pl.program_id(0) == turn)
        def _():
            for k in range(groups):
                plane = here + k
                plane = jnp.where(plane >= groups, plane - groups, plane)
                delta = delta_ref[k].astype(jnp.float32)
                nl[plane, 0, 0] = wl[plane, 0, 0] - delta[:rows_low]
                for g in range(lane_groups):
                    rows = slice(g * sub, (g + 1) * sub)
                    step = delta[rows_low:, g * class_pad : g * class_pad + classes]
                    nt[plane, 0, 0, rows, :] = wt[plane, 0, 0, rows, :] - step


def apply_updates(place, wl, wt, deltas, sizes):
    groups, rows_low, rows_top, classes, class_pad = sizes
    low = wl.reshape(groups, PLANE, 2, rows_low, wl.shape[1])
    top = wt.reshape(groups, PLANE, 2, rows_top, wt.shape[1])

    def spot(turn, place_ref):
        core = jnp.where(turn % 2 == 0, place_ref[2], 1 - place_ref[2])
        return (0, lax.bitwise_xor(place_ref[1], turn // 2), core, 0, 0)

    specs = [pl.BlockSpec((groups, 1, 1) + a.shape[3:], spot) for a in (low, top)]
    nl, nt = pl.pallas_call(
        functools.partial(apply_kernel, sizes),
        grid_spec=pltpu.PrefetchScalarGridSpec(
            num_scalar_prefetch=1,
            grid=(2 * PLANE,),
            in_specs=specs + [VMEM] * len(deltas),
            out_specs=specs,
        ),
        out_shape=[jax.ShapeDtypeStruct(a.shape, jnp.float32) for a in (low, top)],
        compiler_params=pltpu.CompilerParams(vmem_limit_bytes=32 * MIB),
        name="apply_updates",
    )(place, low, top, *deltas)
    return nl.reshape(wl.shape), nt.reshape(wt.shape)


def per_device(
    features,
    owners_near,
    slots_near,
    owners_far,
    slots_far,
    adjacency_low,
    adjacency_top,
    labels,
    weights_low,
    weights_top,
    first_low,
    second_low,
    first_top,
    second_top,
):
    stores = lax.axis_size("store")
    groups = stores // PLANE
    members = stores * lax.axis_size("rep")
    index = lax.axis_index("store")
    here, mine, rep = index // PLANE, index % PLANE, lax.axis_index("rep")
    store_rows = features.shape[0]
    half = store_rows // 2
    near_rows, fan = adjacency_low.shape
    capacity = min(near_rows, PLANE * (2 * near_rows // stores))
    classes = weights_top.shape[1]
    class_pad = -(-classes // LANES) * LANES
    rows_low, rows_top = first_low.shape[0], first_top.shape[0]
    sizes = (groups, rows_low, rows_top, classes, class_pad)
    bf16 = jnp.bfloat16
    place = jnp.stack([here, mine, rep, jnp.int32(fan)]).astype(jnp.int32)

    def across(x, distance):
        return lax.ppermute(x, "store", [(i, i ^ distance) for i in range(stores)])

    def along(x, hops):
        return lax.ppermute(x, "store", [(i, (i + hops * PLANE) % stores) for i in range(stores)])

    def sibling(x):
        return lax.ppermute(x, "rep", [(0, 1), (1, 0)])

    quarter = half // 2
    own = lax.dynamic_slice_in_dim(features, rep * half, half, 0)
    from_x, from_y = across(own, 1), across(own, 2)

    gid_near = owners_near[:, 0] * store_rows + slots_near[:, 0]
    gid_far = owners_far[:, 0] * store_rows + slots_far[:, 0]
    table = jnp.concatenate([gid_near, gid_far]).reshape(-1, LANES)
    table = jnp.pad(table, ((0, -table.shape[0] % 16), (0, 0))).T
    ids, column = compose(
        place, adjacency_low, table, gid_near.reshape(1, near_rows), store_rows, groups, capacity
    )
    ids_all = [ids] + [along(ids, -k) for k in range(1, groups)]
    block = 16
    lists = row_lists(place, ids_all, store_rows, fan, capacity, block)

    from_x, from_y, lists = lax.optimization_barrier((from_x, from_y, lists))
    corner_a, corner_b = across(from_x[:quarter], 2), across(from_y[quarter:], 1)
    pieces = [features, from_x, sibling(from_x), from_y, sibling(from_y)]
    pieces += [corner_a, corner_b, sibling(corner_a), sibling(corner_b)]
    places = [0, store_rows, store_rows + half, 2 * store_rows, 2 * store_rows + half]
    places += [3 * store_rows + quarter * i for i in range(4)]

    blocks = []
    for k in range(groups):
        made = partial_sums([lists[k]], pieces, places, PLANE * store_rows, capacity, block)
        blocks.append(along(made[0], k) if k else made[0])

    scale = 1.0 / (labels.shape[0] * members)
    logits, keep, send = trainer_step(
        place,
        labels[:, None],
        adjacency_top,
        column,
        weights_low,
        weights_top,
        blocks,
        sizes,
        scale,
    )
    total = keep + sibling(send).astype(jnp.float32)
    arrived = [across(total[d].astype(bf16), d) for d in range(1, PLANE)]
    total = total[0] + sum(a.astype(jnp.float32) for a in arrived)
    shares = [total[0]] + [along(total[k].astype(bf16), k) for k in range(1, groups)]
    new_first_low, new_second_low, new_first_top, new_second_top, delta = adam_share(
        shares, first_low, second_low, first_top, second_top, class_pad
    )
    lined = jnp.stack([delta] + [along(delta, -k) for k in range(1, groups)])
    sheets = [lined] + [across(lined, d) for d in range(1, PLANE)]
    deltas = []
    for sheet in sheets:
        deltas += [sheet, sibling(sheet)]
    new_low, new_top = apply_updates(place, weights_low, weights_top, deltas, sizes)
    return (logits, new_low, new_first_low, new_second_low, new_top, new_first_top, new_second_top)


def solution(mesh):
    both = P(("store", "rep"), None)
    return jax.shard_map(
        per_device,
        mesh=mesh,
        in_specs=(P("store", None),)
        + (both,) * 6
        + (P(("store", "rep")), P(), P(), both, both, both, both),
        out_specs=(both, P(), both, both, P(), both, both),
        check_vma=False,
    )
```

```python
import functools
import math

import jax
import jax.numpy as jnp
from jax import lax
from jax.experimental import pallas as pl
from jax.experimental.pallas import tpu as pltpu
from jax.sharding import PartitionSpec as P

beta_one = 0.9
beta_two = 0.999
bias_one = 1.0 - 0.9**10
bias_two = 1.0 - 0.999**10
learn_rate = 0.01
adam_eps = 1e-08

PLANE = 4
LANES = 128
MIB = 1024 * 1024

VMEM = pl.BlockSpec(memory_space=pltpu.VMEM)
SMEM = pl.BlockSpec(memory_space=pltpu.SMEM)


def dot(a, b, ca=1, cb=0):
    return lax.dot_general(a, b, (((ca,), (cb,)), ((), ())), preferred_element_type=jnp.float32)


def compose_kernel(store_rows, groups, capacity, place_ref, adj_ref, table_ref, near_ref, ids_ref, column_ref):
    fan, near_rows = adj_ref.shape
    his = table_ref.shape[1]
    here = place_ref[0]
    table = table_ref[...]
    parts = jnp.concatenate([table // 65536, (table // 256) % 256, table % 256], axis=0)
    parts = parts.astype(jnp.float32).astype(jnp.bfloat16)
    row_hi = lax.broadcasted_iota(jnp.int32, (his, near_rows), 0)
    row_lo = lax.broadcasted_iota(jnp.int32, (LANES, near_rows), 0)
    for column in range(fan):
        position = adj_ref[column : column + 1, :]
        marks = jnp.where(row_hi == position // LANES, 1.0, 0.0).astype(jnp.bfloat16)
        found = dot(parts, marks)
        value = found[:LANES] * 65536.0 + found[LANES : 2 * LANES] * 256.0 + found[2 * LANES :]
        value = jnp.where(row_lo == position % LANES, value, 0.0)
        ids_ref[column : column + 1, :] = jnp.sum(value, axis=0, keepdims=True).astype(jnp.int32)
    near = near_ref[...]
    per_plane = PLANE * store_rows
    plane, row = near // per_plane, near % per_plane + 1
    row_plane = lax.broadcasted_iota(jnp.int32, (groups, near_rows), 0)
    marks = jnp.where(row_plane == plane, 1.0, 0.0)
    earlier = lax.broadcasted_iota(jnp.int32, (near_rows, near_rows), 0) < lax.broadcasted_iota(
        jnp.int32, (near_rows, near_rows), 1
    )
    counts = dot(marks.astype(jnp.bfloat16), jnp.where(earlier, 1.0, 0.0).astype(jnp.bfloat16))
    rank = jnp.sum(counts * marks, axis=0, keepdims=True).astype(jnp.int32)
    wanted = lax.broadcasted_iota(jnp.int32, (groups * capacity, near_rows), 0)
    marks = jnp.where(wanted == plane * capacity + rank, 1.0, 0.0).astype(jnp.bfloat16)
    line = lax.broadcasted_iota(jnp.int32, (8, near_rows), 0)
    halves = jnp.where(line == 0, row // 256, jnp.where(line == 1, row % 256, 0))
    found = dot(halves.astype(jnp.float32).astype(jnp.bfloat16), marks, 1, 1)
    found = (found[0:1] * 256.0 + found[1:2]).astype(jnp.int32)
    for line in range(groups * capacity // near_rows):
        ids_ref[fan + line : fan + line + 1, :] = found[:, line * near_rows : (line + 1) * near_rows]
    column_ref[...] = lax.bitwise_xor(plane, here) * capacity + rank


def compose(place, adjacency, table, near, store_rows, groups, capacity):
    near_rows, fan = adjacency.shape
    rows = fan + groups * capacity // near_rows
    return pl.pallas_call(
        functools.partial(compose_kernel, store_rows, groups, capacity),
        out_shape=(
            jax.ShapeDtypeStruct((rows, near_rows), jnp.int32),
            jax.ShapeDtypeStruct((1, near_rows), jnp.int32),
        ),
        in_specs=[SMEM, VMEM, VMEM, VMEM],
        out_specs=(VMEM, VMEM),
        compiler_params=pltpu.CompilerParams(vmem_limit_bytes=32 * MIB),
        name="compose_ids",
    )(place, adjacency.T, table, near)


def sort_pairs(count):
    pairs = []
    size = 1
    while size < count:
        step = size
        while step >= 1:
            for start in range(step % size, count - step, 2 * step):
                for i in range(min(step, count - start - step)):
                    a, b = start + i, start + i + step
                    if a // (2 * size) == b // (2 * size):
                        pairs.append((a, b))
            step //= 2
        size *= 2
    return pairs


def depths_of(fan):
    return [d for d in (2, 3, 4, 5, 6, 8) if d < fan] + [fan]


def list_kernel(store_rows, fan, capacity, block, place_ref, *refs):
    groups = len(refs) // 2
    ids_refs, out_refs = refs[:groups], refs[groups:]
    here, mine, rep = place_ref[0], place_ref[1], place_ref[2]
    near_rows = ids_refs[0].shape[1]
    per_plane = PLANE * store_rows
    sub = lax.broadcasted_iota(jnp.int32, (near_rows, near_rows), 0)
    lane = lax.broadcasted_iota(jnp.int32, (near_rows, near_rows), 1)
    before = jnp.where(sub < lane, 1.0, 0.0).astype(jnp.bfloat16)
    nodes = lax.broadcasted_iota(jnp.int32, (1, near_rows), 1)
    classes = lax.broadcasted_iota(jnp.int32, (fan + 1, near_rows), 0)

    def turn(row):
        distance, slot = lax.bitwise_xor(row // store_rows, mine), row % store_rows
        turned = slot + rep * (store_rows // 2)
        turned = jnp.where(turned >= store_rows, turned - store_rows, turned)
        return distance * store_rows + jnp.where(distance == 0, slot, turned)

    for ids_ref, out_ref in zip(ids_refs, out_refs):
        gid = ids_ref[:fan, :]
        held = gid // per_plane == here
        row = jnp.where(held, turn(gid % per_plane), per_plane)
        count = jnp.sum(jnp.where(held, 1, 0), axis=0, keepdims=True)
        rows = [row[j : j + 1] for j in range(fan)]
        for a, b in sort_pairs(fan):
            rows[a], rows[b] = jnp.minimum(rows[a], rows[b]), jnp.maximum(rows[a], rows[b])
        marks = jnp.where(classes == count, 1.0, 0.0)
        rank = dot(marks.astype(jnp.bfloat16), before)
        sizes = jnp.sum(marks, axis=1, keepdims=True)
        larger = jnp.zeros((1, 1), jnp.float32)
        place = jnp.zeros((1, near_rows), jnp.float32)
        ends = {}
        for c in range(fan, -1, -1):
            ends[c] = larger
            place = place + marks[c : c + 1] * (rank[c : c + 1] + larger)
            larger = larger + sizes[c : c + 1]
        order = jnp.where(sub == place.astype(jnp.int32), 1.0, 0.0).astype(jnp.bfloat16)
        lines = jnp.concatenate(rows + [nodes], axis=0)
        parts = jnp.concatenate([lines // 256, lines % 256], axis=0)
        found = dot(parts.astype(jnp.float32).astype(jnp.bfloat16), order, 1, 1)
        found = (found[: fan + 1] * 256.0 + found[fan + 1 :]).astype(jnp.int32)
        out_ref[: fan + 1, :] = found * 8
        ahead = jnp.zeros((1, near_rows), jnp.int32)
        for i, d in enumerate(depths_of(fan)[:-1]):
            blocks = (ends[d].astype(jnp.int32) + (block - 1)) // block
            ahead = ahead + jnp.where(nodes == i, blocks, 0)
        out_ref[fan + 1 : fan + 2, :] = ahead
        lists = jnp.concatenate(
            [ids_ref[i : i + 1, :] for i in range(fan, ids_ref.shape[0])], axis=1
        )
        own = jnp.zeros((1, capacity), jnp.int32)
        for g in range(groups):
            own = own + jnp.where(here == g, lists[:, g * capacity : (g + 1) * capacity], 0)
        own = jnp.where(own == 0, per_plane, turn(own - 1))
        out_ref[fan + 2 : fan + 3, :capacity] = own * 8


def row_lists(place, ids_all, store_rows, fan, capacity, block):
    near_rows = ids_all[0].shape[1]
    groups = len(ids_all)
    return pl.pallas_call(
        functools.partial(list_kernel, store_rows, fan, capacity, block),
        out_shape=(jax.ShapeDtypeStruct((fan + 3, near_rows), jnp.int32),) * groups,
        in_specs=[SMEM] + [VMEM] * groups,
        out_specs=(VMEM,) * groups,
        compiler_params=pltpu.CompilerParams(vmem_limit_bytes=32 * MIB),
        name="row_lists",
    )(place, *ids_all)


def partial_kernel(count, joined, places, capacity, block, *refs):
    index_refs, piece_refs = refs[:count], refs[count : count + len(places)]
    sums_ref, near_ref = refs[count + len(places)], refs[-5 - len(places)]
    near_start = sums_ref.shape[1] - capacity if joined else 0
    table, sums, kept = refs[-4 - len(places) : -1 - len(places)]
    buffers = refs[-1 - len(places) : -1]
    arrived = refs[-1]
    fan, near_rows = index_refs[0].shape[0] - 3, index_refs[0].shape[1]
    units = buffers[0].shape[1] // LANES
    total = table.shape[0] // 8 - 1
    chunk = 256

    def row(at):
        return table[pl.ds(pl.multiple_of(at, 8), 8), :]

    def tree(rows):
        while len(rows) > 1:
            odd = rows[-1:] if len(rows) % 2 else []
            rows = [a + b for a, b in zip(rows[0::2], rows[1::2])] + odd
        return rows[0]

    copies = [
        pltpu.make_async_copy(source, buffer, arrived.at[i])
        for i, (source, buffer) in enumerate(zip(piece_refs, buffers))
    ]
    for copy in copies:
        copy.start()
    table[total * 8 :, :] = jnp.zeros((8, LANES), jnp.float32)
    for copy, buffer, start in zip(copies, buffers, places):
        copy.wait()

        def fill(i, carry):
            values = buffer[pl.ds(pl.multiple_of(i * chunk, chunk), chunk), :].astype(jnp.float32)
            base = (start + i * chunk) * 8
            for unit in range(units):
                table[pl.ds(base + unit, chunk, stride=8), :] = values[
                    :, unit * LANES : (unit + 1) * LANES
                ]
            return carry

        lax.fori_loop(0, buffer.shape[0] // chunk, fill, 0)

    near_unroll = 16
    for turn, index_ref in enumerate(index_refs):
        begin = 0
        depths = depths_of(fan)
        for at in range(len(depths) - 1, -1, -1):
            depth = depths[at]

            def step(i, carry):
                for u in range(block):
                    n = i * block + u
                    spot = pl.multiple_of(index_ref[fan, n], 8)
                    sums[pl.ds(spot, 8), :] = tree([row(index_ref[j, n]) for j in range(depth)])
                return carry

            end = index_ref[fan + 1, at - 1] if at else near_rows // block
            lax.fori_loop(begin, end, step, 0)
            begin = end

        def near(i, carry):
            for u in range(near_unroll):
                n = i * near_unroll + u
                kept[pl.ds(pl.multiple_of(n * 8, 8), 8), :] = row(index_ref[fan + 2, n])
            return carry

        lax.fori_loop(0, capacity // near_unroll, near, 0)
        for unit in range(units):
            lanes = slice(unit * LANES, (unit + 1) * LANES)
            sums_ref[turn, :near_rows, lanes] = sums[
                pl.ds(unit, near_rows, stride=8), :
            ].astype(jnp.bfloat16)
            near_ref[turn, near_start : near_start + capacity, lanes] = kept[
                pl.ds(unit, capacity, stride=8), :
            ].astype(jnp.bfloat16)


def partial_sums(lists, pieces, places, total, capacity, block, joined):
    near_rows = lists[0].shape[1]
    width = pieces[0].shape[1]
    heights = [near_rows + capacity] if joined else [near_rows, capacity]
    return pl.pallas_call(
        functools.partial(partial_kernel, len(lists), joined, places, capacity, block),
        out_shape=[jax.ShapeDtypeStruct((len(lists), n, width), jnp.bfloat16) for n in heights],
        in_specs=[SMEM] * len(lists) + [pl.BlockSpec(memory_space=pl.ANY)] * len(pieces),
        out_specs=[VMEM] * len(heights),
        scratch_shapes=[
            pltpu.VMEM(((total + 1) * 8, LANES), jnp.float32),
            pltpu.VMEM(((near_rows + 1) * 8, LANES), jnp.float32),
            pltpu.VMEM(((capacity + 1) * 8, LANES), jnp.float32),
        ]
        + [pltpu.VMEM(piece.shape, piece.dtype) for piece in pieces]
        + [pltpu.SemaphoreType.DMA((len(pieces),))],
        compiler_params=pltpu.CompilerParams(vmem_limit_bytes=60 * MIB),
        name="partial_sums",
    )(*lists, *pieces)


def trainer_kernel(sizes, scale, joined, *refs):
    groups, rows_low, rows_top, classes, class_pad = sizes
    rest = groups - joined
    place_ref, labels_ref, adj_ref, column_ref, wl_ref, wt_ref = refs[:6]
    block_refs, sum_refs, near_refs = refs[6 : 6 + joined], refs[6 + joined : -10 - rest], refs[-10 - rest : -10]
    logits_ref, keep_ref, send_ref, li, hidden, slope, top_in, wt, weights, arrived = refs[-10:]
    seeds, fan_top = adj_ref.shape
    near_rows, low_width = li.shape
    feat = low_width // 2
    width = hidden.shape[1]
    capacity = block_refs[0].shape[0] - near_rows
    here, mine, rep = place_ref[0], place_ref[1], place_ref[2]
    fan_low = place_ref[3].astype(jnp.float32)

    bring = pltpu.make_async_copy(wl_ref, weights, arrived)
    bring.start()
    column = column_ref[...]
    rows_cap = lax.broadcasted_iota(jnp.int32, (capacity, near_rows), 0)
    near = total = None
    for k in range(groups):
        marks = jnp.where(rows_cap + k * capacity == column, 1.0, 0.0).astype(jnp.bfloat16)
        rows = block_refs[k][near_rows:, :] if k < joined else near_refs[k - joined][...]
        term = dot(marks, rows, 0, 0)
        near = term if near is None else near + term
    for ref in block_refs + sum_refs:
        term = ref[:near_rows, :].astype(jnp.float32)
        total = term if total is None else total + term
    li[:, :feat] = near.astype(jnp.bfloat16)
    li[:, feat:] = (total / fan_low).astype(jnp.bfloat16)

    wt[...] = jnp.zeros_like(wt)
    wt[:, :classes] = wt_ref[...].astype(jnp.bfloat16)

    bring.wait()
    factor = math.sqrt(2.0 / math.pi)
    step = 256
    for c in range(width // step):
        cols = slice(c * step, (c + 1) * step)
        v = dot(li[...], weights[:, cols].astype(jnp.bfloat16))
        square = v * v
        t = jnp.tanh(factor * (v + 0.044715 * v * square))
        half = 0.5 * (1.0 + t)
        hidden[:, cols] = (v * half).astype(jnp.bfloat16)
        slope[:, cols] = half + 0.5 * v * (1.0 - t * t) * factor * (1.0 + 3.0 * 0.044715 * square)

    lane_near = lax.broadcasted_iota(jnp.int32, (seeds, near_rows), 1)
    counts = jnp.zeros((seeds, near_rows), jnp.float32)
    for j in range(fan_top):
        counts = counts + jnp.where(adj_ref[:, j : j + 1] == lane_near, 1.0, 0.0)
    counts = counts.astype(jnp.bfloat16)
    top_in[:, :width] = hidden[:seeds, :]
    top_in[:, width:] = (dot(counts, hidden[...]) / fan_top).astype(jnp.bfloat16)
    logits = dot(top_in[...], wt[...])
    logits_ref[...] = logits[:, :classes]
    lane_class = lax.broadcasted_iota(jnp.int32, (seeds, class_pad), 1)
    powers = jnp.where(lane_class < classes, jnp.exp(logits), 0.0)
    chances = powers / jnp.sum(powers, axis=1, keepdims=True)
    targets = jnp.where(lane_class == labels_ref[...], 1.0, 0.0)
    dlogits = ((chances - targets) * scale).astype(jnp.bfloat16)
    dinput = dot(dlogits, wt[...], 1, 1)
    spread = dinput[:, width:] / fan_top
    high = spread.astype(jnp.bfloat16)
    low = (spread - high.astype(jnp.float32)).astype(jnp.bfloat16)
    dhidden = dot(counts, high, 0, 0) + dot(counts, low, 0, 0)
    hidden[:seeds, :] = ((dhidden[:seeds] + dinput[:, :width]) * slope[:seeds, :]).astype(jnp.bfloat16)
    hidden[seeds:, :] = (dhidden[seeds:] * slope[seeds:, :]).astype(jnp.bfloat16)

    first = rep == 0
    members = low_width // rows_low
    stores = members // 2
    lane_groups = width // class_pad
    sub = rows_top // lane_groups

    def slot(store):
        plane, inner = store // PLANE, store % PLANE
        return lax.bitwise_xor(mine, jnp.int32(inner)), lax.bitwise_xor(here, jnp.int32(plane))

    tile = 384
    pair = 2 * rows_low
    for m in range(low_width // tile):
        grad = dot(li[:, m * tile : (m + 1) * tile], hidden[...], 0, 0)
        for s in range(tile // pair):
            even = grad[s * pair : s * pair + rows_low]
            odd = grad[s * pair + rows_low : (s + 1) * pair]
            a, b = slot(m * (tile // pair) + s)
            keep_ref[a, b, :rows_low, :] = jnp.where(first, even, odd)
            send_ref[a, b, :rows_low, :] = jnp.where(first, odd, even).astype(jnp.bfloat16)
    grad = dot(top_in[...], dlogits, 0, 0)
    for s in range(stores):
        even = grad[2 * s * rows_top : (2 * s + 1) * rows_top]
        odd = grad[(2 * s + 1) * rows_top : (2 * s + 2) * rows_top]
        own = jnp.where(first, even, odd)
        other = jnp.where(first, odd, even)
        a, b = slot(s)
        own = jnp.concatenate([own[g * sub : (g + 1) * sub] for g in range(lane_groups)], axis=1)
        other = jnp.concatenate([other[g * sub : (g + 1) * sub] for g in range(lane_groups)], axis=1)
        keep_ref[a, b, rows_low:, :] = own
        send_ref[a, b, rows_low:, :] = other.astype(jnp.bfloat16)


def trainer_step(place, labels, adj_top, column, wl, wt, joined, blocks, sizes, scale):
    groups, rows_low, rows_top, classes, class_pad = sizes
    seeds = adj_top.shape[0]
    low_width, width = wl.shape
    near_rows = column.shape[1]
    rows = rows_low + rows_top * class_pad // width
    return pl.pallas_call(
        functools.partial(trainer_kernel, sizes, scale, joined),
        out_shape=(
            jax.ShapeDtypeStruct((seeds, classes), jnp.float32),
            jax.ShapeDtypeStruct((PLANE, groups, rows, width), jnp.float32),
            jax.ShapeDtypeStruct((PLANE, groups, rows, width), jnp.bfloat16),
        ),
        in_specs=[SMEM] + [VMEM] * 3 + [pl.BlockSpec(memory_space=pl.ANY)] + [VMEM] * (1 + len(blocks)),
        out_specs=(VMEM, VMEM, VMEM),
        scratch_shapes=[
            pltpu.VMEM((near_rows, low_width), jnp.bfloat16),
            pltpu.VMEM((near_rows, width), jnp.bfloat16),
            pltpu.VMEM((near_rows, width), jnp.float32),
            pltpu.VMEM((seeds, 2 * width), jnp.bfloat16),
            pltpu.VMEM((2 * width, class_pad), jnp.bfloat16),
            pltpu.VMEM((low_width, width), jnp.float32),
            pltpu.SemaphoreType.DMA,
        ],
        compiler_params=pltpu.CompilerParams(vmem_limit_bytes=60 * MIB),
        name="trainer_step",
    )(place, labels, adj_top, column, wl, wt, *blocks)


def adam_part(gradient, moment, square):
    moment_new = beta_one * moment + (1.0 - beta_one) * gradient
    square_new = beta_two * square + (1.0 - beta_two) * gradient * gradient
    update = moment_new / bias_one / (jnp.sqrt(square_new / bias_two) + adam_eps)
    return learn_rate * update, moment_new, square_new


def adam_kernel(class_pad, parts, *refs):
    part_refs = refs[:parts]
    ml, sl, mt, st, nml, nsl, nmt, nst, delta = refs[parts:]
    rows_low, width = ml.shape
    rows_top, classes = mt.shape
    lane_groups = width // class_pad
    sub = rows_top // lane_groups
    total = part_refs[0][...]
    for ref in part_refs[1:]:
        total = total + ref[...].astype(jnp.float32)
    step, nml[...], nsl[...] = adam_part(total[:rows_low], ml[...], sl[...])
    top = total[rows_low:]
    pieces = []
    for g in range(lane_groups):
        rows = slice(g * sub, (g + 1) * sub)
        gradient = top[:, g * class_pad : g * class_pad + classes]
        piece, nmt[rows, :], nst[rows, :] = adam_part(gradient, mt[rows, :], st[rows, :])
        pieces.append(
            jnp.concatenate([piece, jnp.zeros((sub, class_pad - classes), jnp.float32)], axis=1)
        )
    whole = jnp.concatenate([step, jnp.concatenate(pieces, axis=1)], axis=0)
    delta[...] = whole.astype(jnp.bfloat16)


def adam_share(parts, ml, sl, mt, st, class_pad):
    rows, width = parts[0].shape
    shape = lambda a: jax.ShapeDtypeStruct(a.shape, jnp.float32)
    return pl.pallas_call(
        functools.partial(adam_kernel, class_pad, len(parts)),
        out_shape=(shape(ml), shape(sl), shape(mt), shape(st), jax.ShapeDtypeStruct((rows, width), jnp.bfloat16)),
        in_specs=[VMEM] * (len(parts) + 4),
        out_specs=(VMEM,) * 5,
        compiler_params=pltpu.CompilerParams(vmem_limit_bytes=32 * MIB),
        name="adam_share",
    )(*parts, ml, sl, mt, st)


def apply_kernel(sizes, place_ref, wl, wt, *refs):
    groups, rows_low, rows_top, classes, class_pad = sizes
    delta_refs, (nl, nt) = refs[: 2 * PLANE], refs[2 * PLANE :]
    here = place_ref[0]
    lane_groups = wl.shape[-1] // class_pad
    sub = rows_top // lane_groups
    for turn, delta_ref in enumerate(delta_refs):

        @pl.when(pl.program_id(0) == turn)
        def _():
            for k in range(groups):
                plane = lax.bitwise_xor(here, jnp.int32(k))
                delta = delta_ref[k].astype(jnp.float32)
                nl[plane, 0, 0] = wl[plane, 0, 0] - delta[:rows_low]
                for g in range(lane_groups):
                    rows = slice(g * sub, (g + 1) * sub)
                    step = delta[rows_low:, g * class_pad : g * class_pad + classes]
                    nt[plane, 0, 0, rows, :] = wt[plane, 0, 0, rows, :] - step


def apply_updates(place, wl, wt, deltas, sizes):
    groups, rows_low, rows_top, classes, class_pad = sizes
    low = wl.reshape(groups, PLANE, 2, rows_low, wl.shape[1])
    top = wt.reshape(groups, PLANE, 2, rows_top, wt.shape[1])

    def spot(turn, place_ref):
        core = jnp.where(turn % 2 == 0, place_ref[2], 1 - place_ref[2])
        return (0, lax.bitwise_xor(place_ref[1], turn // 2), core, 0, 0)

    specs = [pl.BlockSpec((groups, 1, 1) + a.shape[3:], spot) for a in (low, top)]
    nl, nt = pl.pallas_call(
        functools.partial(apply_kernel, sizes),
        grid_spec=pltpu.PrefetchScalarGridSpec(
            num_scalar_prefetch=1,
            grid=(2 * PLANE,),
            in_specs=specs + [VMEM] * len(deltas),
            out_specs=specs,
        ),
        out_shape=[jax.ShapeDtypeStruct(a.shape, jnp.float32) for a in (low, top)],
        compiler_params=pltpu.CompilerParams(vmem_limit_bytes=32 * MIB),
        name="apply_updates",
    )(place, low, top, *deltas)
    return nl.reshape(wl.shape), nt.reshape(wt.shape)


def per_device(
    features,
    owners_near,
    slots_near,
    owners_far,
    slots_far,
    adjacency_low,
    adjacency_top,
    labels,
    weights_low,
    weights_top,
    first_low,
    second_low,
    first_top,
    second_top,
):
    stores = lax.axis_size("store")
    groups = stores // PLANE
    members = stores * lax.axis_size("rep")
    index = lax.axis_index("store")
    here, mine, rep = index // PLANE, index % PLANE, lax.axis_index("rep")
    store_rows = features.shape[0]
    half = store_rows // 2
    near_rows, fan = adjacency_low.shape
    capacity = min(near_rows, PLANE * (2 * near_rows // stores))
    classes = weights_top.shape[1]
    class_pad = -(-classes // LANES) * LANES
    rows_low, rows_top = first_low.shape[0], first_top.shape[0]
    sizes = (groups, rows_low, rows_top, classes, class_pad)
    bf16 = jnp.bfloat16
    place = jnp.stack([here, mine, rep, jnp.int32(fan)]).astype(jnp.int32)

    def across(x, distance):
        return lax.ppermute(x, "store", [(i, i ^ distance) for i in range(stores)])

    def along(x, distance):
        return across(x, distance * PLANE)

    def between(x, moves):
        pairs = [(a * PLANE + i, b * PLANE + i) for a, b in moves for i in range(PLANE)]
        return lax.ppermute(x, "store", pairs)

    def sibling(x):
        return lax.ppermute(x, "rep", [(0, 1), (1, 0)])

    quarter = half // 2
    own = lax.dynamic_slice_in_dim(features, rep * half, half, 0)
    from_x, from_y = across(own, 1), across(own, 2)

    gid_near = owners_near[:, 0] * store_rows + slots_near[:, 0]
    gid_far = owners_far[:, 0] * store_rows + slots_far[:, 0]
    table = jnp.concatenate([gid_near, gid_far]).reshape(-1, LANES)
    table = jnp.pad(table, ((0, -table.shape[0] % 16), (0, 0))).T
    ids, column = compose(
        place, adjacency_low, table, gid_near.reshape(1, near_rows), store_rows, groups, capacity
    )
    ids_all = [ids] + [along(ids, k) for k in range(1, groups)]
    block = 16
    lists = row_lists(place, ids_all, store_rows, fan, capacity, block)

    from_x, from_y, lists = lax.optimization_barrier((from_x, from_y, lists))
    corner_a, corner_b = across(from_x[:quarter], 2), across(from_y[quarter:], 1)
    pieces = [features, from_x, sibling(from_x), from_y, sibling(from_y)]
    pieces += [corner_a, corner_b, sibling(corner_a), sibling(corner_b)]
    places = [0, store_rows, store_rows + half, 2 * store_rows, 2 * store_rows + half]
    places += [3 * store_rows + quarter * i for i in range(4)]

    def summed(turns, joined=True):
        return partial_sums(
            [lists[k] for k in turns], pieces, places, PLANE * store_rows, capacity, block, joined
        )

    if groups == 4:
        sums_far, near_far = summed([3, 2], False)
        handed = between(sums_far, [(0, 1), (3, 2)])
        (beside,), (own_block,) = summed([1]), summed([0])
        near_far = [along(near_far[1], 2), along(near_far[0], 3)]
        handed, near_far, beside = lax.optimization_barrier((handed, near_far, beside))
        handed = handed.astype(jnp.float32)
        for_two = (sums_far[1].astype(jnp.float32) + handed[0]).astype(bf16)
        for_three = (sums_far[0].astype(jnp.float32) + handed[1]).astype(bf16)
        sums_far = [between(for_two, [(1, 3), (2, 0)]), between(for_three, [(1, 2), (2, 1)])]
        joined, blocks = 2, [own_block[0], along(beside[0], 1)] + sums_far + near_far
    else:
        joined, blocks = groups, []
        for k in range(groups):
            (made,) = summed([k])
            blocks.append(along(made[0], k) if k else made[0])

    scale = 1.0 / (labels.shape[0] * members)
    logits, keep, send = trainer_step(
        place,
        labels[:, None],
        adjacency_top,
        column,
        weights_low,
        weights_top,
        joined,
        blocks,
        sizes,
        scale,
    )
    total = keep + sibling(send).astype(jnp.float32)
    arrived = [across(total[d].astype(bf16), d) for d in range(1, PLANE)]
    total = total[0] + sum(a.astype(jnp.float32) for a in arrived)
    shares = [total[0]] + [along(total[k].astype(bf16), k) for k in range(1, groups)]
    new_first_low, new_second_low, new_first_top, new_second_top, delta = adam_share(
        shares, first_low, second_low, first_top, second_top, class_pad
    )
    lined = jnp.stack([delta] + [along(delta, k) for k in range(1, groups)])
    sheets = [lined] + [across(lined, d) for d in range(1, PLANE)]
    deltas = []
    for sheet in sheets:
        deltas += [sheet, sibling(sheet)]
    new_low, new_top = apply_updates(place, weights_low, weights_top, deltas, sizes)
    return (logits, new_low, new_first_low, new_second_low, new_top, new_first_top, new_second_top)


def solution(mesh):
    both = P(("store", "rep"), None)
    return jax.shard_map(
        per_device,
        mesh=mesh,
        in_specs=(P("store", None),)
        + (both,) * 6
        + (P(("store", "rep")), P(), P(), both, both, both, both),
        out_specs=(both, P(), both, both, P(), both, both),
        check_vma=False,
    )
```

```python
import functools
import math

import jax
import jax.numpy as jnp
from jax import lax
from jax.experimental import pallas as pl
from jax.experimental.pallas import tpu as pltpu
from jax.sharding import PartitionSpec as P

beta_one = 0.9
beta_two = 0.999
bias_one = 1.0 - 0.9**10
bias_two = 1.0 - 0.999**10
learn_rate = 0.01
adam_eps = 1e-08

PLANE = 4
LANES = 128
MIB = 1024 * 1024

VMEM = pl.BlockSpec(memory_space=pltpu.VMEM)
SMEM = pl.BlockSpec(memory_space=pltpu.SMEM)


def dot(a, b, ca=1, cb=0):
    return lax.dot_general(a, b, (((ca,), (cb,)), ((), ())), preferred_element_type=jnp.float32)


def compose_kernel(adj_ref, table_ref, ids_ref):
    fan, near_rows = adj_ref.shape
    his = table_ref.shape[1]
    table = table_ref[...]
    parts = jnp.concatenate([table // 65536, (table // 256) % 256, table % 256], axis=0)
    parts = parts.astype(jnp.float32).astype(jnp.bfloat16)
    row_hi = lax.broadcasted_iota(jnp.int32, (his, near_rows), 0)
    row_lo = lax.broadcasted_iota(jnp.int32, (LANES, near_rows), 0)
    for column in range(fan):
        position = adj_ref[column : column + 1, :]
        marks = jnp.where(row_hi == position // LANES, 1.0, 0.0).astype(jnp.bfloat16)
        found = dot(parts, marks)
        value = found[:LANES] * 65536.0 + found[LANES : 2 * LANES] * 256.0 + found[2 * LANES :]
        value = jnp.where(row_lo == position % LANES, value, 0.0)
        ids_ref[column : column + 1, :] = jnp.sum(value, axis=0, keepdims=True).astype(jnp.int32)


def compose(adjacency, table):
    near_rows, fan = adjacency.shape
    return pl.pallas_call(
        compose_kernel,
        out_shape=jax.ShapeDtypeStruct((fan, near_rows), jnp.int32),
        in_specs=[VMEM, VMEM],
        out_specs=VMEM,
        compiler_params=pltpu.CompilerParams(vmem_limit_bytes=32 * MIB),
        name="compose_ids",
    )(adjacency.T, table)


def request_kernel(store_rows, stores, capacity, place_ref, near_ref, request_ref, column_ref):
    groups = stores // PLANE
    near_rows = near_ref.shape[1]
    here, mine = place_ref[0], place_ref[1]
    near = near_ref[...]
    owner, slot = near // store_rows, near % store_rows
    row_owner = lax.broadcasted_iota(jnp.int32, (stores, near_rows), 0)
    marks = jnp.where(row_owner == owner, 1.0, 0.0)
    earlier = lax.broadcasted_iota(jnp.int32, (near_rows, near_rows), 0) < lax.broadcasted_iota(
        jnp.int32, (near_rows, near_rows), 1
    )
    counts = dot(marks.astype(jnp.bfloat16), jnp.where(earlier, 1.0, 0.0).astype(jnp.bfloat16))
    rank = jnp.sum(counts * marks, axis=0, keepdims=True).astype(jnp.int32)
    wanted = lax.broadcasted_iota(jnp.int32, (stores * capacity, near_rows), 0)
    marks = jnp.where(wanted == owner * capacity + rank, 1.0, 0.0).astype(jnp.bfloat16)
    line = lax.broadcasted_iota(jnp.int32, (8, near_rows), 0)
    halves = jnp.where(line == 0, slot // 256, jnp.where(line == 1, slot % 256, 0))
    found = dot(halves.astype(jnp.float32).astype(jnp.bfloat16), marks, 1, 1)
    request_ref[...] = (found[0:1] * 256.0 + found[1:2]).astype(jnp.int32)
    hops = here - owner // PLANE
    hops = jnp.where(hops < 0, hops + groups, hops)
    distance = lax.bitwise_xor(owner % PLANE, mine)
    column_ref[...] = (distance * groups + hops) * capacity + rank


def request_near(place, near, store_rows, stores, capacity):
    return pl.pallas_call(
        functools.partial(request_kernel, store_rows, stores, capacity),
        out_shape=(
            jax.ShapeDtypeStruct((1, stores * capacity), jnp.int32),
            jax.ShapeDtypeStruct(near.shape, jnp.int32),
        ),
        in_specs=[SMEM, VMEM],
        out_specs=(VMEM, VMEM),
        compiler_params=pltpu.CompilerParams(vmem_limit_bytes=32 * MIB),
        name="request_near",
    )(place, near)


def near_kernel(groups, place_ref, request_ref, features_ref, out_ref):
    here, mine = place_ref[0], place_ref[1]
    store_rows = features_ref.shape[0]
    capacity = request_ref.shape[1]
    slots = lax.broadcasted_iota(jnp.int32, (store_rows, PLANE * capacity), 0)
    for k in range(groups):
        plane = here + k
        plane = jnp.where(plane >= groups, plane - groups, plane)
        lines = []
        for d in range(PLANE):
            trainer = plane * PLANE + lax.bitwise_xor(mine, jnp.int32(d))
            lines.append(request_ref[pl.ds(trainer, 1), :])
        marks = jnp.where(slots == jnp.concatenate(lines, axis=1), 1.0, 0.0).astype(jnp.bfloat16)
        out_ref[k] = dot(marks, features_ref[...], 0, 0).astype(jnp.bfloat16)


def near_rows_held(place, requests, features, groups):
    capacity = requests.shape[1]
    return pl.pallas_call(
        functools.partial(near_kernel, groups),
        out_shape=jax.ShapeDtypeStruct((groups, PLANE * capacity, features.shape[1]), jnp.bfloat16),
        in_specs=[SMEM, VMEM, VMEM],
        out_specs=VMEM,
        compiler_params=pltpu.CompilerParams(vmem_limit_bytes=32 * MIB),
        name="near_rows",
    )(place, requests, features)


def sort_pairs(count):
    pairs = []
    size = 1
    while size < count:
        step = size
        while step >= 1:
            for start in range(step % size, count - step, 2 * step):
                for i in range(min(step, count - start - step)):
                    a, b = start + i, start + i + step
                    if a // (2 * size) == b // (2 * size):
                        pairs.append((a, b))
            step //= 2
        size *= 2
    return pairs


def depths_of(fan):
    return [d for d in (2, 3, 4, 5, 6, 8) if d < fan] + [fan]


def list_kernel(store_rows, block, place_ref, *refs):
    groups = len(refs) // 2
    ids_refs, out_refs = refs[:groups], refs[groups:]
    here, mine, rep = place_ref[0], place_ref[1], place_ref[2]
    fan, near_rows = ids_refs[0].shape
    per_plane = PLANE * store_rows
    sub = lax.broadcasted_iota(jnp.int32, (near_rows, near_rows), 0)
    lane = lax.broadcasted_iota(jnp.int32, (near_rows, near_rows), 1)
    before = jnp.where(sub < lane, 1.0, 0.0).astype(jnp.bfloat16)
    nodes = lax.broadcasted_iota(jnp.int32, (1, near_rows), 1)
    classes = lax.broadcasted_iota(jnp.int32, (fan + 1, near_rows), 0)

    def turn(row):
        distance, slot = lax.bitwise_xor(row // store_rows, mine), row % store_rows
        turned = slot + rep * (store_rows // 2)
        turned = jnp.where(turned >= store_rows, turned - store_rows, turned)
        return distance * store_rows + jnp.where(distance == 0, slot, turned)

    for ids_ref, out_ref in zip(ids_refs, out_refs):
        gid = ids_ref[...]
        held = gid // per_plane == here
        row = jnp.where(held, turn(gid % per_plane), per_plane)
        count = jnp.sum(jnp.where(held, 1, 0), axis=0, keepdims=True)
        rows = [row[j : j + 1] for j in range(fan)]
        for a, b in sort_pairs(fan):
            rows[a], rows[b] = jnp.minimum(rows[a], rows[b]), jnp.maximum(rows[a], rows[b])
        marks = jnp.where(classes == count, 1.0, 0.0)
        rank = dot(marks.astype(jnp.bfloat16), before)
        sizes = jnp.sum(marks, axis=1, keepdims=True)
        larger = jnp.zeros((1, 1), jnp.float32)
        place = jnp.zeros((1, near_rows), jnp.float32)
        ends = {}
        for c in range(fan, -1, -1):
            ends[c] = larger
            place = place + marks[c : c + 1] * (rank[c : c + 1] + larger)
            larger = larger + sizes[c : c + 1]
        order = jnp.where(sub == place.astype(jnp.int32), 1.0, 0.0).astype(jnp.bfloat16)
        lines = jnp.concatenate(rows + [nodes], axis=0)
        parts = jnp.concatenate([lines // 256, lines % 256], axis=0)
        found = dot(parts.astype(jnp.float32).astype(jnp.bfloat16), order, 1, 1)
        found = (found[: fan + 1] * 256.0 + found[fan + 1 :]).astype(jnp.int32)
        out_ref[: fan + 1, :] = found * 8
        ahead = jnp.zeros((1, near_rows), jnp.int32)
        for i, d in enumerate(depths_of(fan)[:-1]):
            blocks = (ends[d].astype(jnp.int32) + (block - 1)) // block
            ahead = ahead + jnp.where(nodes == i, blocks, 0)
        out_ref[fan + 1 : fan + 2, :] = ahead


def row_lists(place, ids_all, store_rows, block):
    fan, near_rows = ids_all[0].shape
    groups = len(ids_all)
    return pl.pallas_call(
        functools.partial(list_kernel, store_rows, block),
        out_shape=(jax.ShapeDtypeStruct((fan + 2, near_rows), jnp.int32),) * groups,
        in_specs=[SMEM] + [VMEM] * groups,
        out_specs=(VMEM,) * groups,
        compiler_params=pltpu.CompilerParams(vmem_limit_bytes=32 * MIB),
        name="row_lists",
    )(place, *ids_all)


def partial_kernel(count, places, block, *refs):
    index_refs, piece_refs = refs[:count], refs[count : count + len(places)]
    out_ref, table, sums = refs[-4 - len(places) : -1 - len(places)]
    buffers = refs[-1 - len(places) : -1]
    arrived = refs[-1]
    fan, near_rows = index_refs[0].shape[0] - 2, index_refs[0].shape[1]
    units = buffers[0].shape[1] // LANES
    total = table.shape[0] // 8 - 1
    chunk = 256

    def row(at):
        return table[pl.ds(pl.multiple_of(at, 8), 8), :]

    def tree(rows):
        while len(rows) > 1:
            odd = rows[-1:] if len(rows) % 2 else []
            rows = [a + b for a, b in zip(rows[0::2], rows[1::2])] + odd
        return rows[0]

    copies = [
        pltpu.make_async_copy(source, buffer, arrived.at[i])
        for i, (source, buffer) in enumerate(zip(piece_refs, buffers))
    ]
    for copy in copies:
        copy.start()
    table[total * 8 :, :] = jnp.zeros((8, LANES), jnp.float32)
    for copy, buffer, start in zip(copies, buffers, places):
        copy.wait()

        def fill(i, carry):
            values = buffer[pl.ds(pl.multiple_of(i * chunk, chunk), chunk), :].astype(jnp.float32)
            base = (start + i * chunk) * 8
            for unit in range(units):
                table[pl.ds(base + unit, chunk, stride=8), :] = values[
                    :, unit * LANES : (unit + 1) * LANES
                ]
            return carry

        lax.fori_loop(0, buffer.shape[0] // chunk, fill, 0)

    for turn, index_ref in enumerate(index_refs):
        begin = 0
        depths = depths_of(fan)
        for at in range(len(depths) - 1, -1, -1):
            depth = depths[at]

            def step(i, carry):
                for u in range(block):
                    n = i * block + u
                    spot = pl.multiple_of(index_ref[fan, n], 8)
                    sums[pl.ds(spot, 8), :] = tree([row(index_ref[j, n]) for j in range(depth)])
                return carry

            end = index_ref[fan + 1, at - 1] if at else near_rows // block
            lax.fori_loop(begin, end, step, 0)
            begin = end

        for unit in range(units):
            lanes = slice(unit * LANES, (unit + 1) * LANES)
            out_ref[turn, :near_rows, lanes] = sums[
                pl.ds(unit, near_rows, stride=8), :
            ].astype(jnp.bfloat16)


def partial_sums(lists, pieces, places, total, block):
    near_rows = lists[0].shape[1]
    width = pieces[0].shape[1]
    return pl.pallas_call(
        functools.partial(partial_kernel, len(lists), places, block),
        out_shape=jax.ShapeDtypeStruct((len(lists), near_rows, width), jnp.bfloat16),
        in_specs=[SMEM] * len(lists) + [pl.BlockSpec(memory_space=pl.ANY)] * len(pieces),
        out_specs=VMEM,
        scratch_shapes=[
            pltpu.VMEM(((total + 1) * 8, LANES), jnp.float32),
            pltpu.VMEM(((near_rows + 1) * 8, LANES), jnp.float32),
        ]
        + [pltpu.VMEM(piece.shape, piece.dtype) for piece in pieces]
        + [pltpu.SemaphoreType.DMA((len(pieces),))],
        compiler_params=pltpu.CompilerParams(vmem_limit_bytes=60 * MIB),
        name="partial_sums",
    )(*lists, *pieces)


def trainer_kernel(sizes, scale, *refs):
    groups, rows_low, rows_top, classes, class_pad = sizes
    place_ref, labels_ref, adj_ref, column_ref, wl_ref, wt_ref = refs[:6]
    block_refs, near_refs = refs[6 : 6 + groups], refs[6 + groups : -10]
    logits_ref, keep_ref, send_ref, li, hidden, slope, top_in, wt, weights, arrived = refs[-10:]
    seeds, fan_top = adj_ref.shape
    near_rows, low_width = li.shape
    feat = low_width // 2
    width = hidden.shape[1]
    capacity = near_refs[0].shape[0]
    here, mine, rep = place_ref[0], place_ref[1], place_ref[2]
    fan_low = place_ref[3].astype(jnp.float32)

    bring = pltpu.make_async_copy(wl_ref, weights, arrived)
    bring.start()
    column = column_ref[...]
    rows_cap = lax.broadcasted_iota(jnp.int32, (capacity, near_rows), 0)
    near = None
    for d in range(PLANE):
        marks = jnp.where(rows_cap + d * capacity == column, 1.0, 0.0).astype(jnp.bfloat16)
        term = dot(marks, near_refs[d][...], 0, 0)
        near = term if near is None else near + term
    total = block_refs[0][...].astype(jnp.float32)
    for k in range(1, groups):
        total = total + block_refs[k][...].astype(jnp.float32)
    li[:, :feat] = near.astype(jnp.bfloat16)
    li[:, feat:] = (total / fan_low).astype(jnp.bfloat16)

    wt[...] = jnp.zeros_like(wt)
    wt[:, :classes] = wt_ref[...].astype(jnp.bfloat16)

    bring.wait()
    factor = math.sqrt(2.0 / math.pi)
    step = 256
    for c in range(width // step):
        cols = slice(c * step, (c + 1) * step)
        v = dot(li[...], weights[:, cols].astype(jnp.bfloat16))
        square = v * v
        t = jnp.tanh(factor * (v + 0.044715 * v * square))
        half = 0.5 * (1.0 + t)
        hidden[:, cols] = (v * half).astype(jnp.bfloat16)
        slope[:, cols] = half + 0.5 * v * (1.0 - t * t) * factor * (1.0 + 3.0 * 0.044715 * square)

    lane_near = lax.broadcasted_iota(jnp.int32, (seeds, near_rows), 1)
    counts = jnp.zeros((seeds, near_rows), jnp.float32)
    for j in range(fan_top):
        counts = counts + jnp.where(adj_ref[:, j : j + 1] == lane_near, 1.0, 0.0)
    counts = counts.astype(jnp.bfloat16)
    top_in[:, :width] = hidden[:seeds, :]
    top_in[:, width:] = (dot(counts, hidden[...]) / fan_top).astype(jnp.bfloat16)
    logits = dot(top_in[...], wt[...])
    logits_ref[...] = logits[:, :classes]
    lane_class = lax.broadcasted_iota(jnp.int32, (seeds, class_pad), 1)
    powers = jnp.where(lane_class < classes, jnp.exp(logits), 0.0)
    chances = powers / jnp.sum(powers, axis=1, keepdims=True)
    targets = jnp.where(lane_class == labels_ref[...], 1.0, 0.0)
    dlogits = ((chances - targets) * scale).astype(jnp.bfloat16)
    dinput = dot(dlogits, wt[...], 1, 1)
    spread = dinput[:, width:] / fan_top
    high = spread.astype(jnp.bfloat16)
    low = (spread - high.astype(jnp.float32)).astype(jnp.bfloat16)
    dhidden = dot(counts, high, 0, 0) + dot(counts, low, 0, 0)
    hidden[:seeds, :] = ((dhidden[:seeds] + dinput[:, :width]) * slope[:seeds, :]).astype(jnp.bfloat16)
    hidden[seeds:, :] = (dhidden[seeds:] * slope[seeds:, :]).astype(jnp.bfloat16)

    first = rep == 0
    members = low_width // rows_low
    stores = members // 2
    lane_groups = width // class_pad
    sub = rows_top // lane_groups

    def slot(store):
        plane, inner = store // PLANE, store % PLANE
        relative = plane - here
        relative = jnp.where(relative < 0, relative + groups, relative)
        return lax.bitwise_xor(mine, jnp.int32(inner)), relative

    tile = 384
    pair = 2 * rows_low
    for m in range(low_width // tile):
        grad = dot(li[:, m * tile : (m + 1) * tile], hidden[...], 0, 0)
        for s in range(tile // pair):
            even = grad[s * pair : s * pair + rows_low]
            odd = grad[s * pair + rows_low : (s + 1) * pair]
            a, b = slot(m * (tile // pair) + s)
            keep_ref[a, b, :rows_low, :] = jnp.where(first, even, odd)
            send_ref[a, b, :rows_low, :] = jnp.where(first, odd, even).astype(jnp.bfloat16)
    grad = dot(top_in[...], dlogits, 0, 0)
    for s in range(stores):
        even = grad[2 * s * rows_top : (2 * s + 1) * rows_top]
        odd = grad[(2 * s + 1) * rows_top : (2 * s + 2) * rows_top]
        own = jnp.where(first, even, odd)
        other = jnp.where(first, odd, even)
        a, b = slot(s)
        own = jnp.concatenate([own[g * sub : (g + 1) * sub] for g in range(lane_groups)], axis=1)
        other = jnp.concatenate([other[g * sub : (g + 1) * sub] for g in range(lane_groups)], axis=1)
        keep_ref[a, b, rows_low:, :] = own
        send_ref[a, b, rows_low:, :] = other.astype(jnp.bfloat16)


def trainer_step(place, labels, adj_top, column, wl, wt, blocks, sizes, scale):
    groups, rows_low, rows_top, classes, class_pad = sizes
    seeds = adj_top.shape[0]
    low_width, width = wl.shape
    near_rows = column.shape[1]
    rows = rows_low + rows_top * class_pad // width
    return pl.pallas_call(
        functools.partial(trainer_kernel, sizes, scale),
        out_shape=(
            jax.ShapeDtypeStruct((seeds, classes), jnp.float32),
            jax.ShapeDtypeStruct((PLANE, groups, rows, width), jnp.float32),
            jax.ShapeDtypeStruct((PLANE, groups, rows, width), jnp.bfloat16),
        ),
        in_specs=[SMEM] + [VMEM] * 3 + [pl.BlockSpec(memory_space=pl.ANY)] + [VMEM] * (1 + len(blocks)),
        out_specs=(VMEM, VMEM, VMEM),
        scratch_shapes=[
            pltpu.VMEM((near_rows, low_width), jnp.bfloat16),
            pltpu.VMEM((near_rows, width), jnp.bfloat16),
            pltpu.VMEM((near_rows, width), jnp.float32),
            pltpu.VMEM((seeds, 2 * width), jnp.bfloat16),
            pltpu.VMEM((2 * width, class_pad), jnp.bfloat16),
            pltpu.VMEM((low_width, width), jnp.float32),
            pltpu.SemaphoreType.DMA,
        ],
        compiler_params=pltpu.CompilerParams(vmem_limit_bytes=60 * MIB),
        name="trainer_step",
    )(place, labels, adj_top, column, wl, wt, *blocks)


def adam_part(gradient, moment, square):
    moment_new = beta_one * moment + (1.0 - beta_one) * gradient
    square_new = beta_two * square + (1.0 - beta_two) * gradient * gradient
    update = moment_new / bias_one / (jnp.sqrt(square_new / bias_two) + adam_eps)
    return learn_rate * update, moment_new, square_new


def adam_kernel(class_pad, parts, *refs):
    part_refs = refs[:parts]
    ml, sl, mt, st, nml, nsl, nmt, nst, delta = refs[parts:]
    rows_low, width = ml.shape
    rows_top, classes = mt.shape
    lane_groups = width // class_pad
    sub = rows_top // lane_groups
    total = part_refs[0][...]
    for ref in part_refs[1:]:
        total = total + ref[...].astype(jnp.float32)
    step, nml[...], nsl[...] = adam_part(total[:rows_low], ml[...], sl[...])
    top = total[rows_low:]
    pieces = []
    for g in range(lane_groups):
        rows = slice(g * sub, (g + 1) * sub)
        gradient = top[:, g * class_pad : g * class_pad + classes]
        piece, nmt[rows, :], nst[rows, :] = adam_part(gradient, mt[rows, :], st[rows, :])
        pieces.append(
            jnp.concatenate([piece, jnp.zeros((sub, class_pad - classes), jnp.float32)], axis=1)
        )
    whole = jnp.concatenate([step, jnp.concatenate(pieces, axis=1)], axis=0)
    delta[...] = whole.astype(jnp.bfloat16)


def adam_share(parts, ml, sl, mt, st, class_pad):
    rows, width = parts[0].shape
    shape = lambda a: jax.ShapeDtypeStruct(a.shape, jnp.float32)
    return pl.pallas_call(
        functools.partial(adam_kernel, class_pad, len(parts)),
        out_shape=(shape(ml), shape(sl), shape(mt), shape(st), jax.ShapeDtypeStruct((rows, width), jnp.bfloat16)),
        in_specs=[VMEM] * (len(parts) + 4),
        out_specs=(VMEM,) * 5,
        compiler_params=pltpu.CompilerParams(vmem_limit_bytes=32 * MIB),
        name="adam_share",
    )(*parts, ml, sl, mt, st)


def apply_kernel(sizes, place_ref, wl, wt, *refs):
    groups, rows_low, rows_top, classes, class_pad = sizes
    delta_refs, (nl, nt) = refs[: 2 * PLANE], refs[2 * PLANE :]
    here = place_ref[0]
    lane_groups = wl.shape[-1] // class_pad
    sub = rows_top // lane_groups
    for turn, delta_ref in enumerate(delta_refs):

        @pl.when(pl.program_id(0) == turn)
        def _():
            for k in range(groups):
                plane = here + k
                plane = jnp.where(plane >= groups, plane - groups, plane)
                delta = delta_ref[k].astype(jnp.float32)
                nl[plane, 0, 0] = wl[plane, 0, 0] - delta[:rows_low]
                for g in range(lane_groups):
                    rows = slice(g * sub, (g + 1) * sub)
                    step = delta[rows_low:, g * class_pad : g * class_pad + classes]
                    nt[plane, 0, 0, rows, :] = wt[plane, 0, 0, rows, :] - step


def apply_updates(place, wl, wt, deltas, sizes):
    groups, rows_low, rows_top, classes, class_pad = sizes
    low = wl.reshape(groups, PLANE, 2, rows_low, wl.shape[1])
    top = wt.reshape(groups, PLANE, 2, rows_top, wt.shape[1])

    def spot(turn, place_ref):
        core = jnp.where(turn % 2 == 0, place_ref[2], 1 - place_ref[2])
        return (0, lax.bitwise_xor(place_ref[1], turn // 2), core, 0, 0)

    specs = [pl.BlockSpec((groups, 1, 1) + a.shape[3:], spot) for a in (low, top)]
    nl, nt = pl.pallas_call(
        functools.partial(apply_kernel, sizes),
        grid_spec=pltpu.PrefetchScalarGridSpec(
            num_scalar_prefetch=1,
            grid=(2 * PLANE,),
            in_specs=specs + [VMEM] * len(deltas),
            out_specs=specs,
        ),
        out_shape=[jax.ShapeDtypeStruct(a.shape, jnp.float32) for a in (low, top)],
        compiler_params=pltpu.CompilerParams(vmem_limit_bytes=32 * MIB),
        name="apply_updates",
    )(place, low, top, *deltas)
    return nl.reshape(wl.shape), nt.reshape(wt.shape)


def per_device(
    features,
    owners_near,
    slots_near,
    owners_far,
    slots_far,
    adjacency_low,
    adjacency_top,
    labels,
    weights_low,
    weights_top,
    first_low,
    second_low,
    first_top,
    second_top,
):
    stores = lax.axis_size("store")
    groups = stores // PLANE
    members = stores * lax.axis_size("rep")
    index = lax.axis_index("store")
    here, mine, rep = index // PLANE, index % PLANE, lax.axis_index("rep")
    store_rows = features.shape[0]
    half = store_rows // 2
    near_rows, fan = adjacency_low.shape
    capacity = 2 * near_rows // stores
    classes = weights_top.shape[1]
    class_pad = -(-classes // LANES) * LANES
    rows_low, rows_top = first_low.shape[0], first_top.shape[0]
    sizes = (groups, rows_low, rows_top, classes, class_pad)
    bf16 = jnp.bfloat16
    place = jnp.stack([here, mine, rep, jnp.int32(fan)]).astype(jnp.int32)

    def across(x, distance):
        return lax.ppermute(x, "store", [(i, i ^ distance) for i in range(stores)])

    def along(x, hops):
        return lax.ppermute(x, "store", [(i, (i + hops * PLANE) % stores) for i in range(stores)])

    def sibling(x):
        return lax.ppermute(x, "rep", [(0, 1), (1, 0)])

    gid_near = owners_near[:, 0] * store_rows + slots_near[:, 0]
    requests, column = request_near(place, gid_near.reshape(1, near_rows), store_rows, stores, capacity)
    requests = lax.all_to_all(requests.reshape(stores, capacity), "store", 0, 0, tiled=True)
    quarter = half // 2
    own = lax.dynamic_slice_in_dim(features, rep * half, half, 0)
    own, requests = lax.optimization_barrier((own, requests))
    from_x, from_y = across(own, 1), across(own, 2)

    gid_far = owners_far[:, 0] * store_rows + slots_far[:, 0]
    table = jnp.concatenate([gid_near, gid_far]).reshape(-1, LANES)
    table = jnp.pad(table, ((0, -table.shape[0] % 16), (0, 0))).T
    ids = compose(adjacency_low, table)
    ids_all = [ids] + [along(ids, -k) for k in range(1, groups)]
    block = 16
    lists = row_lists(place, ids_all, store_rows, block)

    held = near_rows_held(place, requests, features, groups)
    held, lists = lax.optimization_barrier((held, lists))
    lined = [held[0]] + [along(held[k], k) for k in range(1, groups)]

    far = groups // 2
    sent = lined.pop(far)
    from_x, from_y, lined = lax.optimization_barrier((from_x, from_y, lined))
    corner_a, corner_b = across(from_x[:quarter], 2), across(from_y[quarter:], 1)
    from_x, from_y, corner_a, corner_b, sent = lax.optimization_barrier(
        (from_x, from_y, corner_a, corner_b, sent)
    )
    lined.insert(far, sent)
    pieces = [features, from_x, sibling(from_x), from_y, sibling(from_y)]
    pieces += [corner_a, corner_b, sibling(corner_a), sibling(corner_b)]
    places = [0, store_rows, store_rows + half, 2 * store_rows, 2 * store_rows + half]
    places += [3 * store_rows + quarter * i for i in range(4)]

    blocks = []
    for k in range(groups):
        made = partial_sums([lists[k]], pieces, places, PLANE * store_rows, block)
        blocks.append(along(made[0], k) if k else made[0])

    nears = []
    for d in range(PLANE):
        sheet = jnp.concatenate([part[d * capacity : (d + 1) * capacity] for part in lined])
        nears.append(across(sheet, d) if d else sheet)

    scale = 1.0 / (labels.shape[0] * members)
    logits, keep, send = trainer_step(
        place,
        labels[:, None],
        adjacency_top,
        column,
        weights_low,
        weights_top,
        blocks + nears,
        sizes,
        scale,
    )
    total = keep + sibling(send).astype(jnp.float32)
    arrived = [across(total[d].astype(bf16), d) for d in range(1, PLANE)]
    total = total[0] + sum(a.astype(jnp.float32) for a in arrived)
    shares = [total[0]] + [along(total[k].astype(bf16), k) for k in range(1, groups)]
    new_first_low, new_second_low, new_first_top, new_second_top, delta = adam_share(
        shares, first_low, second_low, first_top, second_top, class_pad
    )
    lined = jnp.stack([delta] + [along(delta, -k) for k in range(1, groups)])
    sheets = [lined] + [across(lined, d) for d in range(1, PLANE)]
    deltas = []
    for sheet in sheets:
        deltas += [sheet, sibling(sheet)]
    new_low, new_top = apply_updates(place, weights_low, weights_top, deltas, sizes)
    return (logits, new_low, new_first_low, new_second_low, new_top, new_first_top, new_second_top)


def solution(mesh):
    both = P(("store", "rep"), None)
    return jax.shard_map(
        per_device,
        mesh=mesh,
        in_specs=(P("store", None),)
        + (both,) * 6
        + (P(("store", "rep")), P(), P(), both, both, both, both),
        out_specs=(both, P(), both, both, P(), both, both),
        check_vma=False,
    )
```

```python
import functools
import math

import jax
import jax.numpy as jnp
from jax import lax
from jax.experimental import pallas as pl
from jax.experimental.pallas import tpu as pltpu
from jax.sharding import PartitionSpec as P

beta_one = 0.9
beta_two = 0.999
bias_one = 1.0 - 0.9**10
bias_two = 1.0 - 0.999**10
learn_rate = 0.01
adam_eps = 1e-08

PLANE = 4
LANES = 128
MIB = 1024 * 1024

VMEM = pl.BlockSpec(memory_space=pltpu.VMEM)
SMEM = pl.BlockSpec(memory_space=pltpu.SMEM)


def dot(a, b, ca=1, cb=0):
    return lax.dot_general(a, b, (((ca,), (cb,)), ((), ())), preferred_element_type=jnp.float32)


def compose_kernel(adj_ref, table_ref, ids_ref):
    fan, near_rows = adj_ref.shape
    his = table_ref.shape[1]
    table = table_ref[...]
    parts = jnp.concatenate([table // 65536, (table // 256) % 256, table % 256], axis=0)
    parts = parts.astype(jnp.float32).astype(jnp.bfloat16)
    row_hi = lax.broadcasted_iota(jnp.int32, (his, near_rows), 0)
    row_lo = lax.broadcasted_iota(jnp.int32, (LANES, near_rows), 0)
    for column in range(fan):
        position = adj_ref[column : column + 1, :]
        marks = jnp.where(row_hi == position // LANES, 1.0, 0.0).astype(jnp.bfloat16)
        found = dot(parts, marks)
        value = found[:LANES] * 65536.0 + found[LANES : 2 * LANES] * 256.0 + found[2 * LANES :]
        value = jnp.where(row_lo == position % LANES, value, 0.0)
        ids_ref[column : column + 1, :] = jnp.sum(value, axis=0, keepdims=True).astype(jnp.int32)


def compose(adjacency, table):
    near_rows, fan = adjacency.shape
    return pl.pallas_call(
        compose_kernel,
        out_shape=jax.ShapeDtypeStruct((fan, near_rows), jnp.int32),
        in_specs=[VMEM, VMEM],
        out_specs=VMEM,
        compiler_params=pltpu.CompilerParams(vmem_limit_bytes=32 * MIB),
        name="compose_ids",
    )(adjacency.T, table)


def request_kernel(store_rows, stores, capacity, place_ref, near_ref, request_ref, column_ref):
    groups = stores // PLANE
    near_rows = near_ref.shape[1]
    here, mine = place_ref[0], place_ref[1]
    near = near_ref[...]
    owner, slot = near // store_rows, near % store_rows
    row_owner = lax.broadcasted_iota(jnp.int32, (stores, near_rows), 0)
    marks = jnp.where(row_owner == owner, 1.0, 0.0)
    earlier = lax.broadcasted_iota(jnp.int32, (near_rows, near_rows), 0) < lax.broadcasted_iota(
        jnp.int32, (near_rows, near_rows), 1
    )
    counts = dot(marks.astype(jnp.bfloat16), jnp.where(earlier, 1.0, 0.0).astype(jnp.bfloat16))
    rank = jnp.sum(counts * marks, axis=0, keepdims=True).astype(jnp.int32)
    wanted = lax.broadcasted_iota(jnp.int32, (stores * capacity, near_rows), 0)
    marks = jnp.where(wanted == owner * capacity + rank, 1.0, 0.0).astype(jnp.bfloat16)
    line = lax.broadcasted_iota(jnp.int32, (8, near_rows), 0)
    halves = jnp.where(line == 0, slot // 256, jnp.where(line == 1, slot % 256, 0))
    found = dot(halves.astype(jnp.float32).astype(jnp.bfloat16), marks, 1, 1)
    request_ref[...] = (found[0:1] * 256.0 + found[1:2]).astype(jnp.int32)
    hops = here - owner // PLANE
    hops = jnp.where(hops < 0, hops + groups, hops)
    distance = lax.bitwise_xor(owner % PLANE, mine)
    column_ref[...] = (distance * groups + hops) * capacity + rank


def request_near(place, near, store_rows, stores, capacity):
    return pl.pallas_call(
        functools.partial(request_kernel, store_rows, stores, capacity),
        out_shape=(
            jax.ShapeDtypeStruct((1, stores * capacity), jnp.int32),
            jax.ShapeDtypeStruct(near.shape, jnp.int32),
        ),
        in_specs=[SMEM, VMEM],
        out_specs=(VMEM, VMEM),
        compiler_params=pltpu.CompilerParams(vmem_limit_bytes=32 * MIB),
        name="request_near",
    )(place, near)


def near_kernel(groups, place_ref, request_ref, features_ref, out_ref):
    here, mine = place_ref[0], place_ref[1]
    store_rows = features_ref.shape[0]
    capacity = request_ref.shape[1]
    slots = lax.broadcasted_iota(jnp.int32, (store_rows, PLANE * capacity), 0)
    for k in range(groups):
        plane = here + k
        plane = jnp.where(plane >= groups, plane - groups, plane)
        lines = []
        for d in range(PLANE):
            trainer = plane * PLANE + lax.bitwise_xor(mine, jnp.int32(d))
            lines.append(request_ref[pl.ds(trainer, 1), :])
        marks = jnp.where(slots == jnp.concatenate(lines, axis=1), 1.0, 0.0).astype(jnp.bfloat16)
        out_ref[k] = dot(marks, features_ref[...], 0, 0).astype(jnp.bfloat16)


def near_rows_held(place, requests, features, groups):
    capacity = requests.shape[1]
    return pl.pallas_call(
        functools.partial(near_kernel, groups),
        out_shape=jax.ShapeDtypeStruct((groups, PLANE * capacity, features.shape[1]), jnp.bfloat16),
        in_specs=[SMEM, VMEM, VMEM],
        out_specs=VMEM,
        compiler_params=pltpu.CompilerParams(vmem_limit_bytes=32 * MIB),
        name="near_rows",
    )(place, requests, features)


def sort_pairs(count):
    pairs = []
    size = 1
    while size < count:
        step = size
        while step >= 1:
            for start in range(step % size, count - step, 2 * step):
                for i in range(min(step, count - start - step)):
                    a, b = start + i, start + i + step
                    if a // (2 * size) == b // (2 * size):
                        pairs.append((a, b))
            step //= 2
        size *= 2
    return pairs


def depths_of(fan):
    return [d for d in (2, 3, 4, 5, 6, 8) if d < fan] + [fan]


def list_kernel(store_rows, block, place_ref, *refs):
    groups = len(refs) // 2
    ids_refs, out_refs = refs[:groups], refs[groups:]
    here, mine, rep = place_ref[0], place_ref[1], place_ref[2]
    fan, near_rows = ids_refs[0].shape
    per_plane = PLANE * store_rows
    sub = lax.broadcasted_iota(jnp.int32, (near_rows, near_rows), 0)
    lane = lax.broadcasted_iota(jnp.int32, (near_rows, near_rows), 1)
    before = jnp.where(sub < lane, 1.0, 0.0).astype(jnp.bfloat16)
    nodes = lax.broadcasted_iota(jnp.int32, (1, near_rows), 1)
    classes = lax.broadcasted_iota(jnp.int32, (fan + 1, near_rows), 0)

    def turn(row):
        distance, slot = lax.bitwise_xor(row // store_rows, mine), row % store_rows
        turned = slot + rep * (store_rows // 2)
        turned = jnp.where(turned >= store_rows, turned - store_rows, turned)
        return distance * store_rows + jnp.where(distance == 0, slot, turned)

    for ids_ref, out_ref in zip(ids_refs, out_refs):
        gid = ids_ref[...]
        held = gid // per_plane == here
        row = jnp.where(held, turn(gid % per_plane), per_plane)
        count = jnp.sum(jnp.where(held, 1, 0), axis=0, keepdims=True)
        rows = [row[j : j + 1] for j in range(fan)]
        for a, b in sort_pairs(fan):
            rows[a], rows[b] = jnp.minimum(rows[a], rows[b]), jnp.maximum(rows[a], rows[b])
        marks = jnp.where(classes == count, 1.0, 0.0)
        rank = dot(marks.astype(jnp.bfloat16), before)
        sizes = jnp.sum(marks, axis=1, keepdims=True)
        larger = jnp.zeros((1, 1), jnp.float32)
        place = jnp.zeros((1, near_rows), jnp.float32)
        ends = {}
        for c in range(fan, -1, -1):
            ends[c] = larger
            place = place + marks[c : c + 1] * (rank[c : c + 1] + larger)
            larger = larger + sizes[c : c + 1]
        order = jnp.where(sub == place.astype(jnp.int32), 1.0, 0.0).astype(jnp.bfloat16)
        lines = jnp.concatenate(rows + [nodes], axis=0)
        parts = jnp.concatenate([lines // 256, lines % 256], axis=0)
        found = dot(parts.astype(jnp.float32).astype(jnp.bfloat16), order, 1, 1)
        found = (found[: fan + 1] * 256.0 + found[fan + 1 :]).astype(jnp.int32)
        out_ref[: fan + 1, :] = found * 8
        ahead = jnp.zeros((1, near_rows), jnp.int32)
        for i, d in enumerate(depths_of(fan)[:-1]):
            blocks = (ends[d].astype(jnp.int32) + (block - 1)) // block
            ahead = ahead + jnp.where(nodes == i, blocks, 0)
        out_ref[fan + 1 : fan + 2, :] = ahead


def row_lists(place, ids_all, store_rows, block):
    fan, near_rows = ids_all[0].shape
    groups = len(ids_all)
    return pl.pallas_call(
        functools.partial(list_kernel, store_rows, block),
        out_shape=(jax.ShapeDtypeStruct((fan + 2, near_rows), jnp.int32),) * groups,
        in_specs=[SMEM] + [VMEM] * groups,
        out_specs=(VMEM,) * groups,
        compiler_params=pltpu.CompilerParams(vmem_limit_bytes=32 * MIB),
        name="row_lists",
    )(place, *ids_all)


def partial_kernel(count, places, block, *refs):
    index_refs, piece_refs = refs[:count], refs[count : count + len(places)]
    out_ref, table, sums = refs[-4 - len(places) : -1 - len(places)]
    buffers = refs[-1 - len(places) : -1]
    arrived = refs[-1]
    fan, near_rows = index_refs[0].shape[0] - 2, index_refs[0].shape[1]
    units = buffers[0].shape[1] // LANES
    total = table.shape[0] // 8 - 1
    chunk = 256

    def row(at):
        return table[pl.ds(pl.multiple_of(at, 8), 8), :]

    def tree(rows):
        while len(rows) > 1:
            odd = rows[-1:] if len(rows) % 2 else []
            rows = [a + b for a, b in zip(rows[0::2], rows[1::2])] + odd
        return rows[0]

    copies = [
        pltpu.make_async_copy(source, buffer, arrived.at[i])
        for i, (source, buffer) in enumerate(zip(piece_refs, buffers))
    ]
    for copy in copies:
        copy.start()
    table[total * 8 :, :] = jnp.zeros((8, LANES), jnp.float32)
    for copy, buffer, start in zip(copies, buffers, places):
        copy.wait()

        def fill(i, carry):
            values = buffer[pl.ds(pl.multiple_of(i * chunk, chunk), chunk), :].astype(jnp.float32)
            base = (start + i * chunk) * 8
            for unit in range(units):
                table[pl.ds(base + unit, chunk, stride=8), :] = values[
                    :, unit * LANES : (unit + 1) * LANES
                ]
            return carry

        lax.fori_loop(0, buffer.shape[0] // chunk, fill, 0)

    for turn, index_ref in enumerate(index_refs):
        begin = 0
        depths = depths_of(fan)
        for at in range(len(depths) - 1, -1, -1):
            depth = depths[at]

            def step(i, carry):
                for u in range(block):
                    n = i * block + u
                    spot = pl.multiple_of(index_ref[fan, n], 8)
                    sums[pl.ds(spot, 8), :] = tree([row(index_ref[j, n]) for j in range(depth)])
                return carry

            end = index_ref[fan + 1, at - 1] if at else near_rows // block
            lax.fori_loop(begin, end, step, 0)
            begin = end

        for unit in range(units):
            lanes = slice(unit * LANES, (unit + 1) * LANES)
            out_ref[turn, :near_rows, lanes] = sums[
                pl.ds(unit, near_rows, stride=8), :
            ].astype(jnp.bfloat16)


def partial_sums(lists, pieces, places, total, block):
    near_rows = lists[0].shape[1]
    width = pieces[0].shape[1]
    return pl.pallas_call(
        functools.partial(partial_kernel, len(lists), places, block),
        out_shape=jax.ShapeDtypeStruct((len(lists), near_rows, width), jnp.bfloat16),
        in_specs=[SMEM] * len(lists) + [pl.BlockSpec(memory_space=pl.ANY)] * len(pieces),
        out_specs=VMEM,
        scratch_shapes=[
            pltpu.VMEM(((total + 1) * 8, LANES), jnp.float32),
            pltpu.VMEM(((near_rows + 1) * 8, LANES), jnp.float32),
        ]
        + [pltpu.VMEM(piece.shape, piece.dtype) for piece in pieces]
        + [pltpu.SemaphoreType.DMA((len(pieces),))],
        compiler_params=pltpu.CompilerParams(vmem_limit_bytes=50 * MIB),
        name="partial_sums",
    )(*lists, *pieces)


def trainer_kernel(sizes, scale, *refs):
    groups, rows_low, rows_top, classes, class_pad = sizes
    place_ref, labels_ref, adj_ref, column_ref, wl_ref, wt_ref = refs[:6]
    block_refs, near_refs = refs[6 : 6 + groups], refs[6 + groups : -10]
    logits_ref, keep_ref, send_ref, li, hidden, slope, top_in, wt, weights, arrived = refs[-10:]
    seeds, fan_top = adj_ref.shape
    near_rows, low_width = li.shape
    feat = low_width // 2
    width = hidden.shape[1]
    capacity = near_refs[0].shape[0]
    here, mine, rep = place_ref[0], place_ref[1], place_ref[2]
    fan_low = place_ref[3].astype(jnp.float32)

    bring = pltpu.make_async_copy(wl_ref, weights, arrived)
    bring.start()
    column = column_ref[...]
    rows_cap = lax.broadcasted_iota(jnp.int32, (capacity, near_rows), 0)
    near = None
    for d in range(PLANE):
        marks = jnp.where(rows_cap + d * capacity == column, 1.0, 0.0).astype(jnp.bfloat16)
        term = dot(marks, near_refs[d][...], 0, 0)
        near = term if near is None else near + term
    total = block_refs[0][...].astype(jnp.float32)
    for k in range(1, groups):
        total = total + block_refs[k][...].astype(jnp.float32)
    li[:, :feat] = near.astype(jnp.bfloat16)
    li[:, feat:] = (total / fan_low).astype(jnp.bfloat16)

    wt[...] = jnp.zeros_like(wt)
    wt[:, :classes] = wt_ref[...].astype(jnp.bfloat16)

    bring.wait()
    factor = math.sqrt(2.0 / math.pi)
    step = 256
    for c in range(width // step):
        cols = slice(c * step, (c + 1) * step)
        v = dot(li[...], weights[:, cols].astype(jnp.bfloat16))
        square = v * v
        t = jnp.tanh(factor * (v + 0.044715 * v * square))
        half = 0.5 * (1.0 + t)
        hidden[:, cols] = (v * half).astype(jnp.bfloat16)
        slope[:, cols] = half + 0.5 * v * (1.0 - t * t) * factor * (1.0 + 3.0 * 0.044715 * square)

    lane_near = lax.broadcasted_iota(jnp.int32, (seeds, near_rows), 1)
    counts = jnp.zeros((seeds, near_rows), jnp.float32)
    for j in range(fan_top):
        counts = counts + jnp.where(adj_ref[:, j : j + 1] == lane_near, 1.0, 0.0)
    counts = counts.astype(jnp.bfloat16)
    top_in[:, :width] = hidden[:seeds, :]
    top_in[:, width:] = (dot(counts, hidden[...]) / fan_top).astype(jnp.bfloat16)
    logits = dot(top_in[...], wt[...])
    logits_ref[...] = logits[:, :classes]
    lane_class = lax.broadcasted_iota(jnp.int32, (seeds, class_pad), 1)
    powers = jnp.where(lane_class < classes, jnp.exp(logits), 0.0)
    chances = powers / jnp.sum(powers, axis=1, keepdims=True)
    targets = jnp.where(lane_class == labels_ref[...], 1.0, 0.0)
    dlogits = ((chances - targets) * scale).astype(jnp.bfloat16)
    dinput = dot(dlogits, wt[...], 1, 1)
    spread = dinput[:, width:] / fan_top
    high = spread.astype(jnp.bfloat16)
    low = (spread - high.astype(jnp.float32)).astype(jnp.bfloat16)
    dhidden = dot(counts, high, 0, 0) + dot(counts, low, 0, 0)
    hidden[:seeds, :] = ((dhidden[:seeds] + dinput[:, :width]) * slope[:seeds, :]).astype(jnp.bfloat16)
    hidden[seeds:, :] = (dhidden[seeds:] * slope[seeds:, :]).astype(jnp.bfloat16)

    first = rep == 0
    members = low_width // rows_low
    stores = members // 2
    lane_groups = width // class_pad
    sub = rows_top // lane_groups

    def slot(store):
        plane, inner = store // PLANE, store % PLANE
        relative = plane - here
        relative = jnp.where(relative < 0, relative + groups, relative)
        return lax.bitwise_xor(mine, jnp.int32(inner)), relative

    tile = 384
    pair = 2 * rows_low
    for m in range(low_width // tile):
        grad = dot(li[:, m * tile : (m + 1) * tile], hidden[...], 0, 0)
        for s in range(tile // pair):
            even = grad[s * pair : s * pair + rows_low]
            odd = grad[s * pair + rows_low : (s + 1) * pair]
            a, b = slot(m * (tile // pair) + s)
            keep_ref[a, b, :rows_low, :] = jnp.where(first, even, odd)
            send_ref[a, b, :rows_low, :] = jnp.where(first, odd, even).astype(jnp.bfloat16)
    grad = dot(top_in[...], dlogits, 0, 0)
    for s in range(stores):
        even = grad[2 * s * rows_top : (2 * s + 1) * rows_top]
        odd = grad[(2 * s + 1) * rows_top : (2 * s + 2) * rows_top]
        own = jnp.where(first, even, odd)
        other = jnp.where(first, odd, even)
        a, b = slot(s)
        own = jnp.concatenate([own[g * sub : (g + 1) * sub] for g in range(lane_groups)], axis=1)
        other = jnp.concatenate([other[g * sub : (g + 1) * sub] for g in range(lane_groups)], axis=1)
        keep_ref[a, b, rows_low:, :] = own
        send_ref[a, b, rows_low:, :] = other.astype(jnp.bfloat16)


def trainer_step(place, labels, adj_top, column, wl, wt, blocks, sizes, scale):
    groups, rows_low, rows_top, classes, class_pad = sizes
    seeds = adj_top.shape[0]
    low_width, width = wl.shape
    near_rows = column.shape[1]
    rows = rows_low + rows_top * class_pad // width
    return pl.pallas_call(
        functools.partial(trainer_kernel, sizes, scale),
        out_shape=(
            jax.ShapeDtypeStruct((seeds, classes), jnp.float32),
            jax.ShapeDtypeStruct((PLANE, groups, rows, width), jnp.float32),
            jax.ShapeDtypeStruct((PLANE, groups, rows, width), jnp.bfloat16),
        ),
        in_specs=[SMEM] + [VMEM] * 3 + [pl.BlockSpec(memory_space=pl.ANY)] + [VMEM] * (1 + len(blocks)),
        out_specs=(VMEM, VMEM, VMEM),
        scratch_shapes=[
            pltpu.VMEM((near_rows, low_width), jnp.bfloat16),
            pltpu.VMEM((near_rows, width), jnp.bfloat16),
            pltpu.VMEM((near_rows, width), jnp.float32),
            pltpu.VMEM((seeds, 2 * width), jnp.bfloat16),
            pltpu.VMEM((2 * width, class_pad), jnp.bfloat16),
            pltpu.VMEM((low_width, width), jnp.float32),
            pltpu.SemaphoreType.DMA,
        ],
        compiler_params=pltpu.CompilerParams(vmem_limit_bytes=60 * MIB),
        name="trainer_step",
    )(place, labels, adj_top, column, wl, wt, *blocks)


def adam_part(gradient, moment, square):
    moment_new = beta_one * moment + (1.0 - beta_one) * gradient
    square_new = beta_two * square + (1.0 - beta_two) * gradient * gradient
    update = moment_new / bias_one / (jnp.sqrt(square_new / bias_two) + adam_eps)
    return learn_rate * update, moment_new, square_new


def adam_kernel(class_pad, parts, *refs):
    part_refs = refs[:parts]
    ml, sl, mt, st, nml, nsl, nmt, nst, delta = refs[parts:]
    rows_low, width = ml.shape
    rows_top, classes = mt.shape
    lane_groups = width // class_pad
    sub = rows_top // lane_groups
    total = part_refs[0][...]
    for ref in part_refs[1:]:
        total = total + ref[...].astype(jnp.float32)
    step, nml[...], nsl[...] = adam_part(total[:rows_low], ml[...], sl[...])
    top = total[rows_low:]
    pieces = []
    for g in range(lane_groups):
        rows = slice(g * sub, (g + 1) * sub)
        gradient = top[:, g * class_pad : g * class_pad + classes]
        piece, nmt[rows, :], nst[rows, :] = adam_part(gradient, mt[rows, :], st[rows, :])
        pieces.append(
            jnp.concatenate([piece, jnp.zeros((sub, class_pad - classes), jnp.float32)], axis=1)
        )
    whole = jnp.concatenate([step, jnp.concatenate(pieces, axis=1)], axis=0)
    delta[...] = whole.astype(jnp.bfloat16)


def adam_share(parts, ml, sl, mt, st, class_pad):
    rows, width = parts[0].shape
    shape = lambda a: jax.ShapeDtypeStruct(a.shape, jnp.float32)
    return pl.pallas_call(
        functools.partial(adam_kernel, class_pad, len(parts)),
        out_shape=(shape(ml), shape(sl), shape(mt), shape(st), jax.ShapeDtypeStruct((rows, width), jnp.bfloat16)),
        in_specs=[VMEM] * (len(parts) + 4),
        out_specs=(VMEM,) * 5,
        compiler_params=pltpu.CompilerParams(vmem_limit_bytes=32 * MIB),
        name="adam_share",
    )(*parts, ml, sl, mt, st)


def apply_kernel(sizes, place_ref, wl, wt, *refs):
    groups, rows_low, rows_top, classes, class_pad = sizes
    delta_refs, (nl, nt) = refs[: 2 * PLANE], refs[2 * PLANE :]
    here = place_ref[0]
    lane_groups = wl.shape[-1] // class_pad
    sub = rows_top // lane_groups
    for turn, delta_ref in enumerate(delta_refs):

        @pl.when(pl.program_id(0) == turn)
        def _():
            for k in range(groups):
                plane = here + k
                plane = jnp.where(plane >= groups, plane - groups, plane)
                delta = delta_ref[k].astype(jnp.float32)
                nl[plane, 0, 0] = wl[plane, 0, 0] - delta[:rows_low]
                for g in range(lane_groups):
                    rows = slice(g * sub, (g + 1) * sub)
                    step = delta[rows_low:, g * class_pad : g * class_pad + classes]
                    nt[plane, 0, 0, rows, :] = wt[plane, 0, 0, rows, :] - step


def apply_updates(place, wl, wt, deltas, sizes):
    groups, rows_low, rows_top, classes, class_pad = sizes
    low = wl.reshape(groups, PLANE, 2, rows_low, wl.shape[1])
    top = wt.reshape(groups, PLANE, 2, rows_top, wt.shape[1])

    def spot(turn, place_ref):
        core = jnp.where(turn % 2 == 0, place_ref[2], 1 - place_ref[2])
        return (0, lax.bitwise_xor(place_ref[1], turn // 2), core, 0, 0)

    specs = [pl.BlockSpec((groups, 1, 1) + a.shape[3:], spot) for a in (low, top)]
    nl, nt = pl.pallas_call(
        functools.partial(apply_kernel, sizes),
        grid_spec=pltpu.PrefetchScalarGridSpec(
            num_scalar_prefetch=1,
            grid=(2 * PLANE,),
            in_specs=specs + [VMEM] * len(deltas),
            out_specs=specs,
        ),
        out_shape=[jax.ShapeDtypeStruct(a.shape, jnp.float32) for a in (low, top)],
        compiler_params=pltpu.CompilerParams(vmem_limit_bytes=60 * MIB),
        name="apply_updates",
    )(place, low, top, *deltas)
    return nl.reshape(wl.shape), nt.reshape(wt.shape)


def per_device(
    features,
    owners_near,
    slots_near,
    owners_far,
    slots_far,
    adjacency_low,
    adjacency_top,
    labels,
    weights_low,
    weights_top,
    first_low,
    second_low,
    first_top,
    second_top,
):
    stores = lax.axis_size("store")
    groups = stores // PLANE
    members = stores * lax.axis_size("rep")
    index = lax.axis_index("store")
    here, mine, rep = index // PLANE, index % PLANE, lax.axis_index("rep")
    store_rows = features.shape[0]
    half = store_rows // 2
    near_rows, fan = adjacency_low.shape
    capacity = 2 * near_rows // stores
    classes = weights_top.shape[1]
    class_pad = -(-classes // LANES) * LANES
    rows_low, rows_top = first_low.shape[0], first_top.shape[0]
    sizes = (groups, rows_low, rows_top, classes, class_pad)
    bf16 = jnp.bfloat16
    place = jnp.stack([here, mine, rep, jnp.int32(fan)]).astype(jnp.int32)

    def across(x, distance):
        return lax.ppermute(x, "store", [(i, i ^ distance) for i in range(stores)])

    def along(x, hops):
        return lax.ppermute(x, "store", [(i, (i + hops * PLANE) % stores) for i in range(stores)])

    def sibling(x):
        return lax.ppermute(x, "rep", [(0, 1), (1, 0)])

    gid_near = owners_near[:, 0] * store_rows + slots_near[:, 0]
    requests, column = request_near(place, gid_near.reshape(1, near_rows), store_rows, stores, capacity)
    requests = lax.all_to_all(requests.reshape(stores, capacity), "store", 0, 0, tiled=True)
    quarter = half // 2
    own = lax.dynamic_slice_in_dim(features, rep * half, half, 0)
    own, requests = lax.optimization_barrier((own, requests))
    from_x, from_y = across(own, 1), across(own, 2)

    gid_far = owners_far[:, 0] * store_rows + slots_far[:, 0]
    table = jnp.concatenate([gid_near, gid_far]).reshape(-1, LANES)
    table = jnp.pad(table, ((0, -table.shape[0] % 16), (0, 0))).T
    ids = compose(adjacency_low, table)
    ids_all = [ids] + [along(ids, -k) for k in range(1, groups)]
    block = 16
    lists = row_lists(place, ids_all, store_rows, block)

    held = near_rows_held(place, requests, features, groups)
    held, lists = lax.optimization_barrier((held, lists))
    lined = [held[0]] + [along(held[k], k) for k in range(1, groups)]

    far = groups // 2
    sent = lined.pop(far)
    from_x, from_y, lined = lax.optimization_barrier((from_x, from_y, lined))
    corner_a, corner_b = across(from_x[:quarter], 2), across(from_y[quarter:], 1)
    from_x, from_y, corner_a, corner_b, sent = lax.optimization_barrier(
        (from_x, from_y, corner_a, corner_b, sent)
    )
    lined.insert(far, sent)
    pieces = [features, from_x, sibling(from_x), from_y, sibling(from_y)]
    pieces += [corner_a, corner_b, sibling(corner_a), sibling(corner_b)]
    places = [0, store_rows, store_rows + half, 2 * store_rows, 2 * store_rows + half]
    places += [3 * store_rows + quarter * i for i in range(4)]

    blocks = []
    for k in range(groups):
        made = partial_sums([lists[k]], pieces, places, PLANE * store_rows, block)
        blocks.append(along(made[0], k) if k else made[0])

    nears = []
    for d in range(PLANE):
        sheet = jnp.concatenate([part[d * capacity : (d + 1) * capacity] for part in lined])
        nears.append(across(sheet, d) if d else sheet)

    scale = 1.0 / (labels.shape[0] * members)
    logits, keep, send = trainer_step(
        place,
        labels[:, None],
        adjacency_top,
        column,
        weights_low,
        weights_top,
        blocks + nears,
        sizes,
        scale,
    )
    total = keep + sibling(send).astype(jnp.float32)
    arrived = [across(total[d].astype(bf16), d) for d in range(1, PLANE)]
    total = total[0] + sum(a.astype(jnp.float32) for a in arrived)
    shares = [total[0]] + [along(total[k].astype(bf16), k) for k in range(1, groups)]
    new_first_low, new_second_low, new_first_top, new_second_top, delta = adam_share(
        shares, first_low, second_low, first_top, second_top, class_pad
    )
    lined = jnp.stack([delta] + [along(delta, -k) for k in range(1, groups)])
    sheets = [lined] + [across(lined, d) for d in range(1, PLANE)]
    deltas = []
    for sheet in sheets:
        deltas += [sheet, sibling(sheet)]
    new_low, new_top = apply_updates(place, weights_low, weights_top, deltas, sizes)
    return (logits, new_low, new_first_low, new_second_low, new_top, new_first_top, new_second_top)


def solution(mesh):
    both = P(("store", "rep"), None)
    return jax.shard_map(
        per_device,
        mesh=mesh,
        in_specs=(P("store", None),)
        + (both,) * 6
        + (P(("store", "rep")), P(), P(), both, both, both, both),
        out_specs=(both, P(), both, both, P(), both, both),
        check_vma=False,
    )
```

```python
import functools
import math

import jax
import jax.numpy as jnp
from jax import lax
from jax.experimental import pallas as pl
from jax.experimental.pallas import tpu as pltpu
from jax.sharding import PartitionSpec as P

beta_one = 0.9
beta_two = 0.999
bias_one = 1.0 - 0.9**10
bias_two = 1.0 - 0.999**10
learn_rate = 0.01
adam_eps = 1e-08

PLANE = 4
LANES = 128
MIB = 1024 * 1024

VMEM = pl.BlockSpec(memory_space=pltpu.VMEM)
SMEM = pl.BlockSpec(memory_space=pltpu.SMEM)


def dot(a, b, ca=1, cb=0):
    return lax.dot_general(a, b, (((ca,), (cb,)), ((), ())), preferred_element_type=jnp.float32)


def compose_kernel(adj_ref, table_ref, ids_ref):
    fan, near_rows = adj_ref.shape
    his = table_ref.shape[1]
    table = table_ref[...]
    parts = jnp.concatenate([table // 65536, (table // 256) % 256, table % 256], axis=0)
    parts = parts.astype(jnp.float32).astype(jnp.bfloat16)
    row_hi = lax.broadcasted_iota(jnp.int32, (his, near_rows), 0)
    row_lo = lax.broadcasted_iota(jnp.int32, (LANES, near_rows), 0)
    for column in range(fan):
        position = adj_ref[column : column + 1, :]
        marks = jnp.where(row_hi == position // LANES, 1.0, 0.0).astype(jnp.bfloat16)
        found = dot(parts, marks)
        value = found[:LANES] * 65536.0 + found[LANES : 2 * LANES] * 256.0 + found[2 * LANES :]
        value = jnp.where(row_lo == position % LANES, value, 0.0)
        ids_ref[column : column + 1, :] = jnp.sum(value, axis=0, keepdims=True).astype(jnp.int32)


def compose(adjacency, table):
    near_rows, fan = adjacency.shape
    return pl.pallas_call(
        compose_kernel,
        out_shape=jax.ShapeDtypeStruct((fan, near_rows), jnp.int32),
        in_specs=[VMEM, VMEM],
        out_specs=VMEM,
        compiler_params=pltpu.CompilerParams(vmem_limit_bytes=32 * MIB),
        name="compose_ids",
    )(adjacency.T, table)


def request_kernel(store_rows, stores, capacity, place_ref, near_ref, request_ref, column_ref):
    groups = stores // PLANE
    near_rows = near_ref.shape[1]
    here, mine = place_ref[0], place_ref[1]
    near = near_ref[...]
    owner, slot = near // store_rows, near % store_rows
    row_owner = lax.broadcasted_iota(jnp.int32, (stores, near_rows), 0)
    marks = jnp.where(row_owner == owner, 1.0, 0.0)
    earlier = lax.broadcasted_iota(jnp.int32, (near_rows, near_rows), 0) < lax.broadcasted_iota(
        jnp.int32, (near_rows, near_rows), 1
    )
    counts = dot(marks.astype(jnp.bfloat16), jnp.where(earlier, 1.0, 0.0).astype(jnp.bfloat16))
    rank = jnp.sum(counts * marks, axis=0, keepdims=True).astype(jnp.int32)
    wanted = lax.broadcasted_iota(jnp.int32, (stores * capacity, near_rows), 0)
    marks = jnp.where(wanted == owner * capacity + rank, 1.0, 0.0).astype(jnp.bfloat16)
    line = lax.broadcasted_iota(jnp.int32, (8, near_rows), 0)
    halves = jnp.where(line == 0, slot // 256, jnp.where(line == 1, slot % 256, 0))
    found = dot(halves.astype(jnp.float32).astype(jnp.bfloat16), marks, 1, 1)
    request_ref[...] = (found[0:1] * 256.0 + found[1:2]).astype(jnp.int32)
    hops = here - owner // PLANE
    hops = jnp.where(hops < 0, hops + groups, hops)
    distance = lax.bitwise_xor(owner % PLANE, mine)
    column_ref[...] = (distance * groups + hops) * capacity + rank


def request_near(place, near, store_rows, stores, capacity):
    return pl.pallas_call(
        functools.partial(request_kernel, store_rows, stores, capacity),
        out_shape=(
            jax.ShapeDtypeStruct((1, stores * capacity), jnp.int32),
            jax.ShapeDtypeStruct(near.shape, jnp.int32),
        ),
        in_specs=[SMEM, VMEM],
        out_specs=(VMEM, VMEM),
        compiler_params=pltpu.CompilerParams(vmem_limit_bytes=32 * MIB),
        name="request_near",
    )(place, near)


def near_kernel(groups, place_ref, request_ref, features_ref, out_ref):
    here, mine = place_ref[0], place_ref[1]
    store_rows = features_ref.shape[0]
    capacity = request_ref.shape[1]
    slots = lax.broadcasted_iota(jnp.int32, (store_rows, PLANE * capacity), 0)
    for k in range(groups):
        plane = here + k
        plane = jnp.where(plane >= groups, plane - groups, plane)
        lines = []
        for d in range(PLANE):
            trainer = plane * PLANE + lax.bitwise_xor(mine, jnp.int32(d))
            lines.append(request_ref[pl.ds(trainer, 1), :])
        marks = jnp.where(slots == jnp.concatenate(lines, axis=1), 1.0, 0.0).astype(jnp.bfloat16)
        out_ref[k] = dot(marks, features_ref[...], 0, 0).astype(jnp.bfloat16)


def near_rows_held(place, requests, features, groups):
    capacity = requests.shape[1]
    return pl.pallas_call(
        functools.partial(near_kernel, groups),
        out_shape=jax.ShapeDtypeStruct((groups, PLANE * capacity, features.shape[1]), jnp.bfloat16),
        in_specs=[SMEM, VMEM, VMEM],
        out_specs=VMEM,
        compiler_params=pltpu.CompilerParams(vmem_limit_bytes=32 * MIB),
        name="near_rows",
    )(place, requests, features)


def sort_pairs(count):
    pairs = []
    size = 1
    while size < count:
        step = size
        while step >= 1:
            for start in range(step % size, count - step, 2 * step):
                for i in range(min(step, count - start - step)):
                    a, b = start + i, start + i + step
                    if a // (2 * size) == b // (2 * size):
                        pairs.append((a, b))
            step //= 2
        size *= 2
    return pairs


def depths_of(fan):
    return [d for d in (2, 3, 4, 5, 6, 8) if d < fan] + [fan]


def list_kernel(store_rows, block, place_ref, *refs):
    groups = len(refs) // 2
    ids_refs, out_refs = refs[:groups], refs[groups:]
    here, mine, rep = place_ref[0], place_ref[1], place_ref[2]
    fan, near_rows = ids_refs[0].shape
    per_plane = PLANE * store_rows
    sub = lax.broadcasted_iota(jnp.int32, (near_rows, near_rows), 0)
    lane = lax.broadcasted_iota(jnp.int32, (near_rows, near_rows), 1)
    before = jnp.where(sub < lane, 1.0, 0.0).astype(jnp.bfloat16)
    nodes = lax.broadcasted_iota(jnp.int32, (1, near_rows), 1)
    classes = lax.broadcasted_iota(jnp.int32, (fan + 1, near_rows), 0)

    def turn(row):
        distance, slot = lax.bitwise_xor(row // store_rows, mine), row % store_rows
        turned = slot + rep * (store_rows // 2)
        turned = jnp.where(turned >= store_rows, turned - store_rows, turned)
        return distance * store_rows + jnp.where(distance == 0, slot, turned)

    for ids_ref, out_ref in zip(ids_refs, out_refs):
        gid = ids_ref[...]
        held = gid // per_plane == here
        row = jnp.where(held, turn(gid % per_plane), per_plane)
        count = jnp.sum(jnp.where(held, 1, 0), axis=0, keepdims=True)
        rows = [row[j : j + 1] for j in range(fan)]
        for a, b in sort_pairs(fan):
            rows[a], rows[b] = jnp.minimum(rows[a], rows[b]), jnp.maximum(rows[a], rows[b])
        marks = jnp.where(classes == count, 1.0, 0.0)
        rank = dot(marks.astype(jnp.bfloat16), before)
        sizes = jnp.sum(marks, axis=1, keepdims=True)
        larger = jnp.zeros((1, 1), jnp.float32)
        place = jnp.zeros((1, near_rows), jnp.float32)
        ends = {}
        for c in range(fan, -1, -1):
            ends[c] = larger
            place = place + marks[c : c + 1] * (rank[c : c + 1] + larger)
            larger = larger + sizes[c : c + 1]
        order = jnp.where(sub == place.astype(jnp.int32), 1.0, 0.0).astype(jnp.bfloat16)
        lines = jnp.concatenate(rows + [nodes], axis=0)
        parts = jnp.concatenate([lines // 256, lines % 256], axis=0)
        found = dot(parts.astype(jnp.float32).astype(jnp.bfloat16), order, 1, 1)
        found = (found[: fan + 1] * 256.0 + found[fan + 1 :]).astype(jnp.int32)
        out_ref[: fan + 1, :] = found * 8
        ahead = jnp.zeros((1, near_rows), jnp.int32)
        for i, d in enumerate(depths_of(fan)[:-1]):
            blocks = (ends[d].astype(jnp.int32) + (block - 1)) // block
            ahead = ahead + jnp.where(nodes == i, blocks, 0)
        out_ref[fan + 1 : fan + 2, :] = ahead


def row_lists(place, ids_all, store_rows, block):
    fan, near_rows = ids_all[0].shape
    groups = len(ids_all)
    return pl.pallas_call(
        functools.partial(list_kernel, store_rows, block),
        out_shape=(jax.ShapeDtypeStruct((fan + 2, near_rows), jnp.int32),) * groups,
        in_specs=[SMEM] + [VMEM] * groups,
        out_specs=(VMEM,) * groups,
        compiler_params=pltpu.CompilerParams(vmem_limit_bytes=32 * MIB),
        name="row_lists",
    )(place, *ids_all)


def partial_kernel(count, places, block, *refs):
    index_refs, piece_refs = refs[:count], refs[count : count + len(places)]
    out_ref, table, sums = refs[-4 - len(places) : -1 - len(places)]
    buffers = refs[-1 - len(places) : -1]
    arrived = refs[-1]
    fan, near_rows = index_refs[0].shape[0] - 2, index_refs[0].shape[1]
    units = buffers[0].shape[1] // LANES
    total = table.shape[0] // 8 - 1
    chunk = 256

    def row(at):
        return table[pl.ds(pl.multiple_of(at, 8), 8), :]

    def tree(rows):
        while len(rows) > 1:
            odd = rows[-1:] if len(rows) % 2 else []
            rows = [a + b for a, b in zip(rows[0::2], rows[1::2])] + odd
        return rows[0]

    copies = [
        pltpu.make_async_copy(source, buffer, arrived.at[i])
        for i, (source, buffer) in enumerate(zip(piece_refs, buffers))
    ]
    for copy in copies:
        copy.start()
    table[total * 8 :, :] = jnp.zeros((8, LANES), jnp.float32)
    for copy, buffer, start in zip(copies, buffers, places):
        copy.wait()

        def fill(i, carry):
            values = buffer[pl.ds(pl.multiple_of(i * chunk, chunk), chunk), :].astype(jnp.float32)
            base = (start + i * chunk) * 8
            for unit in range(units):
                table[pl.ds(base + unit, chunk, stride=8), :] = values[
                    :, unit * LANES : (unit + 1) * LANES
                ]
            return carry

        lax.fori_loop(0, buffer.shape[0] // chunk, fill, 0)

    for turn, index_ref in enumerate(index_refs):
        begin = 0
        depths = depths_of(fan)
        for at in range(len(depths) - 1, -1, -1):
            depth = depths[at]

            def step(i, carry):
                for u in range(block):
                    n = i * block + u
                    spot = pl.multiple_of(index_ref[fan, n], 8)
                    sums[pl.ds(spot, 8), :] = tree([row(index_ref[j, n]) for j in range(depth)])
                return carry

            end = index_ref[fan + 1, at - 1] if at else near_rows // block
            lax.fori_loop(begin, end, step, 0)
            begin = end

        for unit in range(units):
            lanes = slice(unit * LANES, (unit + 1) * LANES)
            out_ref[turn, :near_rows, lanes] = sums[
                pl.ds(unit, near_rows, stride=8), :
            ].astype(jnp.bfloat16)


def partial_sums(lists, pieces, places, total, block):
    near_rows = lists[0].shape[1]
    width = pieces[0].shape[1]
    return pl.pallas_call(
        functools.partial(partial_kernel, len(lists), places, block),
        out_shape=jax.ShapeDtypeStruct((len(lists), near_rows, width), jnp.bfloat16),
        in_specs=[SMEM] * len(lists) + [pl.BlockSpec(memory_space=pl.ANY)] * len(pieces),
        out_specs=VMEM,
        scratch_shapes=[
            pltpu.VMEM(((total + 1) * 8, LANES), jnp.float32),
            pltpu.VMEM(((near_rows + 1) * 8, LANES), jnp.float32),
        ]
        + [pltpu.VMEM(piece.shape, piece.dtype) for piece in pieces]
        + [pltpu.SemaphoreType.DMA((len(pieces),))],
        compiler_params=pltpu.CompilerParams(vmem_limit_bytes=50 * MIB),
        name="partial_sums",
    )(*lists, *pieces)


def trainer_kernel(sizes, scale, *refs):
    groups, rows_low, rows_top, classes, class_pad = sizes
    place_ref, labels_ref, adj_ref, column_ref, wl_ref, wt_ref = refs[:6]
    block_refs, near_refs = refs[6 : 6 + groups], refs[6 + groups : -10]
    logits_ref, keep_ref, send_ref, li, hidden, slope, top_in, wt, weights, arrived = refs[-10:]
    seeds, fan_top = adj_ref.shape
    near_rows, low_width = li.shape
    feat = low_width // 2
    width = hidden.shape[1]
    capacity = near_refs[0].shape[0]
    here, mine, rep = place_ref[0], place_ref[1], place_ref[2]
    fan_low = place_ref[3].astype(jnp.float32)

    bring = pltpu.make_async_copy(wl_ref, weights, arrived)
    bring.start()
    column = column_ref[...]
    rows_cap = lax.broadcasted_iota(jnp.int32, (capacity, near_rows), 0)
    near = None
    for d in range(PLANE):
        marks = jnp.where(rows_cap + d * capacity == column, 1.0, 0.0).astype(jnp.bfloat16)
        term = dot(marks, near_refs[d][...], 0, 0)
        near = term if near is None else near + term
    total = block_refs[0][...].astype(jnp.float32)
    for k in range(1, groups):
        total = total + block_refs[k][...].astype(jnp.float32)
    li[:, :feat] = near.astype(jnp.bfloat16)
    li[:, feat:] = (total / fan_low).astype(jnp.bfloat16)

    wt[...] = jnp.zeros_like(wt)
    wt[:, :classes] = wt_ref[...].astype(jnp.bfloat16)

    bring.wait()
    factor = math.sqrt(2.0 / math.pi)
    step = 256
    for c in range(width // step):
        cols = slice(c * step, (c + 1) * step)
        v = dot(li[...], weights[:, cols].astype(jnp.bfloat16))
        square = v * v
        t = jnp.tanh(factor * (v + 0.044715 * v * square))
        half = 0.5 * (1.0 + t)
        hidden[:, cols] = (v * half).astype(jnp.bfloat16)
        slope[:, cols] = half + 0.5 * v * (1.0 - t * t) * factor * (1.0 + 3.0 * 0.044715 * square)

    lane_near = lax.broadcasted_iota(jnp.int32, (seeds, near_rows), 1)
    counts = jnp.zeros((seeds, near_rows), jnp.float32)
    for j in range(fan_top):
        counts = counts + jnp.where(adj_ref[:, j : j + 1] == lane_near, 1.0, 0.0)
    counts = counts.astype(jnp.bfloat16)
    top_in[:, :width] = hidden[:seeds, :]
    top_in[:, width:] = (dot(counts, hidden[...]) / fan_top).astype(jnp.bfloat16)
    logits = dot(top_in[...], wt[...])
    logits_ref[...] = logits[:, :classes]
    lane_class = lax.broadcasted_iota(jnp.int32, (seeds, class_pad), 1)
    powers = jnp.where(lane_class < classes, jnp.exp(logits), 0.0)
    chances = powers / jnp.sum(powers, axis=1, keepdims=True)
    targets = jnp.where(lane_class == labels_ref[...], 1.0, 0.0)
    dlogits = ((chances - targets) * scale).astype(jnp.bfloat16)
    dinput = dot(dlogits, wt[...], 1, 1)
    spread = dinput[:, width:] / fan_top
    high = spread.astype(jnp.bfloat16)
    low = (spread - high.astype(jnp.float32)).astype(jnp.bfloat16)
    dhidden = dot(counts, high, 0, 0) + dot(counts, low, 0, 0)
    hidden[:seeds, :] = ((dhidden[:seeds] + dinput[:, :width]) * slope[:seeds, :]).astype(jnp.bfloat16)
    hidden[seeds:, :] = (dhidden[seeds:] * slope[seeds:, :]).astype(jnp.bfloat16)

    first = rep == 0
    members = low_width // rows_low
    stores = members // 2
    lane_groups = width // class_pad
    sub = rows_top // lane_groups

    def slot(store):
        plane, inner = store // PLANE, store % PLANE
        relative = plane - here
        relative = jnp.where(relative < 0, relative + groups, relative)
        return lax.bitwise_xor(mine, jnp.int32(inner)), relative

    tile = 384
    pair = 2 * rows_low
    for m in range(low_width // tile):
        grad = dot(li[:, m * tile : (m + 1) * tile], hidden[...], 0, 0)
        for s in range(tile // pair):
            even = grad[s * pair : s * pair + rows_low]
            odd = grad[s * pair + rows_low : (s + 1) * pair]
            a, b = slot(m * (tile // pair) + s)
            keep_ref[a, b, :rows_low, :] = jnp.where(first, even, odd).astype(jnp.bfloat16)
            send_ref[a, b, :rows_low, :] = jnp.where(first, odd, even).astype(jnp.bfloat16)
    grad = dot(top_in[...], dlogits, 0, 0)
    for s in range(stores):
        even = grad[2 * s * rows_top : (2 * s + 1) * rows_top]
        odd = grad[(2 * s + 1) * rows_top : (2 * s + 2) * rows_top]
        own = jnp.where(first, even, odd)
        other = jnp.where(first, odd, even)
        a, b = slot(s)
        own = jnp.concatenate([own[g * sub : (g + 1) * sub] for g in range(lane_groups)], axis=1)
        other = jnp.concatenate([other[g * sub : (g + 1) * sub] for g in range(lane_groups)], axis=1)
        keep_ref[a, b, rows_low:, :] = own.astype(jnp.bfloat16)
        send_ref[a, b, rows_low:, :] = other.astype(jnp.bfloat16)


def trainer_step(place, labels, adj_top, column, wl, wt, blocks, sizes, scale):
    groups, rows_low, rows_top, classes, class_pad = sizes
    seeds = adj_top.shape[0]
    low_width, width = wl.shape
    near_rows = column.shape[1]
    rows = rows_low + rows_top * class_pad // width
    return pl.pallas_call(
        functools.partial(trainer_kernel, sizes, scale),
        out_shape=(
            jax.ShapeDtypeStruct((seeds, classes), jnp.float32),
            jax.ShapeDtypeStruct((PLANE, groups, rows, width), jnp.bfloat16),
            jax.ShapeDtypeStruct((PLANE, groups, rows, width), jnp.bfloat16),
        ),
        in_specs=[SMEM] + [VMEM] * 3 + [pl.BlockSpec(memory_space=pl.ANY)] + [VMEM] * (1 + len(blocks)),
        out_specs=(VMEM, VMEM, VMEM),
        scratch_shapes=[
            pltpu.VMEM((near_rows, low_width), jnp.bfloat16),
            pltpu.VMEM((near_rows, width), jnp.bfloat16),
            pltpu.VMEM((near_rows, width), jnp.float32),
            pltpu.VMEM((seeds, 2 * width), jnp.bfloat16),
            pltpu.VMEM((2 * width, class_pad), jnp.bfloat16),
            pltpu.VMEM((low_width, width), jnp.float32),
            pltpu.SemaphoreType.DMA,
        ],
        compiler_params=pltpu.CompilerParams(vmem_limit_bytes=60 * MIB),
        name="trainer_step",
    )(place, labels, adj_top, column, wl, wt, *blocks)


def adam_part(gradient, moment, square):
    moment_new = beta_one * moment + (1.0 - beta_one) * gradient
    square_new = beta_two * square + (1.0 - beta_two) * gradient * gradient
    update = moment_new / bias_one / (jnp.sqrt(square_new / bias_two) + adam_eps)
    return learn_rate * update, moment_new, square_new


def adam_kernel(class_pad, parts, *refs):
    part_refs = refs[:parts]
    ml, sl, mt, st, nml, nsl, nmt, nst, delta = refs[parts:]
    rows_low, width = ml.shape
    rows_top, classes = mt.shape
    lane_groups = width // class_pad
    sub = rows_top // lane_groups
    total = part_refs[0][...]
    for ref in part_refs[1:]:
        total = total + ref[...].astype(jnp.float32)
    step, nml[...], nsl[...] = adam_part(total[:rows_low], ml[...], sl[...])
    top = total[rows_low:]
    pieces = []
    for g in range(lane_groups):
        rows = slice(g * sub, (g + 1) * sub)
        gradient = top[:, g * class_pad : g * class_pad + classes]
        piece, nmt[rows, :], nst[rows, :] = adam_part(gradient, mt[rows, :], st[rows, :])
        pieces.append(
            jnp.concatenate([piece, jnp.zeros((sub, class_pad - classes), jnp.float32)], axis=1)
        )
    whole = jnp.concatenate([step, jnp.concatenate(pieces, axis=1)], axis=0)
    delta[...] = whole.astype(jnp.bfloat16)


def adam_share(parts, ml, sl, mt, st, class_pad):
    rows, width = parts[0].shape
    shape = lambda a: jax.ShapeDtypeStruct(a.shape, jnp.float32)
    return pl.pallas_call(
        functools.partial(adam_kernel, class_pad, len(parts)),
        out_shape=(shape(ml), shape(sl), shape(mt), shape(st), jax.ShapeDtypeStruct((rows, width), jnp.bfloat16)),
        in_specs=[VMEM] * (len(parts) + 4),
        out_specs=(VMEM,) * 5,
        compiler_params=pltpu.CompilerParams(vmem_limit_bytes=32 * MIB),
        name="adam_share",
    )(*parts, ml, sl, mt, st)


def apply_kernel(sizes, place_ref, wl, wt, *refs):
    groups, rows_low, rows_top, classes, class_pad = sizes
    delta_refs, (nl, nt) = refs[: 2 * PLANE], refs[2 * PLANE :]
    here = place_ref[0]
    lane_groups = wl.shape[-1] // class_pad
    sub = rows_top // lane_groups
    for turn, delta_ref in enumerate(delta_refs):

        @pl.when(pl.program_id(0) == turn)
        def _():
            for k in range(groups):
                plane = here + k
                plane = jnp.where(plane >= groups, plane - groups, plane)
                delta = delta_ref[k].astype(jnp.float32)
                nl[plane, 0, 0] = wl[plane, 0, 0] - delta[:rows_low]
                for g in range(lane_groups):
                    rows = slice(g * sub, (g + 1) * sub)
                    step = delta[rows_low:, g * class_pad : g * class_pad + classes]
                    nt[plane, 0, 0, rows, :] = wt[plane, 0, 0, rows, :] - step


def apply_updates(place, wl, wt, deltas, sizes):
    groups, rows_low, rows_top, classes, class_pad = sizes
    low = wl.reshape(groups, PLANE, 2, rows_low, wl.shape[1])
    top = wt.reshape(groups, PLANE, 2, rows_top, wt.shape[1])

    def spot(turn, place_ref):
        core = jnp.where(turn % 2 == 0, place_ref[2], 1 - place_ref[2])
        return (0, lax.bitwise_xor(place_ref[1], turn // 2), core, 0, 0)

    specs = [pl.BlockSpec((groups, 1, 1) + a.shape[3:], spot) for a in (low, top)]
    nl, nt = pl.pallas_call(
        functools.partial(apply_kernel, sizes),
        grid_spec=pltpu.PrefetchScalarGridSpec(
            num_scalar_prefetch=1,
            grid=(2 * PLANE,),
            in_specs=specs + [VMEM] * len(deltas),
            out_specs=specs,
        ),
        out_shape=[jax.ShapeDtypeStruct(a.shape, jnp.float32) for a in (low, top)],
        compiler_params=pltpu.CompilerParams(vmem_limit_bytes=60 * MIB),
        name="apply_updates",
    )(place, low, top, *deltas)
    return nl.reshape(wl.shape), nt.reshape(wt.shape)


def per_device(
    features,
    owners_near,
    slots_near,
    owners_far,
    slots_far,
    adjacency_low,
    adjacency_top,
    labels,
    weights_low,
    weights_top,
    first_low,
    second_low,
    first_top,
    second_top,
):
    stores = lax.axis_size("store")
    groups = stores // PLANE
    members = stores * lax.axis_size("rep")
    index = lax.axis_index("store")
    here, mine, rep = index // PLANE, index % PLANE, lax.axis_index("rep")
    store_rows = features.shape[0]
    half = store_rows // 2
    near_rows, fan = adjacency_low.shape
    capacity = 2 * near_rows // stores
    classes = weights_top.shape[1]
    class_pad = -(-classes // LANES) * LANES
    rows_low, rows_top = first_low.shape[0], first_top.shape[0]
    sizes = (groups, rows_low, rows_top, classes, class_pad)
    bf16 = jnp.bfloat16
    place = jnp.stack([here, mine, rep, jnp.int32(fan)]).astype(jnp.int32)

    def across(x, distance):
        return lax.ppermute(x, "store", [(i, i ^ distance) for i in range(stores)])

    def along(x, hops):
        return lax.ppermute(x, "store", [(i, (i + hops * PLANE) % stores) for i in range(stores)])

    def sibling(x):
        return lax.ppermute(x, "rep", [(0, 1), (1, 0)])

    gid_near = owners_near[:, 0] * store_rows + slots_near[:, 0]
    requests, column = request_near(place, gid_near.reshape(1, near_rows), store_rows, stores, capacity)
    requests = lax.all_to_all(requests.reshape(stores, capacity), "store", 0, 0, tiled=True)
    quarter = half // 2
    own = lax.dynamic_slice_in_dim(features, rep * half, half, 0)
    own, requests = lax.optimization_barrier((own, requests))
    from_x, from_y = across(own, 1), across(own, 2)

    gid_far = owners_far[:, 0] * store_rows + slots_far[:, 0]
    table = jnp.concatenate([gid_near, gid_far]).reshape(-1, LANES)
    table = jnp.pad(table, ((0, -table.shape[0] % 16), (0, 0))).T
    ids = compose(adjacency_low, table)
    ids_all = [ids] + [along(ids, -k) for k in range(1, groups)]
    block = 16
    lists = row_lists(place, ids_all, store_rows, block)

    held = near_rows_held(place, requests, features, groups)
    held, lists = lax.optimization_barrier((held, lists))
    lined = [held[0]] + [along(held[k], k) for k in range(1, groups)]

    far = groups // 2
    sent = lined.pop(far)
    from_x, from_y, lined = lax.optimization_barrier((from_x, from_y, lined))
    corner_a, corner_b = across(from_x[:quarter], 2), across(from_y[quarter:], 1)
    from_x, from_y, corner_a, corner_b, sent = lax.optimization_barrier(
        (from_x, from_y, corner_a, corner_b, sent)
    )
    lined.insert(far, sent)
    pieces = [features, from_x, sibling(from_x), from_y, sibling(from_y)]
    pieces += [corner_a, corner_b, sibling(corner_a), sibling(corner_b)]
    places = [0, store_rows, store_rows + half, 2 * store_rows, 2 * store_rows + half]
    places += [3 * store_rows + quarter * i for i in range(4)]

    blocks = []
    for k in range(groups):
        made = partial_sums([lists[k]], pieces, places, PLANE * store_rows, block)
        blocks.append(along(made[0], k) if k else made[0])

    nears = []
    for d in range(PLANE):
        sheet = jnp.concatenate([part[d * capacity : (d + 1) * capacity] for part in lined])
        nears.append(across(sheet, d) if d else sheet)

    scale = 1.0 / (labels.shape[0] * members)
    logits, keep, send = trainer_step(
        place,
        labels[:, None],
        adjacency_top,
        column,
        weights_low,
        weights_top,
        blocks + nears,
        sizes,
        scale,
    )
    total = keep.astype(jnp.float32) + sibling(send).astype(jnp.float32)
    arrived = [across(total[d].astype(bf16), d) for d in range(1, PLANE)]
    total = total[0] + sum(a.astype(jnp.float32) for a in arrived)
    shares = [total[0]] + [along(total[k].astype(bf16), k) for k in range(1, groups)]
    new_first_low, new_second_low, new_first_top, new_second_top, delta = adam_share(
        shares, first_low, second_low, first_top, second_top, class_pad
    )
    lined = jnp.stack([delta] + [along(delta, -k) for k in range(1, groups)])
    sheets = [lined] + [across(lined, d) for d in range(1, PLANE)]
    deltas = []
    for sheet in sheets:
        deltas += [sheet, sibling(sheet)]
    new_low, new_top = apply_updates(place, weights_low, weights_top, deltas, sizes)
    return (logits, new_low, new_first_low, new_second_low, new_top, new_first_top, new_second_top)


def solution(mesh):
    both = P(("store", "rep"), None)
    return jax.shard_map(
        per_device,
        mesh=mesh,
        in_specs=(P("store", None),)
        + (both,) * 6
        + (P(("store", "rep")), P(), P(), both, both, both, both),
        out_specs=(both, P(), both, both, P(), both, both),
        check_vma=False,
    )
```
